32 devices in a mesh: seq: 8 (over y, x, core), fsdp: 4 (over z).
Axes of the slice: x: 2, y: 2, z: 4, core: 2. Of those that a mesh axis runs over, the one named last changes fastest.
Arguments:
- tokens: bfloat16 [2, 4, 1920, 2304], P(None, 'fsdp', 'seq'), may hold values from -6 to 6
- segments: int32 [2, 4, 1920], P(None, 'fsdp', 'seq'), may hold values from 0 to 3, as said below
- w_query: bfloat16 [2304, 2048], P('fsdp'), may hold values from -0.125 to 0.125
- key_weight: bfloat16 [2304, 1024], P('fsdp'), may hold values from -0.125 to 0.125
- value_weight: bfloat16 [2304, 1024], P('fsdp'), may hold values from -0.125 to 0.125
- w_out: bfloat16 [2048, 2304], P('fsdp'), may hold values from -0.125 to 0.125
- w_gate: bfloat16 [2304, 9216], P('fsdp'), may hold values from -0.125 to 0.125
- w_up: bfloat16 [2304, 9216], P('fsdp'), may hold values from -0.125 to 0.125
- w_down: bfloat16 [9216, 2304], P('fsdp'), may hold values from -0.0625 to 0.0625
- gain_attn_in: float32 [2304], replicated, may hold values from 0.5 to 1.5
- gain_attn_out: float32 [2304], replicated, may hold values from 0.5 to 1.5
- gain_ffn_in: float32 [2304], replicated, may hold values from 0.5 to 1.5
- gain_ffn_out: float32 [2304], replicated, may hold values from 0.5 to 1.5
- cotangent: bfloat16 [2, 4, 1920, 2304], P(None, 'fsdp', 'seq'), may hold values from -6 to 6
Outputs:
- mixed_out: bfloat16 [2, 4, 1920, 2304], P(None, 'fsdp', 'seq')
- grad_tokens: float32 [2, 4, 1920, 2304], P(None, 'fsdp', 'seq')
- grad_query: float32 [2304, 2048], P('fsdp', 'seq')
- grad_key: float32 [2304, 1024], P('fsdp', 'seq')
- grad_value: float32 [2304, 1024], P('fsdp', 'seq')
- grad_out: float32 [2048, 2304], P('fsdp', 'seq')
- grad_gate: float32 [2304, 9216], P('fsdp', 'seq')
- grad_up: float32 [2304, 9216], P('fsdp', 'seq')
- grad_down: float32 [9216, 2304], P('fsdp', 'seq')
- grad_attn_in: float32 [2304], replicated
- grad_attn_out: float32 [2304], replicated
- grad_ffn_in: float32 [2304], replicated
- grad_ffn_out: float32 [2304], replicated
The draws below stay inside these ranges and needn't reach their ends.
Inputs may be any that keep to these rules, and one draw needn't show every extreme that they name: `segments`: in each sequence the segment numbers start at 0, never fall, and rise by at most one from token to token; tokens with equal numbers form one document. For every sequence index of a micro-batch, one of the 2 micro-batches, drawn from the seed, is a single document; every other sequence holds exactly four documents.
All inputs are finite; a program needn't handle non-finite values.
Results may differ from the reference program's by a relative error of at most 0.02.
Values may be sent and summed in bfloat16 or wider, within the bound.
A program may use at most 576 MiB of HBM per device.

```python
import math
import jax
import jax.numpy as jnp
from jax import lax

MODEL_WIDTH = 2304
QUERY_HEADS = 8
KEY_VALUE_HEADS = 4
HEAD_SIZE = 256
FF = 9216
CAP = 50
WIN = 1024
MB = 2
LENGTH = 1920
SEQS = 4


def draw_segments(key, part):
    key = jax.random.fold_in(key, 11)
    cut_key, pick_key = jax.random.split(key)
    scores = jax.random.randint(cut_key, (MB, SEQS, LENGTH - 1), 0, 65536) * LENGTH
    scores = scores + jnp.arange(LENGTH - 1, dtype=jnp.int32)[None, None, :]
    order = jnp.argsort(scores, axis=-1, stable=True)
    ranks = jnp.argsort(order, axis=-1, stable=True)
    cut_marks = (ranks < 3).astype(jnp.int32)
    cut_marks = jnp.concatenate([jnp.zeros((MB, SEQS, 1), jnp.int32), cut_marks], axis=-1)
    single = jax.random.randint(pick_key, (SEQS,), 0, MB)
    keep_cuts = (jnp.arange(MB)[:, None] != single[None, :]).astype(jnp.int32)[:, :, None]
    return jnp.cumsum(cut_marks * keep_cuts, axis=-1).astype(jnp.int32)


def block_scale(rng, dims, cuts, low, top_value):
    factor_of = 1.0
    for dim, shards_of in cuts:
        steps = jax.random.uniform(jax.random.fold_in(jax.random.fold_in(rng, 6), dim), (shards_of,), jnp.float32, low / len(cuts), top_value / len(cuts))
        factor_of = factor_of * jnp.repeat(jnp.exp(steps), dims[dim] // shards_of).reshape((-1,) + (1,) * (len(dims) - 1 - dim))
    return factor_of


def normal_values(own_key, extent, scale, limit, cuts=(), kind=jnp.bfloat16):
    array = jax.random.normal(own_key, extent, jnp.float32) * scale
    if len(cuts) > 0:
        array = block_scale(own_key, extent, cuts, -0.22, 0.18) * array
    return jnp.clip(array, min=-limit, max=limit).astype(kind)


def setup_inputs(seed: int = 0) -> dict:
    splits = jax.random.split(jax.random.key(seed), 15)
    tokens = normal_values(splits[0], (MB, SEQS, LENGTH, MODEL_WIDTH), 1.0, 6.0, ((1, 4), (2, 8)))
    segments = draw_segments(jax.random.fold_in(splits[14], 71), 0)
    w_query = normal_values(splits[2], (MODEL_WIDTH, QUERY_HEADS * HEAD_SIZE), MODEL_WIDTH ** -0.5, 0.125, ((0, 4),))
    key_weight = normal_values(splits[3], (MODEL_WIDTH, KEY_VALUE_HEADS * HEAD_SIZE), MODEL_WIDTH ** -0.5, 0.125, ((0, 4),))
    value_weight = normal_values(splits[4], (MODEL_WIDTH, KEY_VALUE_HEADS * HEAD_SIZE), MODEL_WIDTH ** -0.5, 0.125, ((0, 4),))
    w_out = normal_values(splits[5], (QUERY_HEADS * HEAD_SIZE, MODEL_WIDTH), (QUERY_HEADS * HEAD_SIZE) ** -0.5, 0.125, ((0, 4),))
    w_gate = normal_values(splits[6], (MODEL_WIDTH, FF), MODEL_WIDTH ** -0.5, 0.125, ((0, 4),))
    w_up = normal_values(splits[7], (MODEL_WIDTH, FF), MODEL_WIDTH ** -0.5, 0.125, ((0, 4),))
    w_down = normal_values(splits[8], (FF, MODEL_WIDTH), FF ** -0.5, 0.0625, ((0, 4),))
    gain_attn_in = jnp.clip(1.0 + 0.1 * jax.random.normal(splits[9], (MODEL_WIDTH,), jnp.float32), 0.5, 1.5)
    gain_attn_out = jnp.clip(1.0 + 0.1 * jax.random.normal(splits[10], (MODEL_WIDTH,), jnp.float32), 0.5, 1.5)
    gain_ffn_in = jnp.clip(1.0 + 0.1 * jax.random.normal(splits[11], (MODEL_WIDTH,), jnp.float32), 0.5, 1.5)
    gain_ffn_out = jnp.clip(1.0 + 0.1 * jax.random.normal(splits[12], (MODEL_WIDTH,), jnp.float32), 0.5, 1.5)
    cotangent = normal_values(splits[13], (MB, SEQS, LENGTH, MODEL_WIDTH), 1.0, 6.0, ((1, 4), (2, 8)))
    return dict(tokens=tokens, segments=segments, w_query=w_query, key_weight=key_weight, value_weight=value_weight, w_out=w_out, w_gate=w_gate, w_up=w_up, w_down=w_down, gain_attn_in=gain_attn_in, gain_attn_out=gain_attn_out, gain_ffn_in=gain_ffn_in, gain_ffn_out=gain_ffn_out, cotangent=cotangent)


@jax.custom_vjp
def low(v):
    return lax.optimization_barrier(v.astype(jnp.bfloat16)).astype(jnp.float32)

@jax.custom_vjp
def low_back(v):
    return v

def low_keep(v):
    return (low(v), None)

def low_pass(kept, grad):
    return (grad,)

def back_keep(v):
    return (v, None)

def back_low(kept, grad):
    return (low(grad),)
low.defvjp(low_keep, low_pass)
low_back.defvjp(back_keep, back_low)
epsilon = 1e-06
highest_precision = lax.Precision.HIGHEST

def rms_gain(stream, gain):
    return stream * lax.rsqrt(lax.optimization_barrier(jnp.mean(stream * stream, axis=-1, keepdims=True)) + epsilon) * gain

def angles(position, size):
    frequency = 10000.0 ** (-jnp.arange(size // 2, dtype=jnp.float32) * 2.0 / size)
    phase_angle = position.astype(jnp.float32)[:, None] * frequency[None, :]
    return (jnp.cos(phase_angle)[:, None, :], jnp.sin(phase_angle)[:, None, :])

def rotate(value_rows, cosine_table, sine_table):
    half_size = value_rows.shape[-1] // 2
    first_half = value_rows[..., :half_size]
    second = value_rows[..., half_size:]
    return jnp.concatenate([first_half * cosine_table - second * sine_table, second * cosine_table + first_half * sine_table], axis=-1)

def doc_positions(segment):
    places = jnp.arange(segment.shape[0], dtype=jnp.int32)
    previous = jnp.concatenate([segment[:1] - 1, segment[:-1]])
    starts = jnp.where(segment != previous, places, 0).astype(jnp.int32)
    return places - lax.cummax(starts, axis=0)

def layer(stream, segment, w_query, key_weight, value_weight, w_out, w_gate, w_up, w_down, gain_one, gain_two, gain_three, gain_four):
    sequence_length = stream.shape[0]
    cosine_table, sine_table = angles(doc_positions(segment), HEAD_SIZE)
    normed_input = low(rms_gain(stream, gain_one))
    query_rows = low_back(jnp.dot(normed_input, w_query, precision=highest_precision)).reshape(sequence_length, QUERY_HEADS, HEAD_SIZE)
    key_rows = low_back(jnp.dot(normed_input, key_weight, precision=highest_precision)).reshape(sequence_length, KEY_VALUE_HEADS, HEAD_SIZE)
    value_rows = low_back(jnp.dot(normed_input, value_weight, precision=highest_precision)).reshape(sequence_length, KEY_VALUE_HEADS, HEAD_SIZE)
    query_rows = low(rotate(query_rows, cosine_table, sine_table) * (1.0 / math.sqrt(HEAD_SIZE)))
    key_rows = low(rotate(key_rows, cosine_table, sine_table))
    value_rows = low(value_rows)
    grouped_heads = query_rows.reshape(sequence_length, KEY_VALUE_HEADS, QUERY_HEADS // KEY_VALUE_HEADS, HEAD_SIZE)
    score = low_back(jnp.einsum('qhgd,khd->hgqk', grouped_heads, key_rows, precision=highest_precision))
    capped = CAP * jnp.tanh(score / CAP)
    places = jnp.arange(sequence_length, dtype=jnp.int32)
    distance = places[:, None] - places[None, :]
    allowed = (segment[:, None] == segment[None, :]) & (distance >= 0) & (distance < WIN)
    capped = jnp.where(allowed, capped, -jnp.inf)
    prob = jax.nn.softmax(capped, axis=-1)
    attended = jnp.einsum('hgqk,khd->qhgd', low(prob), value_rows, precision=highest_precision).reshape(sequence_length, QUERY_HEADS * HEAD_SIZE)
    attended = low(low_back(attended))
    mixed = low_back(jnp.dot(attended, w_out, precision=highest_precision))
    middle = stream + rms_gain(mixed, gain_two)
    ffn_in = low(rms_gain(middle, gain_three))
    gate_proj = low_back(jnp.dot(ffn_in, w_gate, precision=highest_precision))
    up_proj = low_back(jnp.dot(ffn_in, w_up, precision=highest_precision))
    hidden = low(jax.nn.gelu(gate_proj, approximate=True) * up_proj)
    down_proj = low_back(jnp.dot(hidden, w_down, precision=highest_precision))
    return middle + rms_gain(down_proj, gain_four)

def reference(tokens, segments, w_query, key_weight, value_weight, w_out, w_gate, w_up, w_down, gain_attn_in, gain_attn_out, gain_ffn_in, gain_ffn_out, cotangent):
    flat_tokens = tokens.astype(jnp.float32).reshape(MB * SEQS, LENGTH, MODEL_WIDTH)
    flat_segments = segments.reshape(MB * SEQS, LENGTH).astype(jnp.int32)
    weight_list = (w_query.astype(jnp.float32), key_weight.astype(jnp.float32), value_weight.astype(jnp.float32), w_out.astype(jnp.float32), w_gate.astype(jnp.float32), w_up.astype(jnp.float32), w_down.astype(jnp.float32), gain_attn_in, gain_attn_out, gain_ffn_in, gain_ffn_out)

    def forward(stream_all, *weight_args):

        def per_sequence(paired):
            return jax.checkpoint(layer)(paired[0], paired[1], *weight_args)
        return lax.map(per_sequence, (stream_all, flat_segments))
    layer_out, pullback = jax.vjp(forward, flat_tokens, *weight_list)
    gradients = pullback(cotangent.astype(jnp.float32).reshape(MB * SEQS, LENGTH, MODEL_WIDTH))
    mixed_out = layer_out.reshape(MB, SEQS, LENGTH, MODEL_WIDTH).astype(jnp.bfloat16)
    grad_tokens = gradients[0].reshape(MB, SEQS, LENGTH, MODEL_WIDTH)
    return (mixed_out, grad_tokens, gradients[1], gradients[2], gradients[3], gradients[4], gradients[5], gradients[6], gradients[7], gradients[8], gradients[9], gradients[10], gradients[11])
```

```python
import functools
import math

import jax
import jax.numpy as jnp
from jax import lax
from jax.experimental import pallas as pl
from jax.experimental.pallas import tpu as pltpu
from jax.sharding import PartitionSpec as P

QUERY_HEADS = 8
KEY_VALUE_HEADS = 4
HEAD_SIZE = 256
CAP = 50
WIN = 1024


epsilon = 1e-06


def shifted(value, axis, steps):
    count = lax.axis_size(axis)
    initial, last = (max(0, -steps), min(count, count - steps))
    return lax.ppermute(value, axis, [(source, source + steps) for source in range(initial, last)])


def rms_gain(stream, gain):
    return stream * lax.rsqrt(jnp.mean(stream * stream, axis=-1, keepdims=True) + epsilon) * gain


def geglu(gate_proj, up_proj):
    return jax.nn.gelu(gate_proj, approximate=True) * up_proj


def angles(position, size):
    frequency = 10000.0 ** (-jnp.arange(size // 2, dtype=jnp.float32) * 2.0 / size)
    phase_angle = position.astype(jnp.float32)[:, None] * frequency[None, :]
    return (jnp.cos(phase_angle)[:, None, :], jnp.sin(phase_angle)[:, None, :])


def rotate(value_rows, cosine_table, sine_table, direction):
    half_size = value_rows.shape[-1] // 2
    first_half = value_rows[..., :half_size]
    second = value_rows[..., half_size:]
    return jnp.concatenate(
        [
            first_half * cosine_table - direction * second * sine_table,
            second * cosine_table + direction * first_half * sine_table,
        ],
        axis=-1,
    )


def doc_starts(segment):
    lower = segment[None, :] < segment[:, None]
    return jnp.sum(lower.astype(jnp.int32), axis=1)


def final_dot(left_side, right_side):
    return jnp.dot(left_side, right_side, preferred_element_type=jnp.float32)


def dot_back(left_side, right_side):
    return lax.dot_general(
        left_side, right_side, (((1,), (1,)), ((), ())), preferred_element_type=jnp.float32
    )


def dot_rows(left_side, right_side):
    return lax.dot_general(
        left_side, right_side, (((0,), (0,)), ((), ())), preferred_element_type=jnp.float32
    )


def fetch_attention(w_query, key_weight, value_weight, w_out):
    return (
        lax.all_gather(w_query, "fsdp", axis=0, tiled=True),
        lax.all_gather(key_weight, "fsdp", axis=0, tiled=True),
        lax.all_gather(value_weight, "fsdp", axis=0, tiled=True),
        lax.all_gather(w_out, "fsdp", axis=0, tiled=True),
    )


def key_window(kv_pair, halo_count):
    arrived = [shifted(kv_pair, "seq", offset) for offset in range(halo_count, 0, -1)]
    return jnp.concatenate(arrived + [kv_pair], axis=1)


def window_grads(paired_gradient, halo_count, token_rows):
    summed = paired_gradient[:, halo_count * token_rows :]
    for offset in range(1, halo_count + 1):
        begin = (halo_count - offset) * token_rows
        summed = summed + shifted(
            paired_gradient[:, begin : begin + token_rows].astype(jnp.bfloat16), "seq", -offset
        ).astype(jnp.float32)
    return summed


def window_mask(seg_here, seg_whole, seq_place, token_rows, halo_count):
    padded = jnp.concatenate([jnp.full((halo_count * token_rows,), -1, jnp.int32), seg_whole])
    key_seg = lax.dynamic_slice_in_dim(
        padded, seq_place * token_rows, (halo_count + 1) * token_rows
    )
    query_pos = seq_place * token_rows + jnp.arange(token_rows, dtype=jnp.int32)
    key_pos = (
        seq_place * token_rows
        - halo_count * token_rows
        + jnp.arange((halo_count + 1) * token_rows, dtype=jnp.int32)
    )
    distance = query_pos[:, None] - key_pos[None, :]
    return (seg_here[:, None] == key_seg[None, :]) & (distance >= 0) & (distance < WIN)


def line_gather(rows):
    count = lax.axis_size("fsdp")
    place = lax.axis_index("fsdp")
    up, down = [rows], [rows]
    for hop in range(1, count):
        up.append(
            lax.ppermute(up[-1], "fsdp", [(i, i + 1) for i in range(hop - 1, count - 1)])
        )
        down.append(
            lax.ppermute(down[-1], "fsdp", [(i, i - 1) for i in range(1, count - hop + 1)])
        )

    def assemble(here, from_low, from_high):
        parts = [from_low[here - j] if j <= here else from_high[j - here] for j in range(count)]
        return jnp.concatenate(parts, axis=0)

    return lax.switch(
        place, [functools.partial(assemble, here) for here in range(count)], up, down
    )


def line_scatter(partial):
    count = lax.axis_size("fsdp")
    place = lax.axis_index("fsdp")
    rows = partial.shape[0] // count

    def piece(offset):
        index = jnp.clip(place + offset, 0, count - 1)
        return lax.dynamic_slice_in_dim(partial, index * rows, rows).astype(jnp.float32)

    total = piece(0)
    for sign in (1, -1):
        carried = None
        for hop in range(count - 1, 0, -1):
            running = piece(sign * hop)
            if carried is not None:
                running = running + carried.astype(jnp.float32)
            if sign > 0:
                pairs = [(i, i + 1) for i in range(count - hop)]
            else:
                pairs = [(i, i - 1) for i in range(hop, count)]
            carried = lax.ppermute(running.astype(jnp.bfloat16), "fsdp", pairs)
        if carried is not None:
            total = total + carried.astype(jnp.float32)
    return total


def gather_tokens(rows):
    return lax.all_gather(rows, "seq", axis=0, tiled=True)


def scatter_tokens(partial):
    return lax.psum_scatter(
        partial.astype(jnp.bfloat16), "seq", scatter_dimension=0, tiled=True
    ).astype(jnp.float32)


def swap_parts(value, split_axis, concat_axis):
    return lax.all_to_all(
        value, "seq", split_axis=split_axis, concat_axis=concat_axis, tiled=True
    )


def score_parts(query, key, low_bound, row_start, col_start):
    raw = lax.dot_general(
        query, key, (((1,), (1,)), ((), ())), preferred_element_type=jnp.float32
    )
    bent = jnp.tanh(raw * (1.0 / CAP))
    shape = raw.shape
    row = row_start + lax.broadcasted_iota(jnp.int32, shape, 0)
    col = col_start + lax.broadcasted_iota(jnp.int32, shape, 1)
    allowed = (col <= row) & (col >= low_bound)
    return bent, jnp.where(allowed, CAP * bent, -1e30)


def attend_kernel(block, reach, q_ref, k_ref, v_ref, low_ref, out_ref, log_ref):
    index = pl.program_id(0)

    def run(blocks):
        first = (index - (blocks - 1)) * block
        span = pl.ds(pl.multiple_of(first, block), blocks * block)
        _, capped = score_parts(
            q_ref[...], k_ref[span, :], low_ref[...], index * block, first
        )
        peak = jnp.max(capped, axis=-1, keepdims=True)
        power = jnp.exp(capped - peak)
        total = jnp.sum(power, axis=-1, keepdims=True)
        prob = (power * (1.0 / total)).astype(jnp.bfloat16)
        out = jnp.dot(prob, v_ref[span, :], preferred_element_type=jnp.float32)
        out_ref[...] = out.astype(jnp.bfloat16)
        log_ref[...] = peak + jnp.log(total)

    for blocks in range(1, reach + 1):
        if blocks < reach:
            pl.when(index == blocks - 1)(functools.partial(run, blocks))
        else:
            pl.when(index >= blocks - 1)(functools.partial(run, blocks))


def turn_back(value, cosine, sine):
    half = value.shape[-1] // 2
    first, second = value[:, :half], value[:, half:]
    return jnp.concatenate(
        [first * cosine + second * sine, second * cosine - first * sine], axis=-1
    )


def attend_back_kernel(
    block,
    reach,
    q_ref,
    k_ref,
    v_ref,
    g_ref,
    low_ref,
    log_ref,
    cos_ref,
    sin_ref,
    dq_ref,
    dk_ref,
    dv_ref,
):
    index = pl.program_id(0)
    steps = pl.num_programs(0)

    @pl.when(index == 0)
    def _():
        dk_ref[...] = jnp.zeros_like(dk_ref)
        dv_ref[...] = jnp.zeros_like(dv_ref)

    own = pl.ds(pl.multiple_of(index * block, block), block)

    def run(blocks):
        first = (index - (blocks - 1)) * block
        span = pl.ds(pl.multiple_of(first, block), blocks * block)
        query, grad = q_ref[...], g_ref[...]
        key = k_ref[span, :]
        bent, capped = score_parts(query, key, low_ref[...], index * block, first)
        prob = jnp.exp(capped - log_ref[...])
        grad_prob = lax.dot_general(
            grad, v_ref[span, :], (((1,), (1,)), ((), ())), preferred_element_type=jnp.float32
        )
        delta = jnp.sum(prob * grad_prob, axis=-1, keepdims=True)
        grad_score = (prob * (grad_prob - delta) * (1.0 - bent * bent)).astype(jnp.bfloat16)
        dq = jnp.dot(grad_score, key, preferred_element_type=jnp.float32)
        dq = dq * (1.0 / math.sqrt(HEAD_SIZE))
        dq_ref[...] = turn_back(dq, cos_ref[own, :], sin_ref[own, :]).astype(jnp.bfloat16)
        across = (((0,), (0,)), ((), ()))
        dk_ref[span, :] += lax.dot_general(
            grad_score, query, across, preferred_element_type=jnp.float32
        )
        dv_ref[span, :] += lax.dot_general(
            prob.astype(jnp.bfloat16), grad, across, preferred_element_type=jnp.float32
        )

    for blocks in range(1, reach + 1):
        if blocks < reach:
            pl.when(index == blocks - 1)(functools.partial(run, blocks))
        else:
            pl.when(index >= blocks - 1)(functools.partial(run, blocks))

    @pl.when(index == steps - 1)
    def _():
        dk_ref[...] = turn_back(dk_ref[...], cos_ref[...], sin_ref[...])


def block_shape(length):
    for block in (384, 256, 128):
        if length % block == 0:
            reach = min(length // block, (WIN - 1 + block - 1) // block + 1)
            return block, reach
    raise ValueError("sequence length")


def attend(query, key, value, low_bound):
    length = query.shape[0]
    block, reach = block_shape(length)
    whole = pl.BlockSpec((length, HEAD_SIZE), lambda i: (0, 0))
    rows = pl.BlockSpec((block, HEAD_SIZE), lambda i: (i, 0))
    line = pl.BlockSpec((block, 1), lambda i: (i, 0))
    area = block * block * reach * (length // block)
    return pl.pallas_call(
        functools.partial(attend_kernel, block, reach),
        grid=(length // block,),
        in_specs=[rows, whole, whole, line],
        out_specs=[rows, line],
        out_shape=[
            jax.ShapeDtypeStruct((length, HEAD_SIZE), jnp.bfloat16),
            jax.ShapeDtypeStruct((length, 1), jnp.float32),
        ],
        compiler_params=pltpu.CompilerParams(vmem_limit_bytes=40 * 2**20),
        cost_estimate=pl.CostEstimate(
            flops=4 * area * HEAD_SIZE, bytes_accessed=10 * length * HEAD_SIZE, transcendentals=2 * area
        ),
        name="attend",
    )(query, key, value, low_bound)


def attend_back(query, key, value, grad, low_bound, log_total, cosine, sine):
    length = query.shape[0]
    block, reach = block_shape(length)
    whole = pl.BlockSpec((length, HEAD_SIZE), lambda i: (0, 0))
    half = pl.BlockSpec((length, HEAD_SIZE // 2), lambda i: (0, 0))
    rows = pl.BlockSpec((block, HEAD_SIZE), lambda i: (i, 0))
    line = pl.BlockSpec((block, 1), lambda i: (i, 0))
    area = block * block * reach * (length // block)
    return pl.pallas_call(
        functools.partial(attend_back_kernel, block, reach),
        grid=(length // block,),
        in_specs=[rows, whole, whole, rows, line, line, half, half],
        out_specs=[rows, whole, whole],
        out_shape=[
            jax.ShapeDtypeStruct((length, HEAD_SIZE), jnp.bfloat16),
            jax.ShapeDtypeStruct((length, HEAD_SIZE), jnp.float32),
            jax.ShapeDtypeStruct((length, HEAD_SIZE), jnp.float32),
        ],
        compiler_params=pltpu.CompilerParams(vmem_limit_bytes=48 * 2**20),
        cost_estimate=pl.CostEstimate(
            flops=10 * area * HEAD_SIZE, bytes_accessed=24 * length * HEAD_SIZE, transcendentals=2 * area
        ),
        name="attend_back",
    )(query, key, value, grad, low_bound, log_total, cosine, sine)


class ByHeads:
    def __init__(self, w_query, key_weight, value_weight, w_out):
        place = lax.axis_index("seq")
        count = lax.axis_size("seq")
        layers = lax.axis_size("fsdp")
        half = HEAD_SIZE // 2

        def columns(weight, width):
            return lax.dynamic_slice_in_dim(weight, place * width, width, axis=1)

        joined = jnp.concatenate(
            [columns(w_query, HEAD_SIZE), columns(key_weight, half), columns(value_weight, half)],
            axis=1,
        )
        self.joined = line_gather(joined)
        own = self.joined[:, HEAD_SIZE:]
        other = lax.ppermute(own, "seq", [(i, i ^ 1) for i in range(count)])
        odd = place % 2 == 1
        low, high = jnp.where(odd, other, own), jnp.where(odd, own, other)
        self.weights = jnp.concatenate(
            [self.joined[:, :HEAD_SIZE], low[:, :half], high[:, :half], low[:, half:], high[:, half:]],
            axis=1,
        )
        depth = HEAD_SIZE // count
        here = QUERY_HEADS // layers
        part = w_out.reshape(here, count, depth, w_out.shape[1])
        part = lax.dynamic_index_in_dim(part, place, axis=1, keepdims=False)
        part = line_gather(part.reshape(here * depth, -1))
        self.out_rows = swap_parts(part, 0, 0)
        self.records = []

    def forward(self, normed, seg_whole):
        length = seg_whole.shape[0]
        whole = gather_tokens(normed)
        starts = doc_starts(seg_whole)
        places = jnp.arange(length, dtype=jnp.int32)
        low_bound = jnp.maximum(starts, places - (WIN - 1))[:, None]
        cosine, sine = angles(places - starts, HEAD_SIZE)
        cosine, sine = cosine[:, 0], sine[:, 0]
        rows = final_dot(whole, self.weights)
        query, key, value = (rows[:, HEAD_SIZE * i : HEAD_SIZE * (i + 1)] for i in range(3))
        query = rotate(query, cosine, sine, 1.0) * (1.0 / math.sqrt(HEAD_SIZE))
        query = query.astype(jnp.bfloat16)
        key = rotate(key, cosine, sine, 1.0).astype(jnp.bfloat16)
        value = value.astype(jnp.bfloat16)
        attended, log_total = attend(query, key, value, low_bound)
        mixed = scatter_tokens(final_dot(attended, self.out_rows))
        return mixed, (whole, query, key, value, low_bound, log_total, cosine, sine, attended)

    def backward(self, grad_mixed_b, saved):
        whole, query, key, value, low_bound, log_total, cosine, sine, attended = saved
        half = HEAD_SIZE // 2
        count = lax.axis_size("seq")
        grad_whole = gather_tokens(grad_mixed_b)
        grad_att = dot_back(grad_whole, self.out_rows).astype(jnp.bfloat16)
        dq, dk, dv = attend_back(
            query, key, value, grad_att, low_bound, log_total, cosine, sine
        )
        odd = lax.axis_index("seq") % 2 == 1
        low = jnp.concatenate([dk[:, :half], dv[:, :half]], axis=1)
        high = jnp.concatenate([dk[:, half:], dv[:, half:]], axis=1)
        away = jnp.where(odd, low, high)
        kept = jnp.where(odd, high, low)
        came = lax.ppermute(away, "seq", [(i, i ^ 1) for i in range(count)])
        dkv = (kept + came).astype(jnp.bfloat16)
        grads = jnp.concatenate([dq, dkv], axis=1)
        self.records.append((whole, grads, attended, grad_whole))
        return scatter_tokens(dot_back(grads, self.joined))

    def weight_grads(self):
        half = HEAD_SIZE // 2
        out = sum(dot_rows(r[2], r[3]) for r in self.records).astype(jnp.bfloat16)
        out = line_scatter(swap_parts(out, 1, 0))
        joined = sum(dot_rows(r[0], r[1]) for r in self.records).astype(jnp.bfloat16)
        joined = line_scatter(joined)
        return (
            joined[:, :HEAD_SIZE],
            joined[:, HEAD_SIZE : HEAD_SIZE + half],
            joined[:, HEAD_SIZE + half :],
            out,
        )


class ByTokens:
    def __init__(self, w_query, key_weight, value_weight, w_out):
        self.weights = fetch_attention(w_query, key_weight, value_weight, w_out)
        self.records = []

    def forward(self, normed, seg_whole):
        token_rows = normed.shape[0]
        halo_count = (WIN - 2 + token_rows) // token_rows
        w_query, key_weight, value_weight, w_out = self.weights
        seq_place = lax.axis_index("seq")
        seg_here = lax.dynamic_slice_in_dim(seg_whole, seq_place * token_rows, token_rows)
        position = jnp.arange(seg_whole.shape[0], dtype=jnp.int32) - doc_starts(seg_whole)
        position = lax.dynamic_slice_in_dim(position, seq_place * token_rows, token_rows)
        cosine, sine = angles(position, HEAD_SIZE)
        query = rotate(
            final_dot(normed, w_query).reshape(token_rows, QUERY_HEADS, HEAD_SIZE),
            cosine,
            sine,
            1.0,
        )
        query = (query * (1.0 / math.sqrt(HEAD_SIZE))).astype(jnp.bfloat16)
        key = rotate(
            final_dot(normed, key_weight).reshape(token_rows, KEY_VALUE_HEADS, HEAD_SIZE),
            cosine,
            sine,
            1.0,
        ).astype(jnp.bfloat16)
        value = final_dot(normed, value_weight).reshape(token_rows, KEY_VALUE_HEADS, HEAD_SIZE)
        pair = key_window(jnp.stack([key, value.astype(jnp.bfloat16)]), halo_count)
        allowed = window_mask(seg_here, seg_whole, seq_place, token_rows, halo_count)
        query = query.reshape(token_rows, KEY_VALUE_HEADS, -1, HEAD_SIZE)
        score = jnp.einsum("qhgd,khd->hgqk", query, pair[0], preferred_element_type=jnp.float32)
        capped = jnp.where(allowed, CAP * jnp.tanh(score / CAP), -jnp.inf)
        peak = jnp.max(capped, axis=-1, keepdims=True)
        power = jnp.exp(capped - peak)
        total = jnp.sum(power, axis=-1, keepdims=True)
        attended = jnp.einsum(
            "hgqk,khd->qhgd",
            (power / total).astype(jnp.bfloat16),
            pair[1],
            preferred_element_type=jnp.float32,
        )
        attended = attended.reshape(token_rows, QUERY_HEADS * HEAD_SIZE).astype(jnp.bfloat16)
        mixed = final_dot(attended, w_out)
        log_total = peak + jnp.log(total)
        return mixed, (normed, query, pair, allowed, log_total, cosine, sine, attended)

    def backward(self, grad_mixed_b, saved):
        normed, query, pair, allowed, log_total, cosine, sine, attended = saved
        token_rows = normed.shape[0]
        halo_count = (WIN - 2 + token_rows) // token_rows
        w_query, key_weight, value_weight, w_out = self.weights
        grad_att = dot_back(grad_mixed_b, w_out).astype(jnp.bfloat16)
        grad_att = grad_att.reshape(token_rows, KEY_VALUE_HEADS, -1, HEAD_SIZE)
        score = jnp.einsum("qhgd,khd->hgqk", query, pair[0], preferred_element_type=jnp.float32)
        bent = jnp.tanh(score / CAP)
        prob = jnp.exp(jnp.where(allowed, CAP * bent, -jnp.inf) - log_total)
        grad_prob = jnp.einsum(
            "qhgd,khd->hgqk", grad_att, pair[1], preferred_element_type=jnp.float32
        )
        delta = jnp.sum(prob * grad_prob, axis=-1, keepdims=True)
        grad_score = (prob * (grad_prob - delta) * (1.0 - bent * bent)).astype(jnp.bfloat16)
        dq = jnp.einsum("hgqk,khd->qhgd", grad_score, pair[0], preferred_element_type=jnp.float32)
        dk = jnp.einsum("hgqk,qhgd->khd", grad_score, query, preferred_element_type=jnp.float32)
        dv = jnp.einsum(
            "hgqk,qhgd->khd", prob.astype(jnp.bfloat16), grad_att, preferred_element_type=jnp.float32
        )
        paired = window_grads(jnp.stack([dk, dv]), halo_count, token_rows)
        dq = rotate(
            dq.reshape(token_rows, QUERY_HEADS, HEAD_SIZE) * (1.0 / math.sqrt(HEAD_SIZE)),
            cosine,
            sine,
            -1.0,
        )
        dq = dq.reshape(token_rows, -1).astype(jnp.bfloat16)
        dk = rotate(paired[0], cosine, sine, -1.0).reshape(token_rows, -1).astype(jnp.bfloat16)
        dv = paired[1].reshape(token_rows, -1).astype(jnp.bfloat16)
        self.records.append((normed, dq, dk, dv, attended, grad_mixed_b))
        return dot_back(dq, w_query) + dot_back(dk, key_weight) + dot_back(dv, value_weight)

    def weight_grads(self):
        normed, dq, dk, dv, attended, grad_mixed_b = (
            jnp.concatenate(parts, axis=0) for parts in zip(*self.records)
        )
        normed, attended = gather_tokens(normed), gather_tokens(attended)
        sums = []
        for rows, grads in ((normed, dq), (normed, dk), (normed, dv), (attended, grad_mixed_b)):
            column_sum = dot_rows(rows, swap_parts(grads, 1, 0)).astype(jnp.bfloat16)
            owned = lax.psum_scatter(column_sum, "fsdp", scatter_dimension=0, tiled=True)
            sums.append(owned.astype(jnp.float32))
        return tuple(sums)


class FeedForward:
    def __init__(self, w_gate, w_up, w_down):
        place = lax.axis_index("seq")
        count = lax.axis_size("seq")
        hidden = w_gate.shape[1]
        self.run = hidden // (count * count)

        def columns(weight):
            parts = [
                lax.dynamic_slice_in_dim(
                    weight, (t * count + place) * self.run, self.run, axis=1
                )
                for t in range(count)
            ]
            return jnp.concatenate(parts, axis=1)

        here = w_down.shape[0] // (count * self.run)
        part = w_down.reshape(here, count, self.run, w_down.shape[1])
        part = lax.dynamic_index_in_dim(part, place, axis=1, keepdims=False)
        self.gate = line_gather(columns(w_gate))
        self.up = line_gather(columns(w_up))
        self.down = line_gather(part.reshape(here * self.run, -1))
        self.records = []

    def forward(self, ffn_in):
        whole = gather_tokens(ffn_in)
        gate_proj = final_dot(whole, self.gate)
        up_proj = final_dot(whole, self.up)
        hidden = geglu(gate_proj, up_proj).astype(jnp.bfloat16)
        down_proj = scatter_tokens(final_dot(hidden, self.down))
        return down_proj, (whole, gate_proj, up_proj, hidden)

    def backward(self, grad_down_b, saved):
        whole, gate_proj, up_proj, hidden = saved
        grad_whole = gather_tokens(grad_down_b)
        grad_hidden = dot_back(grad_whole, self.down)
        _, pullback = jax.vjp(geglu, gate_proj, up_proj)
        grad_gate, grad_up = pullback(grad_hidden)
        grad_gate, grad_up = grad_gate.astype(jnp.bfloat16), grad_up.astype(jnp.bfloat16)
        self.records.append((whole, hidden, grad_whole, grad_gate, grad_up))
        return scatter_tokens(dot_back(grad_gate, self.gate) + dot_back(grad_up, self.up))

    def weight_grads(self):
        down = sum(dot_rows(r[1], r[2]) for r in self.records).astype(jnp.bfloat16)
        gate = sum(dot_rows(r[0], r[3]) for r in self.records).astype(jnp.bfloat16)
        up = sum(dot_rows(r[0], r[4]) for r in self.records).astype(jnp.bfloat16)
        count = lax.axis_size("seq")

        down = line_scatter(down).astype(jnp.bfloat16)
        here = down.shape[0] // self.run
        down = swap_parts(down.reshape(1, here, self.run, -1), 3, 0)
        down = down.transpose(1, 0, 2, 3).reshape(here * count * self.run, -1)

        def columns(summed):
            summed = line_scatter(summed).astype(jnp.bfloat16)
            return swap_parts(summed, 1, 1).astype(jnp.float32)

        return columns(gate), columns(up), down.astype(jnp.float32)


def on_device(
    tokens,
    segments,
    w_query,
    key_weight,
    value_weight,
    w_out,
    w_gate,
    w_up,
    w_down,
    gain_attn_in,
    gain_attn_out,
    gain_ffn_in,
    gain_ffn_out,
    cotangent,
):
    micro_count = tokens.shape[0]
    seg_gathered = lax.all_gather(segments, "seq", axis=2, tiled=True)
    by_heads = lax.axis_size("seq") == QUERY_HEADS and QUERY_HEADS % lax.axis_size("fsdp") == 0
    attention = (ByHeads if by_heads else ByTokens)(w_query, key_weight, value_weight, w_out)
    ffn = FeedForward(w_gate, w_up, w_down)
    results, input_grads = [], []
    gain_early = jnp.zeros((3, tokens.shape[3]), jnp.float32)
    gain_late = jnp.zeros((1, tokens.shape[3]), jnp.float32)
    for batch_index in range(micro_count):
        stream = tokens[batch_index, 0].astype(jnp.float32)
        normed = rms_gain(stream, gain_attn_in).astype(jnp.bfloat16)
        mixed, attention_saved = attention.forward(normed, seg_gathered[batch_index, 0])
        middle = stream + rms_gain(mixed, gain_attn_out)
        ffn_in = rms_gain(middle, gain_ffn_in).astype(jnp.bfloat16)
        down_proj, ffn_saved = ffn.forward(ffn_in)
        result = middle + rms_gain(down_proj, gain_ffn_out)
        results.append(result.astype(jnp.bfloat16))

        grad_result = cotangent[batch_index, 0].astype(jnp.float32)
        _, pullback = jax.vjp(rms_gain, down_proj, gain_ffn_out)
        grad_down, grad_gain_four = pullback(grad_result)
        grad_ffn_in = ffn.backward(grad_down.astype(jnp.bfloat16), ffn_saved)
        _, pullback = jax.vjp(rms_gain, middle, gain_ffn_in)
        grad_middle, grad_gain_three = pullback(grad_ffn_in)
        grad_middle = grad_result + grad_middle
        _, pullback = jax.vjp(rms_gain, mixed, gain_attn_out)
        grad_mixed, grad_gain_two = pullback(grad_middle)
        grad_normed = attention.backward(grad_mixed.astype(jnp.bfloat16), attention_saved)
        _, pullback = jax.vjp(rms_gain, stream, gain_attn_in)
        grad_stream, grad_gain_one = pullback(grad_normed)
        input_grads.append(grad_middle + grad_stream)
        gain_early = gain_early + jnp.stack([grad_gain_two, grad_gain_three, grad_gain_four])
        gain_late = gain_late + grad_gain_one[None]
    grad_gate, grad_up, grad_down = ffn.weight_grads()
    grad_query, grad_key, grad_value, grad_out = attention.weight_grads()
    gain_early = lax.psum(gain_early, ("seq", "fsdp"))
    gain_late = lax.psum(gain_late, ("seq", "fsdp"))
    return (
        jnp.stack(results)[:, None],
        jnp.stack(input_grads)[:, None],
        grad_query,
        grad_key,
        grad_value,
        grad_out,
        grad_gate,
        grad_up,
        grad_down,
        gain_late[0],
        gain_early[0],
        gain_early[1],
        gain_early[2],
    )


def solution(mesh):
    in_specs = (
        P(None, "fsdp", "seq", None),
        P(None, "fsdp", "seq"),
        P("fsdp", None),
        P("fsdp", None),
        P("fsdp", None),
        P("fsdp", None),
        P("fsdp", None),
        P("fsdp", None),
        P("fsdp", None),
        P(),
        P(),
        P(),
        P(),
        P(None, "fsdp", "seq", None),
    )
    out_specs = (
        P(None, "fsdp", "seq", None),
        P(None, "fsdp", "seq", None),
        P("fsdp", "seq"),
        P("fsdp", "seq"),
        P("fsdp", "seq"),
        P("fsdp", "seq"),
        P("fsdp", "seq"),
        P("fsdp", "seq"),
        P("fsdp", "seq"),
        P(),
        P(),
        P(),
        P(),
    )
    return jax.shard_map(
        on_device, mesh=mesh, in_specs=in_specs, out_specs=out_specs, check_vma=False
    )
```

```python
import functools
import math

import jax
import jax.numpy as jnp
from jax import lax
from jax.experimental import pallas as pl
from jax.experimental.pallas import tpu as pltpu
from jax.sharding import PartitionSpec as P

QUERY_HEADS = 8
KEY_VALUE_HEADS = 4
HEAD_SIZE = 256
CAP = 50
WIN = 1024
DOCUMENTS = 4
VMEM_LIMIT = 60 * 2**20
SPAN_BYTES = 270_000_000


epsilon = 1e-06


def shifted(value, axis, steps):
    count = lax.axis_size(axis)
    initial, last = (max(0, -steps), min(count, count - steps))
    return lax.ppermute(value, axis, [(source, source + steps) for source in range(initial, last)])


def rms_gain(stream, gain):
    return stream * lax.rsqrt(jnp.mean(stream * stream, axis=-1, keepdims=True) + epsilon) * gain


def geglu(gate_proj, up_proj):
    return jax.nn.gelu(gate_proj, approximate=True) * up_proj


def angles(position, size):
    frequency = 10000.0 ** (-jnp.arange(size // 2, dtype=jnp.float32) * 2.0 / size)
    phase_angle = position.astype(jnp.float32)[..., None] * frequency
    return (jnp.cos(phase_angle), jnp.sin(phase_angle))


def rotate(value_rows, cosine_table, sine_table, direction):
    half_size = value_rows.shape[-1] // 2
    first_half = value_rows[..., :half_size]
    second = value_rows[..., half_size:]
    return jnp.concatenate(
        [
            first_half * cosine_table - direction * second * sine_table,
            second * cosine_table + direction * first_half * sine_table,
        ],
        axis=-1,
    )


def doc_starts(segment):
    starts = jnp.zeros_like(segment)
    for number in range(1, DOCUMENTS):
        count = jnp.sum((segment < number).astype(jnp.int32), axis=-1, keepdims=True)
        starts = jnp.where(segment >= number, count, starts)
    return starts


def final_dot(left_side, right_side):
    return jnp.dot(left_side, right_side, preferred_element_type=jnp.float32)


def dot_back(left_side, right_side):
    contract = (((left_side.ndim - 1,), (1,)), ((), ()))
    return lax.dot_general(left_side, right_side, contract, preferred_element_type=jnp.float32)


def dot_rows(left_side, right_side):
    left_side = left_side.reshape(-1, left_side.shape[-1])
    right_side = right_side.reshape(-1, right_side.shape[-1])
    return lax.dot_general(
        left_side, right_side, (((0,), (0,)), ((), ())), preferred_element_type=jnp.float32
    )


def fetch_attention(w_query, key_weight, value_weight, w_out):
    return (
        lax.all_gather(w_query, "fsdp", axis=0, tiled=True),
        lax.all_gather(key_weight, "fsdp", axis=0, tiled=True),
        lax.all_gather(value_weight, "fsdp", axis=0, tiled=True),
        lax.all_gather(w_out, "fsdp", axis=0, tiled=True),
    )


def key_window(kv_pair, halo_count):
    arrived = [shifted(kv_pair, "seq", offset) for offset in range(halo_count, 0, -1)]
    return jnp.concatenate(arrived + [kv_pair], axis=1)


def window_grads(paired_gradient, halo_count, token_rows):
    summed = paired_gradient[:, halo_count * token_rows :]
    for offset in range(1, halo_count + 1):
        begin = (halo_count - offset) * token_rows
        summed = summed + shifted(
            paired_gradient[:, begin : begin + token_rows].astype(jnp.bfloat16), "seq", -offset
        ).astype(jnp.float32)
    return summed


def window_mask(seg_here, seg_whole, seq_place, token_rows, halo_count):
    padded = jnp.concatenate([jnp.full((halo_count * token_rows,), -1, jnp.int32), seg_whole])
    key_seg = lax.dynamic_slice_in_dim(
        padded, seq_place * token_rows, (halo_count + 1) * token_rows
    )
    query_pos = seq_place * token_rows + jnp.arange(token_rows, dtype=jnp.int32)
    key_pos = (
        seq_place * token_rows
        - halo_count * token_rows
        + jnp.arange((halo_count + 1) * token_rows, dtype=jnp.int32)
    )
    distance = query_pos[:, None] - key_pos[None, :]
    return (seg_here[:, None] == key_seg[None, :]) & (distance >= 0) & (distance < WIN)


def gather_rows(rows):
    return lax.all_gather(rows, "fsdp", axis=0, tiled=True)


def scatter_rows(partial):
    summed = lax.psum_scatter(
        partial.astype(jnp.bfloat16), "fsdp", scatter_dimension=0, tiled=True
    )
    return summed.astype(jnp.float32)


def swap_parts(value, split_axis, concat_axis):
    return lax.all_to_all(
        value, "seq", split_axis=split_axis, concat_axis=concat_axis, tiled=True
    )


MESH = pl.DeviceIdType.MESH


def plane_places():
    me = lax.axis_index("seq")
    other_core = me + 1 - 2 * (me % 2)
    along_x = me + 2 - 4 * ((me // 2) % 2)
    along_y = me + 4 - 8 * (me // 4)
    return me, other_core, along_x, along_y


def greet(neighbours):
    barrier = pltpu.get_barrier_semaphore()
    for neighbour in neighbours:
        pl.semaphore_signal(barrier, inc=1, device_id={"seq": neighbour}, device_id_type=MESH)
    pl.semaphore_wait(barrier, len(neighbours))


def gather_kernel(counts, rows, compute, *refs):
    weight_count, extra_count, out_count = counts
    refs = list(refs)
    take = lambda n: [refs.pop(0) for _ in range(n)]
    (local_ref,), weight_refs, extra_refs = take(1), take(weight_count), take(extra_count)
    (whole_ref,), out_refs = take(1), take(out_count)
    send_sem, recv_sem, own_sem = take(3)
    if compute is not None:
        (x_buf,), weight_bufs, extra_bufs, out_bufs = (
            take(1),
            take(weight_count),
            take(extra_count),
            take(out_count),
        )
        weight_sem, load_sem, store_sem = take(3)

    me, other_core, along_x, along_y = plane_places()
    across = along_x + along_y - me

    def piece(batch, place):
        return whole_ref.at[batch, pl.ds(pl.multiple_of(place * rows, 16), rows)]

    def transfer(slot, source, batch, place, target):
        return pltpu.make_async_remote_copy(
            src_ref=source,
            dst_ref=piece(batch, place),
            send_sem=send_sem.at[slot],
            recv_sem=recv_sem.at[slot],
            device_id={"seq": target},
            device_id_type=MESH,
        )

    def forward(slot, batch, place, target):
        return transfer(slot, piece(batch, place), batch, place, target)

    moves = [
        transfer(0, local_ref.at[0], 0, me, along_x),
        transfer(1, local_ref.at[1], 1, me, along_x),
        transfer(2, local_ref.at[1], 1, me, along_y),
        transfer(3, local_ref.at[0], 0, me, along_y),
        forward(4, 0, along_x, along_y),
        forward(5, 1, along_y, along_x),
        transfer(6, local_ref.at[0], 0, me, other_core),
        transfer(7, local_ref.at[1], 1, me, other_core),
        forward(8, 0, along_x, other_core),
        forward(9, 1, along_x, other_core),
        forward(10, 1, along_y, other_core),
        forward(11, 0, along_y, other_core),
        forward(12, 0, across, other_core),
        forward(13, 1, across, other_core),
    ]
    greet((other_core, along_x, along_y))
    for slot in (0, 2, 6, 7, 1, 3):
        moves[slot].start()
    owns = [
        pltpu.make_async_copy(local_ref.at[batch], piece(batch, me), own_sem.at[batch])
        for batch in range(2)
    ]
    for own in owns:
        own.start()
    if compute is not None:
        fetches = [
            pltpu.make_async_copy(ref, buf, weight_sem.at[i])
            for i, (ref, buf) in enumerate(zip(weight_refs, weight_bufs))
        ]
        for fetch in fetches:
            fetch.start()
    stores = []

    def unit(place, batch):
        if compute is None:
            return
        span = pl.ds(pl.multiple_of((place // 2) * (2 * rows), 16), 2 * rows)
        loads = [
            pltpu.make_async_copy(ref.at[batch, span], buf, load_sem.at[i])
            for i, (ref, buf) in enumerate(
                zip([whole_ref] + extra_refs, [x_buf] + extra_bufs)
            )
        ]
        for load in loads:
            load.start()
        step = len(stores)
        if step == 0:
            for fetch in fetches:
                fetch.wait()
        if step >= 2:
            for store in stores[step - 2]:
                store.wait()
        for load in loads:
            load.wait()
        slot = step % 2
        compute(x_buf, weight_bufs, extra_bufs, [buf.at[slot] for buf in out_bufs])
        stores.append(
            [
                pltpu.make_async_copy(buf.at[slot], ref.at[batch, span], store_sem.at[slot, i])
                for i, (ref, buf) in enumerate(zip(out_refs, out_bufs))
            ]
        )
        for store in stores[-1]:
            store.start()

    for batch in range(2):
        owns[batch].wait()
        moves[6 + batch].wait_recv()
        unit(me, batch)
    moves[0].wait_recv()
    moves[4].start()
    moves[8].start()
    moves[2].wait_recv()
    moves[5].start()
    moves[10].start()
    moves[8].wait_recv()
    unit(along_x, 0)
    moves[10].wait_recv()
    unit(along_y, 1)
    moves[1].wait_recv()
    moves[9].start()
    moves[3].wait_recv()
    moves[11].start()
    moves[9].wait_recv()
    unit(along_x, 1)
    moves[11].wait_recv()
    unit(along_y, 0)
    moves[4].wait_recv()
    moves[12].start()
    moves[5].wait_recv()
    moves[13].start()
    moves[12].wait_recv()
    unit(across, 0)
    moves[13].wait_recv()
    unit(across, 1)
    for move in moves:
        move.wait_send()
    for group in stores[-2:]:
        for store in group:
            store.wait()


def plane_gather(local, ident, name, weights=(), extras=(), outs=(), compute=None, flops=0):
    batches, rows, width = local.shape
    length = rows * lax.axis_size("seq")
    whole = jax.ShapeDtypeStruct((batches, length, width), local.dtype)
    scratch = [
        pltpu.SemaphoreType.DMA((14,)),
        pltpu.SemaphoreType.DMA((14,)),
        pltpu.SemaphoreType.DMA((2,)),
    ]
    if compute is not None:
        scratch += [pltpu.VMEM((2 * rows, width), local.dtype)]
        scratch += [pltpu.VMEM(weight.shape, weight.dtype) for weight in weights]
        scratch += [pltpu.VMEM((2 * rows, extra.shape[2]), extra.dtype) for extra in extras]
        scratch += [pltpu.VMEM((2, 2 * rows, wide), kind) for wide, kind in outs]
        scratch += [
            pltpu.SemaphoreType.DMA((len(weights),)),
            pltpu.SemaphoreType.DMA((1 + len(extras),)),
            pltpu.SemaphoreType.DMA((2, len(outs))),
        ]
    any_space = pl.BlockSpec(memory_space=pl.ANY)
    out_shape = [whole] + [
        jax.ShapeDtypeStruct((batches, length, wide), kind) for wide, kind in outs
    ]
    return pl.pallas_call(
        functools.partial(
            gather_kernel, (len(weights), len(extras), len(outs)), rows, compute
        ),
        in_specs=[any_space] * (1 + len(weights) + len(extras)),
        out_specs=[any_space] * len(out_shape),
        out_shape=out_shape,
        scratch_shapes=scratch,
        compiler_params=pltpu.CompilerParams(
            collective_id=ident, has_side_effects=True, vmem_limit_bytes=VMEM_LIMIT
        ),
        cost_estimate=pl.CostEstimate(
            flops=flops, bytes_accessed=SPAN_BYTES, transcendentals=0
        ),
        name=name,
    )(local, *weights, *extras)


def scatter_kernel(counts, rows, compute, *refs):
    part_count, weight_count = counts
    refs = list(refs)
    take = lambda n: [refs.pop(0) for _ in range(n)]
    part_refs, weight_refs, (out_ref,) = take(part_count), take(weight_count), take(1)
    part_bufs, weight_bufs = take(part_count), take(weight_count)
    sums, from_core, from_link, out_buf = take(4)
    weight_sem, load_sem, out_sem, core_send, core_recv, link_send, link_recv = take(7)

    me, other_core, along_x, along_y = plane_places()
    across = along_x + along_y - me
    core = me % 2
    kept = pl.ds(pl.multiple_of(core * rows, 16), rows)
    given = pl.ds(pl.multiple_of((1 - core) * rows, 16), rows)
    units = [
        (across, 0),
        (across, 1),
        (along_x, 0),
        (along_y, 1),
        (along_x, 1),
        (along_y, 0),
        (me, 0),
        (me, 1),
    ]
    targets = [along_x, along_y, along_x, along_y, along_x, along_y]
    added = {4: (1,), 5: (0,), 6: (2, 5), 7: (3, 4)}

    def load(step):
        place, batch = units[step]
        span = pl.ds(pl.multiple_of((place // 2) * (2 * rows), 16), 2 * rows)
        return [
            pltpu.make_async_copy(ref.at[batch, span], buf.at[step % 2], load_sem.at[step % 2, i])
            for i, (ref, buf) in enumerate(zip(part_refs, part_bufs))
        ]

    loads = [load(step) for step in range(8)]
    fetches = [
        pltpu.make_async_copy(ref, buf, weight_sem.at[i])
        for i, (ref, buf) in enumerate(zip(weight_refs, weight_bufs))
    ]
    for copy in loads[0] + fetches:
        copy.start()
    gives = [
        pltpu.make_async_remote_copy(
            src_ref=sums.at[step, given],
            dst_ref=from_core.at[step],
            send_sem=core_send.at[step],
            recv_sem=core_recv.at[step],
            device_id={"seq": other_core},
            device_id_type=MESH,
        )
        for step in range(8)
    ]
    sends = [
        pltpu.make_async_remote_copy(
            src_ref=sums.at[step, kept],
            dst_ref=from_link.at[step],
            send_sem=link_send.at[step],
            recv_sem=link_recv.at[step],
            device_id={"seq": targets[step]},
            device_id_type=MESH,
        )
        for step in range(6)
    ]
    greet((other_core, along_x, along_y))
    outs = []

    def finish(step):
        gives[step].wait_recv()
        total = sums[step, kept].astype(jnp.float32) + from_core[step].astype(jnp.float32)
        for arrived in added.get(step, ()):
            sends[arrived].wait_recv()
            total = total + from_link[arrived].astype(jnp.float32)
        if step < 6:
            sums[step, kept] = total.astype(jnp.bfloat16)
            sends[step].start()
        else:
            out_buf[step - 6] = total
            outs.append(
                pltpu.make_async_copy(
                    out_buf.at[step - 6], out_ref.at[step - 6], out_sem.at[step - 6]
                )
            )
            outs[-1].start()

    for step in range(8):
        for copy in loads[step]:
            copy.wait()
        if step == 0:
            for fetch in fetches:
                fetch.wait()
        if step < 7:
            for copy in loads[step + 1]:
                copy.start()
        compute([buf.at[step % 2] for buf in part_bufs], weight_bufs, sums.at[step])
        gives[step].start()
        if step >= 1:
            finish(step - 1)
    finish(7)
    for move in gives + sends:
        move.wait_send()
    for out in outs:
        out.wait()


def plane_scatter(parts, weights, compute, width, ident, name, flops):
    batches, length = parts[0].shape[:2]
    rows = length // lax.axis_size("seq")
    any_space = pl.BlockSpec(memory_space=pl.ANY)
    scratch = [pltpu.VMEM((2, 2 * rows, part.shape[2]), part.dtype) for part in parts]
    scratch += [pltpu.VMEM(weight.shape, weight.dtype) for weight in weights]
    scratch += [
        pltpu.VMEM((8, 2 * rows, width), jnp.bfloat16),
        pltpu.VMEM((8, rows, width), jnp.bfloat16),
        pltpu.VMEM((6, rows, width), jnp.bfloat16),
        pltpu.VMEM((2, rows, width), jnp.float32),
        pltpu.SemaphoreType.DMA((len(weights),)),
        pltpu.SemaphoreType.DMA((2, len(parts))),
        pltpu.SemaphoreType.DMA((2,)),
        pltpu.SemaphoreType.DMA((8,)),
        pltpu.SemaphoreType.DMA((8,)),
        pltpu.SemaphoreType.DMA((6,)),
        pltpu.SemaphoreType.DMA((6,)),
    ]
    return pl.pallas_call(
        functools.partial(scatter_kernel, (len(parts), len(weights)), rows, compute),
        in_specs=[any_space] * (len(parts) + len(weights)),
        out_specs=any_space,
        out_shape=jax.ShapeDtypeStruct((batches, rows, width), jnp.float32),
        scratch_shapes=scratch,
        compiler_params=pltpu.CompilerParams(
            collective_id=ident, has_side_effects=True, vmem_limit_bytes=VMEM_LIMIT
        ),
        cost_estimate=pl.CostEstimate(
            flops=flops, bytes_accessed=SPAN_BYTES, transcendentals=0
        ),
        name=name,
    )(*parts, *weights)


TILE = 384


def tiles(width, body):
    tile = TILE if width % TILE == 0 else 128

    def step(index, carry):
        body(pl.ds(pl.multiple_of(index * tile, tile), tile))
        return carry

    lax.fori_loop(0, width // tile, step, 0)


GELU_SCALE = 0.7978845608
GELU_CUBE = 0.044715


def gelu_parts(gate):
    square = gate * gate
    bent = jnp.tanh(GELU_SCALE * gate * (1.0 + GELU_CUBE * square))
    half = 0.5 * (1.0 + bent)
    slope = half + 0.5 * gate * (1.0 - bent * bent) * GELU_SCALE * (1.0 + 3.0 * GELU_CUBE * square)
    return gate * half, slope


def hidden_compute(x_buf, weights, extras, outs):
    gate_w, up_w = weights
    gate_out, up_out, hidden_out = outs

    def body(span):
        gate = final_dot(x_buf[...], gate_w[:, span])
        up = final_dot(x_buf[...], up_w[:, span])
        gate_out[:, span] = gate.astype(gate_out.dtype)
        up_out[:, span] = up.astype(up_out.dtype)
        hidden_out[:, span] = (gelu_parts(gate)[0] * up).astype(hidden_out.dtype)

    tiles(gate_w.shape[1], body)


def hidden_back_compute(x_buf, weights, extras, outs):
    (down_w,) = weights
    gate_in, up_in = extras
    gate_out, up_out = outs

    def body(span):
        grad = dot_back(x_buf[...], down_w[span, :])
        value, slope = gelu_parts(gate_in[:, span].astype(jnp.float32))
        gate_out[:, span] = (grad * up_in[:, span].astype(jnp.float32) * slope).astype(
            gate_out.dtype
        )
        up_out[:, span] = (grad * value).astype(up_out.dtype)

    tiles(down_w.shape[0], body)


def rows_compute(parts, weights, out):
    def body(span):
        out[:, span] = final_dot(parts[0][...], weights[0][:, span]).astype(out.dtype)

    tiles(weights[0].shape[1], body)


def back_compute(parts, weights, out):
    def body(span):
        total = dot_back(parts[0][...], weights[0][span, :])
        for part, weight in zip(parts[1:], weights[1:]):
            total = total + dot_back(part[...], weight[span, :])
        out[:, span] = total.astype(out.dtype)

    tiles(weights[0].shape[0], body)


def head_back_compute(x_buf, weights, extras, outs):
    outs[0][...] = dot_back(x_buf[...], weights[0][...]).astype(outs[0].dtype)


def score_parts(query, key, low_bound, row_start, col_start):
    raw = lax.dot_general(
        query, key, (((1,), (1,)), ((), ())), preferred_element_type=jnp.float32
    )
    bent = jnp.tanh(raw * (1.0 / CAP))
    shape = raw.shape
    row = row_start + lax.broadcasted_iota(jnp.int32, shape, 0)
    col = col_start + lax.broadcasted_iota(jnp.int32, shape, 1)
    allowed = (col <= row) & (col >= low_bound)
    return bent, jnp.where(allowed, CAP * bent, -1e30)


def attend_kernel(block, reach, q_ref, k_ref, v_ref, low_ref, out_ref, log_ref):
    index = pl.program_id(1)

    def run(blocks):
        first = (index - (blocks - 1)) * block
        span = pl.ds(pl.multiple_of(first, block), blocks * block)
        _, capped = score_parts(
            q_ref[...], k_ref[span, :], low_ref[...], index * block, first
        )
        peak = jnp.max(capped, axis=-1, keepdims=True)
        power = jnp.exp(capped - peak)
        total = jnp.sum(power, axis=-1, keepdims=True)
        prob = (power * (1.0 / total)).astype(jnp.bfloat16)
        out = jnp.dot(prob, v_ref[span, :], preferred_element_type=jnp.float32)
        out_ref[...] = out.astype(jnp.bfloat16)
        log_ref[...] = peak + jnp.log(total)

    for blocks in range(1, reach + 1):
        if blocks < reach:
            pl.when(index == blocks - 1)(functools.partial(run, blocks))
        else:
            pl.when(index >= blocks - 1)(functools.partial(run, blocks))


def turn_back(value, cosine, sine):
    half = value.shape[-1] // 2
    first, second = value[:, :half], value[:, half:]
    return jnp.concatenate(
        [first * cosine + second * sine, second * cosine - first * sine], axis=-1
    )


def attend_back_kernel(
    block,
    reach,
    q_ref,
    k_ref,
    v_ref,
    g_ref,
    low_ref,
    log_ref,
    cos_ref,
    sin_ref,
    dq_ref,
    low_out_ref,
    high_out_ref,
    dk_ref,
    dv_ref,
):
    index = pl.program_id(1)
    steps = pl.num_programs(1)

    @pl.when(index == 0)
    def _():
        dk_ref[...] = jnp.zeros_like(dk_ref)
        dv_ref[...] = jnp.zeros_like(dv_ref)

    own = pl.ds(pl.multiple_of(index * block, block), block)

    def run(blocks):
        first = (index - (blocks - 1)) * block
        span = pl.ds(pl.multiple_of(first, block), blocks * block)
        query, grad = q_ref[...], g_ref[...]
        key = k_ref[span, :]
        bent, capped = score_parts(query, key, low_ref[...], index * block, first)
        prob = jnp.exp(capped - log_ref[...])
        grad_prob = lax.dot_general(
            grad, v_ref[span, :], (((1,), (1,)), ((), ())), preferred_element_type=jnp.float32
        )
        delta = jnp.sum(prob * grad_prob, axis=-1, keepdims=True)
        grad_score = (prob * (grad_prob - delta) * (1.0 - bent * bent)).astype(jnp.bfloat16)
        dq = jnp.dot(grad_score, key, preferred_element_type=jnp.float32)
        dq = dq * (1.0 / math.sqrt(HEAD_SIZE))
        dq_ref[...] = turn_back(dq, cos_ref[own, :], sin_ref[own, :]).astype(jnp.bfloat16)
        across = (((0,), (0,)), ((), ()))
        dk_ref[span, :] += lax.dot_general(
            grad_score, query, across, preferred_element_type=jnp.float32
        )
        dv_ref[span, :] += lax.dot_general(
            prob.astype(jnp.bfloat16), grad, across, preferred_element_type=jnp.float32
        )

    for blocks in range(1, reach + 1):
        if blocks < reach:
            pl.when(index == blocks - 1)(functools.partial(run, blocks))
        else:
            pl.when(index >= blocks - 1)(functools.partial(run, blocks))

    @pl.when(index == steps - 1)
    def _():
        half = HEAD_SIZE // 2
        dk = turn_back(dk_ref[...], cos_ref[...], sin_ref[...])
        for part, out_ref in enumerate((low_out_ref, high_out_ref)):
            lanes = slice(part * half, (part + 1) * half)
            out_ref[:, :half] = dk[:, lanes].astype(jnp.bfloat16)
            out_ref[:, half:] = dv_ref[:, lanes].astype(jnp.bfloat16)


def block_shape(length):
    for block in (384, 256, 128):
        if length % block == 0:
            reach = min(length // block, (WIN - 1 + block - 1) // block + 1)
            return block, reach
    raise ValueError("sequence length")


def attend_specs(length, block):
    whole = pl.BlockSpec((None, length, HEAD_SIZE), lambda m, i: (m, 0, 0))
    half = pl.BlockSpec((None, length, HEAD_SIZE // 2), lambda m, i: (m, 0, 0))
    rows = pl.BlockSpec((None, block, HEAD_SIZE), lambda m, i: (m, i, 0))
    line = pl.BlockSpec((None, block, 1), lambda m, i: (m, i, 0))
    return whole, half, rows, line


def attend(query, key, value, low_bound):
    batches, length = query.shape[:2]
    block, reach = block_shape(length)
    whole, half, rows, line = attend_specs(length, block)
    area = batches * block * block * reach * (length // block)
    return pl.pallas_call(
        functools.partial(attend_kernel, block, reach),
        grid=(batches, length // block),
        in_specs=[rows, whole, whole, line],
        out_specs=[rows, line],
        out_shape=[
            jax.ShapeDtypeStruct((batches, length, HEAD_SIZE), jnp.bfloat16),
            jax.ShapeDtypeStruct((batches, length, 1), jnp.float32),
        ],
        compiler_params=pltpu.CompilerParams(vmem_limit_bytes=40 * 2**20),
        cost_estimate=pl.CostEstimate(
            flops=4 * area * HEAD_SIZE,
            bytes_accessed=10 * batches * length * HEAD_SIZE,
            transcendentals=2 * area,
        ),
        name="attend",
    )(query, key, value, low_bound)


def attend_back(query, key, value, grad, low_bound, log_total, cosine, sine):
    batches, length = query.shape[:2]
    block, reach = block_shape(length)
    whole, half, rows, line = attend_specs(length, block)
    area = batches * block * block * reach * (length // block)
    return pl.pallas_call(
        functools.partial(attend_back_kernel, block, reach),
        grid=(batches, length // block),
        in_specs=[rows, whole, whole, rows, line, line, half, half],
        out_specs=[rows, whole, whole],
        out_shape=[jax.ShapeDtypeStruct((batches, length, HEAD_SIZE), jnp.bfloat16)] * 3,
        scratch_shapes=[pltpu.VMEM((length, HEAD_SIZE), jnp.float32)] * 2,
        compiler_params=pltpu.CompilerParams(vmem_limit_bytes=48 * 2**20),
        cost_estimate=pl.CostEstimate(
            flops=10 * area * HEAD_SIZE,
            bytes_accessed=24 * batches * length * HEAD_SIZE,
            transcendentals=2 * area,
        ),
        name="attend_back",
    )(query, key, value, grad, low_bound, log_total, cosine, sine)


class ByHeads:
    def __init__(self, w_query, key_weight, value_weight, w_out):
        place = lax.axis_index("seq")
        count = lax.axis_size("seq")
        layers = lax.axis_size("fsdp")
        half = HEAD_SIZE // 2

        def columns(weight, width):
            return lax.dynamic_slice_in_dim(weight, place * width, width, axis=1)

        joined = jnp.concatenate(
            [columns(w_query, HEAD_SIZE), columns(key_weight, half), columns(value_weight, half)],
            axis=1,
        )
        self.joined = gather_rows(joined)
        own = self.joined[:, HEAD_SIZE:]
        other = lax.ppermute(own, "seq", [(i, i ^ 1) for i in range(count)])
        odd = place % 2 == 1
        low, high = jnp.where(odd, other, own), jnp.where(odd, own, other)
        self.weights = jnp.concatenate(
            [self.joined[:, :HEAD_SIZE], low[:, :half], high[:, :half], low[:, half:], high[:, half:]],
            axis=1,
        )
        depth = HEAD_SIZE // count
        here = QUERY_HEADS // layers
        part = w_out.reshape(here, count, depth, w_out.shape[1])
        part = lax.dynamic_index_in_dim(part, place, axis=1, keepdims=False)
        part = gather_rows(part.reshape(here * depth, -1))
        self.out_rows = swap_parts(part, 0, 0)

    def forward(self, normed, seg_whole):
        batches, length = seg_whole.shape
        (whole,) = plane_gather(normed, 0, "gather_normed")
        starts = doc_starts(seg_whole)
        places = jnp.arange(length, dtype=jnp.int32)
        low_bound = jnp.maximum(starts, places - (WIN - 1))[..., None]
        cosine, sine = angles(places - starts, HEAD_SIZE)
        rows = final_dot(whole, self.weights)
        query, key, value = (rows[..., HEAD_SIZE * i : HEAD_SIZE * (i + 1)] for i in range(3))
        query = rotate(query, cosine, sine, 1.0) * (1.0 / math.sqrt(HEAD_SIZE))
        query = query.astype(jnp.bfloat16)
        key = rotate(key, cosine, sine, 1.0).astype(jnp.bfloat16)
        value = value.astype(jnp.bfloat16)
        attended, log_total = attend(query, key, value, low_bound)
        width = normed.shape[-1]
        flops = 2 * batches * length * HEAD_SIZE * width
        mixed = plane_scatter(
            [attended], [self.out_rows], rows_compute, width, 1, "scatter_mixed", flops
        )
        return mixed, (whole, query, key, value, low_bound, log_total, cosine, sine, attended)

    def backward(self, grad_mixed_b, saved):
        whole, query, key, value, low_bound, log_total, cosine, sine, attended = saved
        batches, length = key.shape[:2]
        width = grad_mixed_b.shape[-1]
        count = lax.axis_size("seq")
        grad_whole, grad_att = plane_gather(
            grad_mixed_b,
            2,
            "gather_grad_mixed",
            weights=[self.out_rows],
            outs=[(HEAD_SIZE, jnp.bfloat16)],
            compute=head_back_compute,
            flops=2 * batches * length * HEAD_SIZE * width,
        )
        dq, low, high = attend_back(
            query, key, value, grad_att, low_bound, log_total, cosine, sine
        )
        odd = lax.axis_index("seq") % 2 == 1
        came = lax.ppermute(
            jnp.where(odd, low, high), "seq", [(i, i ^ 1) for i in range(count)]
        )
        kept = jnp.where(odd, high, low)
        dkv = (kept.astype(jnp.float32) + came.astype(jnp.float32)).astype(jnp.bfloat16)
        grads = jnp.concatenate([dq, dkv], axis=-1)
        self.record = (whole, grads, attended, grad_whole)
        flops = 4 * batches * length * HEAD_SIZE * width
        return plane_scatter(
            [grads], [self.joined], back_compute, width, 3, "scatter_grad_normed", flops
        )

    def weight_grads(self):
        half = HEAD_SIZE // 2
        whole, grads, attended, grad_whole = self.record
        out = dot_rows(attended, grad_whole).astype(jnp.bfloat16)
        out = scatter_rows(swap_parts(out, 1, 0))
        joined = scatter_rows(dot_rows(whole, grads))
        return (
            joined[:, :HEAD_SIZE],
            joined[:, HEAD_SIZE : HEAD_SIZE + half],
            joined[:, HEAD_SIZE + half :],
            out,
        )


class ByTokens:
    def __init__(self, w_query, key_weight, value_weight, w_out):
        self.weights = fetch_attention(w_query, key_weight, value_weight, w_out)
        self.records = []

    def forward(self, normed, seg_whole):
        done = [self.forward_one(*pair) for pair in zip(normed, seg_whole)]
        return jnp.stack([mixed for mixed, _ in done]), [saved for _, saved in done]

    def forward_one(self, normed, seg_whole):
        token_rows = normed.shape[0]
        halo_count = (WIN - 2 + token_rows) // token_rows
        w_query, key_weight, value_weight, w_out = self.weights
        seq_place = lax.axis_index("seq")
        seg_here = lax.dynamic_slice_in_dim(seg_whole, seq_place * token_rows, token_rows)
        position = jnp.arange(seg_whole.shape[0], dtype=jnp.int32) - doc_starts(seg_whole)
        position = lax.dynamic_slice_in_dim(position, seq_place * token_rows, token_rows)
        cosine, sine = (table[:, None] for table in angles(position, HEAD_SIZE))
        query = rotate(
            final_dot(normed, w_query).reshape(token_rows, QUERY_HEADS, HEAD_SIZE),
            cosine,
            sine,
            1.0,
        )
        query = (query * (1.0 / math.sqrt(HEAD_SIZE))).astype(jnp.bfloat16)
        key = rotate(
            final_dot(normed, key_weight).reshape(token_rows, KEY_VALUE_HEADS, HEAD_SIZE),
            cosine,
            sine,
            1.0,
        ).astype(jnp.bfloat16)
        value = final_dot(normed, value_weight).reshape(token_rows, KEY_VALUE_HEADS, HEAD_SIZE)
        pair = key_window(jnp.stack([key, value.astype(jnp.bfloat16)]), halo_count)
        allowed = window_mask(seg_here, seg_whole, seq_place, token_rows, halo_count)
        query = query.reshape(token_rows, KEY_VALUE_HEADS, -1, HEAD_SIZE)
        score = jnp.einsum("qhgd,khd->hgqk", query, pair[0], preferred_element_type=jnp.float32)
        capped = jnp.where(allowed, CAP * jnp.tanh(score / CAP), -jnp.inf)
        peak = jnp.max(capped, axis=-1, keepdims=True)
        power = jnp.exp(capped - peak)
        total = jnp.sum(power, axis=-1, keepdims=True)
        attended = jnp.einsum(
            "hgqk,khd->qhgd",
            (power / total).astype(jnp.bfloat16),
            pair[1],
            preferred_element_type=jnp.float32,
        )
        attended = attended.reshape(token_rows, QUERY_HEADS * HEAD_SIZE).astype(jnp.bfloat16)
        mixed = final_dot(attended, w_out)
        log_total = peak + jnp.log(total)
        return mixed, (normed, query, pair, allowed, log_total, cosine, sine, attended)

    def backward(self, grad_mixed_b, saved):
        return jnp.stack([self.backward_one(*pair) for pair in zip(grad_mixed_b, saved)])

    def backward_one(self, grad_mixed_b, saved):
        normed, query, pair, allowed, log_total, cosine, sine, attended = saved
        token_rows = normed.shape[0]
        halo_count = (WIN - 2 + token_rows) // token_rows
        w_query, key_weight, value_weight, w_out = self.weights
        grad_att = dot_back(grad_mixed_b, w_out).astype(jnp.bfloat16)
        grad_att = grad_att.reshape(token_rows, KEY_VALUE_HEADS, -1, HEAD_SIZE)
        score = jnp.einsum("qhgd,khd->hgqk", query, pair[0], preferred_element_type=jnp.float32)
        bent = jnp.tanh(score / CAP)
        prob = jnp.exp(jnp.where(allowed, CAP * bent, -jnp.inf) - log_total)
        grad_prob = jnp.einsum(
            "qhgd,khd->hgqk", grad_att, pair[1], preferred_element_type=jnp.float32
        )
        delta = jnp.sum(prob * grad_prob, axis=-1, keepdims=True)
        grad_score = (prob * (grad_prob - delta) * (1.0 - bent * bent)).astype(jnp.bfloat16)
        dq = jnp.einsum("hgqk,khd->qhgd", grad_score, pair[0], preferred_element_type=jnp.float32)
        dk = jnp.einsum("hgqk,qhgd->khd", grad_score, query, preferred_element_type=jnp.float32)
        dv = jnp.einsum(
            "hgqk,qhgd->khd", prob.astype(jnp.bfloat16), grad_att, preferred_element_type=jnp.float32
        )
        paired = window_grads(jnp.stack([dk, dv]), halo_count, token_rows)
        dq = rotate(
            dq.reshape(token_rows, QUERY_HEADS, HEAD_SIZE) * (1.0 / math.sqrt(HEAD_SIZE)),
            cosine,
            sine,
            -1.0,
        )
        dq = dq.reshape(token_rows, -1).astype(jnp.bfloat16)
        dk = rotate(paired[0], cosine, sine, -1.0).reshape(token_rows, -1).astype(jnp.bfloat16)
        dv = paired[1].reshape(token_rows, -1).astype(jnp.bfloat16)
        self.records.append((normed, dq, dk, dv, attended, grad_mixed_b))
        return dot_back(dq, w_query) + dot_back(dk, key_weight) + dot_back(dv, value_weight)

    def weight_grads(self):
        normed, dq, dk, dv, attended, grad_mixed_b = (
            jnp.concatenate(parts, axis=0) for parts in zip(*self.records)
        )
        normed = lax.all_gather(normed, "seq", axis=0, tiled=True)
        attended = lax.all_gather(attended, "seq", axis=0, tiled=True)
        sums = []
        for rows, grads in ((normed, dq), (normed, dk), (normed, dv), (attended, grad_mixed_b)):
            column_sum = dot_rows(rows, swap_parts(grads, 1, 0)).astype(jnp.bfloat16)
            owned = lax.psum_scatter(column_sum, "fsdp", scatter_dimension=0, tiled=True)
            sums.append(owned.astype(jnp.float32))
        return tuple(sums)


class FeedForward:
    def __init__(self, w_gate, w_up, w_down, by_kernel):
        place = lax.axis_index("seq")
        count = lax.axis_size("seq")
        self.by_kernel = by_kernel
        self.run = w_gate.shape[1] // (count * count)

        def columns(weight):
            parts = [
                lax.dynamic_slice_in_dim(
                    weight, (t * count + place) * self.run, self.run, axis=1
                )
                for t in range(count)
            ]
            return jnp.concatenate(parts, axis=1)

        here = w_down.shape[0] // (count * self.run)
        part = w_down.reshape(here, count, self.run, w_down.shape[1])
        part = lax.dynamic_index_in_dim(part, place, axis=1, keepdims=False)
        self.gate = gather_rows(columns(w_gate))
        self.up = gather_rows(columns(w_up))
        self.down = gather_rows(part.reshape(here * self.run, -1))

    def forward(self, ffn_in):
        hidden_width, width = self.down.shape
        if self.by_kernel:
            rows = ffn_in.shape[0] * ffn_in.shape[1] * lax.axis_size("seq")
            whole, gate_proj, up_proj, hidden = plane_gather(
                ffn_in,
                4,
                "gather_ffn_in",
                weights=[self.gate, self.up],
                outs=[(hidden_width, jnp.bfloat16)] * 3,
                compute=hidden_compute,
                flops=4 * rows * width * hidden_width,
            )
            flops = 2 * rows * width * hidden_width
            down_proj = plane_scatter(
                [hidden], [self.down], rows_compute, width, 5, "scatter_down", flops
            )
        else:
            whole = lax.all_gather(ffn_in, "seq", axis=1, tiled=True)
            gate_proj = final_dot(whole, self.gate)
            up_proj = final_dot(whole, self.up)
            hidden = geglu(gate_proj, up_proj).astype(jnp.bfloat16)
            down_proj = lax.psum_scatter(
                final_dot(hidden, self.down).astype(jnp.bfloat16),
                "seq",
                scatter_dimension=1,
                tiled=True,
            ).astype(jnp.float32)
        return down_proj, (whole, gate_proj, up_proj, hidden)

    def backward(self, grad_down_b, saved):
        whole, gate_proj, up_proj, hidden = saved
        hidden_width, width = self.down.shape
        if self.by_kernel:
            rows = whole.shape[0] * whole.shape[1]
            grad_whole, grad_gate, grad_up = plane_gather(
                grad_down_b,
                6,
                "gather_grad_down",
                weights=[self.down],
                extras=[gate_proj, up_proj],
                outs=[(hidden_width, jnp.bfloat16)] * 2,
                compute=hidden_back_compute,
                flops=2 * rows * width * hidden_width,
            )
            grad_ffn_in = plane_scatter(
                [grad_gate, grad_up],
                [self.gate, self.up],
                back_compute,
                width,
                7,
                "scatter_grad_ffn_in",
                4 * rows * width * hidden_width,
            )
        else:
            grad_whole = lax.all_gather(grad_down_b, "seq", axis=1, tiled=True)
            grad_hidden = dot_back(grad_whole, self.down)
            _, pullback = jax.vjp(geglu, gate_proj, up_proj)
            grad_gate, grad_up = (g.astype(jnp.bfloat16) for g in pullback(grad_hidden))
            partial = dot_back(grad_gate, self.gate) + dot_back(grad_up, self.up)
            grad_ffn_in = lax.psum_scatter(
                partial.astype(jnp.bfloat16), "seq", scatter_dimension=1, tiled=True
            ).astype(jnp.float32)
        self.record = (whole, hidden, grad_whole, grad_gate, grad_up)
        return grad_ffn_in

    def weight_grads(self):
        whole, hidden, grad_whole, grad_gate, grad_up = self.record
        count = lax.axis_size("seq")

        down = scatter_rows(dot_rows(hidden, grad_whole)).astype(jnp.bfloat16)
        here = down.shape[0] // self.run
        down = swap_parts(down.reshape(1, here, self.run, -1), 3, 0)
        down = down.transpose(1, 0, 2, 3).reshape(here * count * self.run, -1)

        def columns(grads):
            summed = scatter_rows(dot_rows(whole, grads)).astype(jnp.bfloat16)
            return swap_parts(summed, 1, 1).astype(jnp.float32)

        return columns(grad_gate), columns(grad_up), down.astype(jnp.float32)


def on_device(
    tokens,
    segments,
    w_query,
    key_weight,
    value_weight,
    w_out,
    w_gate,
    w_up,
    w_down,
    gain_attn_in,
    gain_attn_out,
    gain_ffn_in,
    gain_ffn_out,
    cotangent,
):
    seg_whole = lax.all_gather(segments, "seq", axis=2, tiled=True)[:, 0]
    by_kernel = (
        lax.axis_size("seq") == QUERY_HEADS
        and tokens.shape[0] == 2
        and QUERY_HEADS % lax.axis_size("fsdp") == 0
    )
    attention = (ByHeads if by_kernel else ByTokens)(w_query, key_weight, value_weight, w_out)
    ffn = FeedForward(w_gate, w_up, w_down, by_kernel)

    stream = tokens[:, 0].astype(jnp.float32)
    normed = rms_gain(stream, gain_attn_in).astype(jnp.bfloat16)
    mixed, attention_saved = attention.forward(normed, seg_whole)
    middle = stream + rms_gain(mixed, gain_attn_out)
    ffn_in = rms_gain(middle, gain_ffn_in).astype(jnp.bfloat16)
    down_proj, ffn_saved = ffn.forward(ffn_in)
    result = middle + rms_gain(down_proj, gain_ffn_out)

    grad_result = cotangent[:, 0].astype(jnp.float32)
    _, pullback = jax.vjp(rms_gain, down_proj, gain_ffn_out)
    grad_down, grad_gain_four = pullback(grad_result)
    grad_ffn_in = ffn.backward(grad_down.astype(jnp.bfloat16), ffn_saved)
    _, pullback = jax.vjp(rms_gain, middle, gain_ffn_in)
    grad_middle, grad_gain_three = pullback(grad_ffn_in)
    grad_middle = grad_result + grad_middle
    _, pullback = jax.vjp(rms_gain, mixed, gain_attn_out)
    grad_mixed, grad_gain_two = pullback(grad_middle)
    grad_normed = attention.backward(grad_mixed.astype(jnp.bfloat16), attention_saved)
    _, pullback = jax.vjp(rms_gain, stream, gain_attn_in)
    grad_stream, grad_gain_one = pullback(grad_normed)
    grad_stream = grad_middle + grad_stream

    w_gate_grad, w_up_grad, w_down_grad = ffn.weight_grads()
    query_grad, key_grad, value_grad, out_grad = attention.weight_grads()
    gain_early = jnp.stack([grad_gain_two, grad_gain_three, grad_gain_four])
    gain_early = lax.psum(gain_early, ("seq", "fsdp"))
    gain_late = lax.psum(grad_gain_one, ("seq", "fsdp"))
    return (
        result.astype(jnp.bfloat16)[:, None],
        grad_stream[:, None],
        query_grad,
        key_grad,
        value_grad,
        out_grad,
        w_gate_grad,
        w_up_grad,
        w_down_grad,
        gain_late,
        gain_early[0],
        gain_early[1],
        gain_early[2],
    )


def solution(mesh):
    in_specs = (
        P(None, "fsdp", "seq", None),
        P(None, "fsdp", "seq"),
        P("fsdp", None),
        P("fsdp", None),
        P("fsdp", None),
        P("fsdp", None),
        P("fsdp", None),
        P("fsdp", None),
        P("fsdp", None),
        P(),
        P(),
        P(),
        P(),
        P(None, "fsdp", "seq", None),
    )
    out_specs = (
        P(None, "fsdp", "seq", None),
        P(None, "fsdp", "seq", None),
        P("fsdp", "seq"),
        P("fsdp", "seq"),
        P("fsdp", "seq"),
        P("fsdp", "seq"),
        P("fsdp", "seq"),
        P("fsdp", "seq"),
        P("fsdp", "seq"),
        P(),
        P(),
        P(),
        P(),
    )
    return jax.shard_map(
        on_device, mesh=mesh, in_specs=in_specs, out_specs=out_specs, check_vma=False
    )
```

```python
import functools
import math

import jax
import jax.numpy as jnp
from jax import lax
from jax.experimental import pallas as pl
from jax.experimental.pallas import tpu as pltpu
from jax.sharding import PartitionSpec as P

QUERY_HEADS = 8
KEY_VALUE_HEADS = 4
HEAD_SIZE = 256
CAP = 50
WIN = 1024
DOCUMENTS = 4
VMEM_LIMIT = 60 * 2**20
SPAN_BYTES = 270_000_000


epsilon = 1e-06


def shifted(value, axis, steps):
    count = lax.axis_size(axis)
    initial, last = (max(0, -steps), min(count, count - steps))
    return lax.ppermute(value, axis, [(source, source + steps) for source in range(initial, last)])


def rms_gain(stream, gain):
    return stream * lax.rsqrt(jnp.mean(stream * stream, axis=-1, keepdims=True) + epsilon) * gain


def geglu(gate_proj, up_proj):
    return jax.nn.gelu(gate_proj, approximate=True) * up_proj


def angles(position, size):
    frequency = 10000.0 ** (-jnp.arange(size // 2, dtype=jnp.float32) * 2.0 / size)
    phase_angle = position.astype(jnp.float32)[..., None] * frequency
    return (jnp.cos(phase_angle), jnp.sin(phase_angle))


def rotate(value_rows, cosine_table, sine_table, direction):
    half_size = value_rows.shape[-1] // 2
    first_half = value_rows[..., :half_size]
    second = value_rows[..., half_size:]
    return jnp.concatenate(
        [
            first_half * cosine_table - direction * second * sine_table,
            second * cosine_table + direction * first_half * sine_table,
        ],
        axis=-1,
    )


def doc_starts(segment):
    starts = jnp.zeros_like(segment)
    for number in range(1, DOCUMENTS):
        count = jnp.sum((segment < number).astype(jnp.int32), axis=-1, keepdims=True)
        starts = jnp.where(segment >= number, count, starts)
    return starts


def final_dot(left_side, right_side):
    return jnp.dot(left_side, right_side, preferred_element_type=jnp.float32)


def dot_back(left_side, right_side):
    contract = (((left_side.ndim - 1,), (1,)), ((), ()))
    return lax.dot_general(left_side, right_side, contract, preferred_element_type=jnp.float32)


def dot_rows(left_side, right_side):
    left_side = left_side.reshape(-1, left_side.shape[-1])
    right_side = right_side.reshape(-1, right_side.shape[-1])
    return lax.dot_general(
        left_side, right_side, (((0,), (0,)), ((), ())), preferred_element_type=jnp.float32
    )


def fetch_attention(w_query, key_weight, value_weight, w_out):
    return (
        lax.all_gather(w_query, "fsdp", axis=0, tiled=True),
        lax.all_gather(key_weight, "fsdp", axis=0, tiled=True),
        lax.all_gather(value_weight, "fsdp", axis=0, tiled=True),
        lax.all_gather(w_out, "fsdp", axis=0, tiled=True),
    )


def key_window(kv_pair, halo_count):
    arrived = [shifted(kv_pair, "seq", offset) for offset in range(halo_count, 0, -1)]
    return jnp.concatenate(arrived + [kv_pair], axis=1)


def window_grads(paired_gradient, halo_count, token_rows):
    summed = paired_gradient[:, halo_count * token_rows :]
    for offset in range(1, halo_count + 1):
        begin = (halo_count - offset) * token_rows
        summed = summed + shifted(
            paired_gradient[:, begin : begin + token_rows].astype(jnp.bfloat16), "seq", -offset
        ).astype(jnp.float32)
    return summed


def window_mask(seg_here, seg_whole, seq_place, token_rows, halo_count):
    padded = jnp.concatenate([jnp.full((halo_count * token_rows,), -1, jnp.int32), seg_whole])
    key_seg = lax.dynamic_slice_in_dim(
        padded, seq_place * token_rows, (halo_count + 1) * token_rows
    )
    query_pos = seq_place * token_rows + jnp.arange(token_rows, dtype=jnp.int32)
    key_pos = (
        seq_place * token_rows
        - halo_count * token_rows
        + jnp.arange((halo_count + 1) * token_rows, dtype=jnp.int32)
    )
    distance = query_pos[:, None] - key_pos[None, :]
    return (seg_here[:, None] == key_seg[None, :]) & (distance >= 0) & (distance < WIN)


def gather_rows(rows):
    return lax.all_gather(rows, "fsdp", axis=0, tiled=True)


def scatter_rows(partial):
    return lax.psum_scatter(
        partial.astype(jnp.bfloat16), "fsdp", scatter_dimension=0, tiled=True
    )


def swap_parts(value, split_axis, concat_axis):
    return lax.all_to_all(
        value, "seq", split_axis=split_axis, concat_axis=concat_axis, tiled=True
    )


MESH = pl.DeviceIdType.MESH


def plane_places():
    me = lax.axis_index("seq")
    other_core = me + 1 - 2 * (me % 2)
    along_x = me + 2 - 4 * ((me // 2) % 2)
    along_y = me + 4 - 8 * (me // 4)
    return me, other_core, along_x, along_y


def greet(neighbours):
    barrier = pltpu.get_barrier_semaphore()
    for neighbour in neighbours:
        pl.semaphore_signal(barrier, inc=1, device_id={"seq": neighbour}, device_id_type=MESH)
    pl.semaphore_wait(barrier, len(neighbours))


BRAID = 384


def braid_width(arrays):
    return sum(array.shape[-1] for array in arrays)


def copies_into(sources, target, sem):
    if len(sources) == 1:
        return [pltpu.make_async_copy(sources[0], target, sem.at[0])]
    groups = sources[0].shape[-1] // BRAID
    copies = []
    for group in range(groups):
        for part, source in enumerate(sources):
            at = group * len(sources) + part
            copies.append(
                pltpu.make_async_copy(
                    source.at[:, pl.ds(group * BRAID, BRAID)],
                    target.at[:, pl.ds(at * BRAID, BRAID)],
                    sem.at[at],
                )
            )
    return copies


def copy_count(arrays):
    return 1 if len(arrays) == 1 else braid_width(arrays) // BRAID


def unit_rows(place, rows):
    return pl.ds(pl.multiple_of((place // 2) * (2 * rows), 16), 2 * rows)


class Job:
    def __init__(
        self, compute, weights=(), extras=(), outs=(), sums=(), side=(), tables=(), spare=None, flops=0
    ):
        self.compute, self.flops, self.spare = compute, flops, spare
        self.tables = list(tables)
        self.weights, self.extras, self.outs = list(weights), list(extras), list(outs)
        self.sums, self.side = list(sums), list(side)


def gather_kernel(job, rows, *refs):
    refs = list(refs)
    take = lambda n: [refs.pop(0) for _ in range(n)]
    (local_ref,) = take(1)
    weight_refs, extra_refs, side_refs = (
        take(len(job.weights)),
        take(len(job.extras)),
        take(len(job.side)),
    )
    table_refs = take(len(job.tables))
    (whole_ref,), out_refs, final_refs = take(1), take(len(job.outs)), take(len(job.sums))
    made_refs = take(len(job.spare[1]) if job.spare else 0)
    send_sem, recv_sem, own_sem, x_buf = take(4)
    weight_bufs = take(1 if job.weights else 0)
    extra_bufs, side_bufs, out_bufs = (
        take(len(job.extras)),
        take(len(job.side)),
        take(len(job.outs)),
    )
    sum_bufs, final_bufs = take(len(job.sums)), take(len(job.sums))
    weight_sem, load_sem, side_sem, store_sem, final_sem = take(5)

    me, other_core, along_x, along_y = plane_places()
    across = along_x + along_y - me
    core = me % 2

    def piece(batch, place):
        return whole_ref.at[batch, pl.ds(pl.multiple_of(place * rows, 16), rows)]

    def transfer(slot, source, batch, place, target):
        return pltpu.make_async_remote_copy(
            src_ref=source,
            dst_ref=piece(batch, place),
            send_sem=send_sem.at[slot],
            recv_sem=recv_sem.at[slot],
            device_id={"seq": target},
            device_id_type=MESH,
        )

    def forward(slot, batch, place, target):
        return transfer(slot, piece(batch, place), batch, place, target)

    moves = [
        transfer(0, local_ref.at[0], 0, me, along_x),
        transfer(1, local_ref.at[1], 1, me, along_x),
        transfer(2, local_ref.at[1], 1, me, along_y),
        transfer(3, local_ref.at[0], 0, me, along_y),
        forward(4, 0, along_x, along_y),
        forward(5, 1, along_y, along_x),
        transfer(6, local_ref.at[0], 0, me, other_core),
        transfer(7, local_ref.at[1], 1, me, other_core),
        forward(8, 0, along_x, other_core),
        forward(9, 1, along_x, other_core),
        forward(10, 1, along_y, other_core),
        forward(11, 0, along_y, other_core),
        forward(12, 0, across, other_core),
        forward(13, 1, across, other_core),
    ]
    greet((other_core, along_x, along_y))
    for slot in (0, 2, 1, 3, 6, 7):
        moves[slot].start()
    owns = [
        pltpu.make_async_copy(local_ref.at[batch], piece(batch, me), own_sem.at[batch])
        for batch in range(2)
    ]
    for own in owns:
        own.start()
    fetches = copies_into(weight_refs, weight_bufs[0], weight_sem) if job.weights else []
    for fetch in fetches:
        fetch.start()
    if job.spare:
        job.spare[0](table_refs, made_refs)
    stores = []
    done = {"side": 0}

    def own_half(which):
        return x_buf.at[pl.ds(pl.multiple_of(which * rows, 16), rows)]

    def unit(place, batch, own=False):
        if job.compute is None:
            return
        span = unit_rows(place, rows)
        if own:
            loads = [
                pltpu.make_async_copy(local_ref.at[batch], own_half(core), load_sem.at[0]),
                pltpu.make_async_copy(
                    piece(batch, other_core), own_half(1 - core), load_sem.at[1]
                ),
            ]
        else:
            loads = [pltpu.make_async_copy(whole_ref.at[batch, span], x_buf, load_sem.at[0])]
        loads += [
            pltpu.make_async_copy(ref.at[batch, span], buf, load_sem.at[2 + i])
            for i, (ref, buf) in enumerate(zip(extra_refs, extra_bufs))
        ]
        for load in loads:
            load.start()
        step = len(stores)
        if step == 0:
            for fetch in fetches:
                fetch.wait()
        if step >= 2:
            for store in stores[step - 2]:
                store.wait()
        for load in loads:
            load.wait()
        slot = step % 2
        job.compute(
            x_buf, weight_bufs, extra_bufs, [buf.at[slot] for buf in out_bufs], sum_bufs, step == 0
        )
        stores.append(
            [
                pltpu.make_async_copy(buf.at[slot], ref.at[batch, span], store_sem.at[slot, i])
                for i, (ref, buf) in enumerate(zip(out_refs, out_bufs))
            ]
        )
        for store in stores[-1]:
            store.start()

    def side(count):
        if not job.side:
            return
        for _ in range(count):
            chunk = done["side"]
            done["side"] += 1
            run_side(chunk, rows, side_refs, side_bufs, sum_bufs[0], side_sem)

    for batch in range(2):
        moves[6 + batch].wait_recv()
        unit(me, batch, own=True)
        side(1)
    moves[0].wait_recv()
    moves[4].start()
    moves[8].start()
    moves[2].wait_recv()
    moves[5].start()
    moves[10].start()
    side(2)
    moves[8].wait_recv()
    unit(along_x, 0)
    moves[10].wait_recv()
    unit(along_y, 1)
    side(1)
    moves[1].wait_recv()
    moves[9].start()
    moves[3].wait_recv()
    moves[11].start()
    side(3)
    moves[9].wait_recv()
    unit(along_x, 1)
    moves[11].wait_recv()
    unit(along_y, 0)
    if job.side:
        finish_sums(sum_bufs, final_bufs, final_refs, final_sem)
    moves[4].wait_recv()
    moves[12].start()
    moves[5].wait_recv()
    moves[13].start()
    moves[12].wait_recv()
    unit(across, 0)
    moves[13].wait_recv()
    unit(across, 1)
    if not job.side:
        finish_sums(sum_bufs, final_bufs, final_refs, final_sem)
    for move in moves:
        move.wait_send()
    for own in owns:
        own.wait()
    for group in stores[-2:]:
        for store in group:
            store.wait()


def run_side(chunk, rows, refs, bufs, total, sem):
    span = pl.ds((chunk % 4) * 2 * rows, 2 * rows)
    loads = [
        pltpu.make_async_copy(ref.at[chunk // 4, span], buf, sem.at[i])
        for i, (ref, buf) in enumerate(zip(refs, bufs))
    ]
    for load in loads:
        load.start()
    for load in loads:
        load.wait()
    add_outer(bufs[0], bufs[1], total, chunk == 0)


def finish_sums(sum_bufs, final_bufs, final_refs, sem):
    for i, (total, buf, ref) in enumerate(zip(sum_bufs, final_bufs, final_refs)):
        copies = []
        for block in range(total.shape[0] // BRAID):
            slot = block % 2
            span = pl.ds(block * BRAID, BRAID)
            if block >= 2:
                copies[block - 2].wait()
            buf[slot] = total[span, :].astype(buf.dtype)
            copies.append(pltpu.make_async_copy(buf.at[slot], ref.at[span], sem.at[i, slot]))
            copies[-1].start()
        for copy in copies[-2:]:
            copy.wait()


def plane_gather(local, ident, name, job=None):
    job = job or Job(None)
    batches, rows, width = local.shape
    length = rows * lax.axis_size("seq")
    semaphores = pltpu.SemaphoreType.DMA
    scratch = [semaphores((14,)), semaphores((14,)), semaphores((2,))]
    scratch += [pltpu.VMEM((2 * rows if job.compute else 8, width), local.dtype)]
    if job.weights:
        depth = job.weights[0].shape[0]
        scratch += [pltpu.VMEM((depth, braid_width(job.weights)), job.weights[0].dtype)]
    for arrays in (job.extras, job.side):
        scratch += [pltpu.VMEM((2 * rows, array.shape[2]), array.dtype) for array in arrays]
    scratch += [pltpu.VMEM((2, 2 * rows, wide), kind) for wide, kind in job.outs]
    scratch += [pltpu.VMEM(shape, jnp.float32) for shape in job.sums]
    scratch += [pltpu.VMEM((2, BRAID, shape[1]), jnp.bfloat16) for shape in job.sums]
    scratch += [
        semaphores((copy_count(job.weights) if job.weights else 1,)),
        semaphores((2 + len(job.extras),)),
        semaphores((max(1, len(job.side)),)),
        semaphores((2, max(1, len(job.outs)))),
        semaphores((max(1, len(job.sums)), 2)),
    ]
    any_space = pl.BlockSpec(memory_space=pl.ANY)
    out_shape = [jax.ShapeDtypeStruct((batches, length, width), local.dtype)]
    out_shape += [jax.ShapeDtypeStruct((batches, length, wide), kind) for wide, kind in job.outs]
    out_shape += [jax.ShapeDtypeStruct(shape, jnp.bfloat16) for shape in job.sums]
    inputs = [local, *job.weights, *job.extras, *job.side]
    in_specs = [any_space] * len(inputs)
    in_specs += [pl.BlockSpec(memory_space=pltpu.VMEM)] * len(job.tables)
    out_specs = [any_space] * len(out_shape)
    if job.spare:
        out_shape += job.spare[1]
        out_specs += [pl.BlockSpec(memory_space=pltpu.VMEM)] * len(job.spare[1])
    return pl.pallas_call(
        functools.partial(gather_kernel, job, rows),
        in_specs=in_specs,
        out_specs=out_specs,
        out_shape=out_shape,
        scratch_shapes=scratch,
        compiler_params=pltpu.CompilerParams(
            collective_id=ident, has_side_effects=True, vmem_limit_bytes=VMEM_LIMIT
        ),
        cost_estimate=pl.CostEstimate(
            flops=job.flops, bytes_accessed=SPAN_BYTES, transcendentals=0
        ),
        name=name,
    )(*inputs, *job.tables)


def scatter_kernel(job, rows, *refs):
    refs = list(refs)
    take = lambda n: [refs.pop(0) for _ in range(n)]
    part_refs, weight_refs, side_refs = (
        take(len(job.extras)),
        take(len(job.weights)),
        take(len(job.side)),
    )
    (out_ref,), final_refs = take(1), take(len(job.sums))
    part_buf, weight_buf, sums, held, from_core, from_link, out_buf = take(7)
    side_bufs, sum_bufs, final_bufs = take(len(job.side)), take(len(job.sums)), take(len(job.sums))
    weight_sem, load_sem, side_sem, final_sem, out_sem = take(5)
    core_send, core_recv, link_send, link_recv, credit = take(5)

    me, other_core, along_x, along_y = plane_places()
    across = along_x + along_y - me
    core = me % 2
    kept = pl.ds(pl.multiple_of(core * rows, 16), rows)
    given = pl.ds(pl.multiple_of((1 - core) * rows, 16), rows)
    units = [
        (across, 0),
        (across, 1),
        (along_x, 0),
        (along_y, 1),
        (along_x, 1),
        (along_y, 0),
        (me, 0),
        (me, 1),
    ]
    targets = [along_x, along_y, along_x, along_y, along_x, along_y]
    added = {4: (1,), 5: (0,), 6: (2, 5), 7: (3, 4)}

    def load(step):
        place, batch = units[step]
        span = unit_rows(place, rows)
        sources = [ref.at[batch, span] for ref in part_refs]
        return copies_into(sources, part_buf.at[step % 2], load_sem.at[step % 2])

    loads = [load(step) for step in range(8)]
    fetches = copies_into(weight_refs, weight_buf, weight_sem)
    for copy in loads[0] + fetches:
        copy.start()
    gives = [
        pltpu.make_async_remote_copy(
            src_ref=sums.at[step % 2, given],
            dst_ref=from_core.at[step % 4],
            send_sem=core_send.at[step],
            recv_sem=core_recv.at[step],
            device_id={"seq": other_core},
            device_id_type=MESH,
        )
        for step in range(8)
    ]
    sends = [
        pltpu.make_async_remote_copy(
            src_ref=held.at[step],
            dst_ref=from_link.at[step],
            send_sem=link_send.at[step],
            recv_sem=link_recv.at[step],
            device_id={"seq": targets[step]},
            device_id_type=MESH,
        )
        for step in range(6)
    ]
    greet((other_core, along_x, along_y))

    def finish(step):
        gives[step].wait_recv()
        total = sums[step % 2, kept].astype(jnp.float32)
        total = total + from_core[step % 4].astype(jnp.float32)
        if step < 4:
            pl.semaphore_signal(credit, inc=1, device_id={"seq": other_core}, device_id_type=MESH)
        for arrived in added.get(step, ()):
            sends[arrived].wait_recv()
            total = total + from_link[arrived].astype(jnp.float32)
        if step < 6:
            held[step] = total.astype(jnp.bfloat16)
            sends[step].start()
        else:
            out = pltpu.make_async_copy(out_buf, out_ref.at[step - 6], out_sem.at[step - 6])
            out_buf[...] = total
            out.start()
            out.wait()

    done = {"side": 0}

    def side(count):
        if not job.side:
            return
        for _ in range(count):
            chunk = done["side"]
            done["side"] += 1
            run_side(chunk, rows, side_refs, side_bufs, sum_bufs[0], side_sem)

    for step in range(8):
        for copy in loads[step]:
            copy.wait()
        if step == 0:
            for fetch in fetches:
                fetch.wait()
        if step < 7:
            for copy in loads[step + 1]:
                copy.start()
        if step >= 2:
            gives[step - 2].wait_send()
        job.compute(part_buf.at[step % 2], weight_buf, sums.at[step % 2])
        if step >= 4:
            pl.semaphore_wait(credit, 1)
        gives[step].start()
        if step >= 1:
            finish(step - 1)
        side((0, 0, 1, 1, 1, 1, 2, 2)[step])
    if job.side:
        finish_sums(sum_bufs, final_bufs, final_refs, final_sem)
    finish(7)
    for move in gives[6:] + sends:
        move.wait_send()


def plane_scatter(parts, width, ident, name, job):
    job.extras = list(parts)
    batches, length = parts[0].shape[:2]
    rows = length // lax.axis_size("seq")
    any_space = pl.BlockSpec(memory_space=pl.ANY)
    semaphores = pltpu.SemaphoreType.DMA
    weights = job.weights
    scratch = [
        pltpu.VMEM((2, 2 * rows, braid_width(parts)), parts[0].dtype),
        pltpu.VMEM((weights[0].shape[0], braid_width(weights)), weights[0].dtype),
        pltpu.VMEM((2, 2 * rows, width), jnp.bfloat16),
        pltpu.VMEM((6, rows, width), jnp.bfloat16),
        pltpu.VMEM((4, rows, width), jnp.bfloat16),
        pltpu.VMEM((6, rows, width), jnp.bfloat16),
        pltpu.VMEM((rows, width), jnp.float32),
    ]
    scratch += [pltpu.VMEM((2 * rows, array.shape[2]), array.dtype) for array in job.side]
    scratch += [pltpu.VMEM(shape, jnp.float32) for shape in job.sums]
    scratch += [pltpu.VMEM((2, BRAID, shape[1]), jnp.bfloat16) for shape in job.sums]
    scratch += [
        semaphores((copy_count(weights),)),
        semaphores((2, copy_count(parts))),
        semaphores((max(1, len(job.side)),)),
        semaphores((max(1, len(job.sums)), 2)),
        semaphores((2,)),
        semaphores((8,)),
        semaphores((8,)),
        semaphores((6,)),
        semaphores((6,)),
        pltpu.SemaphoreType.REGULAR,
    ]
    out_shape = [jax.ShapeDtypeStruct((batches, rows, width), jnp.float32)]
    out_shape += [jax.ShapeDtypeStruct(shape, jnp.bfloat16) for shape in job.sums]
    inputs = [*parts, *weights, *job.side]
    return pl.pallas_call(
        functools.partial(scatter_kernel, job, rows),
        in_specs=[any_space] * len(inputs),
        out_specs=[any_space] * len(out_shape),
        out_shape=out_shape,
        scratch_shapes=scratch,
        compiler_params=pltpu.CompilerParams(
            collective_id=ident, has_side_effects=True, vmem_limit_bytes=VMEM_LIMIT
        ),
        cost_estimate=pl.CostEstimate(
            flops=job.flops, bytes_accessed=SPAN_BYTES, transcendentals=0
        ),
        name=name,
    )(*inputs)


def small_sum_kernel(over_layers, value_ref, out_ref, plane_buf, layer_buf, *sems):
    plane_send, plane_recv, layer_send, layer_recv = sems
    neighbours = plane_places()[1:]
    layer, layers = lax.axis_index("fsdp"), lax.axis_size("fsdp")
    others = [lax.rem(layer + hop, layers) for hop in range(1, layers)] if over_layers else []
    barrier = pltpu.get_barrier_semaphore()
    for neighbour in neighbours:
        pl.semaphore_signal(barrier, inc=1, device_id={"seq": neighbour}, device_id_type=MESH)
    for other in others:
        pl.semaphore_signal(barrier, inc=1, device_id={"fsdp": other}, device_id_type=MESH)
    pl.semaphore_wait(barrier, len(neighbours) + len(others))
    out_ref[...] = value_ref[...]
    copies = []
    for turn, neighbour in enumerate(neighbours):
        plane_buf[turn, 0] = out_ref[...]
        copies.append(
            pltpu.make_async_remote_copy(
                src_ref=plane_buf.at[turn, 0],
                dst_ref=plane_buf.at[turn, 1],
                send_sem=plane_send.at[turn],
                recv_sem=plane_recv.at[turn],
                device_id={"seq": neighbour},
                device_id_type=MESH,
            )
        )
        copies[-1].start()
        copies[-1].wait_recv()
        out_ref[...] = plane_buf[turn, 0] + plane_buf[turn, 1]
    if over_layers:
        layer_buf[layer] = out_ref[...]
        layer_copies = [
            pltpu.make_async_remote_copy(
                src_ref=layer_buf.at[layer],
                dst_ref=layer_buf.at[layer],
                send_sem=layer_send.at[hop],
                recv_sem=layer_recv.at[hop],
                device_id={"fsdp": other},
                device_id_type=MESH,
            )
            for hop, other in enumerate(others)
        ]
        for copy in layer_copies:
            copy.start()
        for copy in layer_copies:
            copy.wait_recv()
        total = layer_buf[0]
        for index in range(1, layers):
            total = total + layer_buf[index]
        out_ref[...] = total
        copies += layer_copies
    for copy in copies:
        copy.wait_send()


def small_sum(value, over_layers, ident, name):
    layers = lax.axis_size("fsdp")
    semaphores = pltpu.SemaphoreType.DMA
    return pl.pallas_call(
        functools.partial(small_sum_kernel, over_layers),
        in_specs=[pl.BlockSpec(memory_space=pltpu.VMEM)],
        out_specs=pl.BlockSpec(memory_space=pltpu.VMEM),
        out_shape=jax.ShapeDtypeStruct(value.shape, jnp.float32),
        scratch_shapes=[
            pltpu.VMEM((3, 2) + value.shape, jnp.float32),
            pltpu.VMEM((layers,) + value.shape, jnp.float32),
            semaphores((3,)),
            semaphores((3,)),
            semaphores((layers,)),
            semaphores((layers,)),
        ],
        compiler_params=pltpu.CompilerParams(collective_id=ident, has_side_effects=True),
        name=name,
    )(value)


def tiles(width, tile, body):
    def step(index, carry):
        body(pl.ds(pl.multiple_of(index * tile, 128), tile))
        return carry

    lax.fori_loop(0, width // tile, step, 0)


GELU_SCALE = 0.7978845608
GELU_CUBE = 0.044715


def gelu_parts(gate):
    square = gate * gate
    bent = jnp.tanh(GELU_SCALE * gate * (1.0 + GELU_CUBE * square))
    half = 0.5 * (1.0 + bent)
    slope = half + 0.5 * gate * (1.0 - bent * bent) * GELU_SCALE * (1.0 + 3.0 * GELU_CUBE * square)
    return gate * half, slope


def add_outer(left, right, total, first):
    def body(span):
        outer = lax.dot_general(
            left[:, span], right[...], (((0,), (0,)), ((), ())), preferred_element_type=jnp.float32
        )
        total[span, :] = outer if first else total[span, :] + outer

    tiles(left.shape[1], BRAID, body)


def hidden_compute(x_buf, weights, extras, outs, sums, first):
    gate_out, up_out, hidden_out = outs
    (weight,) = weights

    def step(index, carry):
        both = pl.ds(pl.multiple_of(index * 2 * BRAID, 128), 2 * BRAID)
        span = pl.ds(pl.multiple_of(index * BRAID, 128), BRAID)
        product = final_dot(x_buf[...], weight[:, both])
        gate, up = product[:, :BRAID], product[:, BRAID:]
        gate_out[:, span] = gate.astype(gate_out.dtype)
        up_out[:, span] = up.astype(up_out.dtype)
        hidden_out[:, span] = (gelu_parts(gate)[0] * up).astype(hidden_out.dtype)
        return carry

    lax.fori_loop(0, weight.shape[1] // (2 * BRAID), step, 0)


def hidden_back_compute(x_buf, weights, extras, outs, sums, first):
    (down_w,) = weights
    gate_in, up_in, hidden_in = extras
    gate_out, up_out = outs
    product = dot_back(x_buf[...], down_w[...])
    for start in range(0, product.shape[1], BRAID):
        span = slice(start, start + BRAID)
        grad = product[:, span]
        value, slope = gelu_parts(gate_in[:, span].astype(jnp.float32))
        gate_out[:, span] = (grad * up_in[:, span].astype(jnp.float32) * slope).astype(
            gate_out.dtype
        )
        up_out[:, span] = (grad * value).astype(up_out.dtype)
    add_outer(hidden_in, x_buf, sums[0], first)


def head_back_compute(x_buf, weights, extras, outs, sums, first):
    outs[0][...] = dot_back(x_buf[...], weights[0][...]).astype(outs[0].dtype)


def rows_compute(part, weight, out):
    def body(span):
        out[:, span] = final_dot(part[...], weight[:, span]).astype(out.dtype)

    tiles(weight.shape[1], 2 * BRAID, body)


def back_compute(part, weight, out):
    def body(span):
        out[:, span] = dot_back(part[...], weight[span, :]).astype(out.dtype)

    tiles(weight.shape[0], 2 * BRAID, body)


def score_parts(query, key, low_bound, row_start, col_start):
    raw = lax.dot_general(
        query, key, (((1,), (1,)), ((), ())), preferred_element_type=jnp.float32
    )
    bent = jnp.tanh(raw * (1.0 / CAP))
    shape = raw.shape
    row = row_start + lax.broadcasted_iota(jnp.int32, shape, 0)
    col = col_start + lax.broadcasted_iota(jnp.int32, shape, 1)
    allowed = (col <= row) & (col >= low_bound)
    return bent, jnp.where(allowed, CAP * bent, -1e30)


def attend_kernel(block, reach, q_ref, k_ref, v_ref, low_ref, out_ref, log_ref):
    index = pl.program_id(1)

    def run(blocks):
        first = (index - (blocks - 1)) * block
        span = pl.ds(pl.multiple_of(first, block), blocks * block)
        _, capped = score_parts(
            q_ref[...], k_ref[span, :], low_ref[...], index * block, first
        )
        peak = jnp.max(capped, axis=-1, keepdims=True)
        power = jnp.exp(capped - peak)
        total = jnp.sum(power, axis=-1, keepdims=True)
        prob = (power * (1.0 / total)).astype(jnp.bfloat16)
        out = jnp.dot(prob, v_ref[span, :], preferred_element_type=jnp.float32)
        out_ref[...] = out.astype(jnp.bfloat16)
        log_ref[...] = peak + jnp.log(total)

    for blocks in range(1, reach + 1):
        if blocks < reach:
            pl.when(index == blocks - 1)(functools.partial(run, blocks))
        else:
            pl.when(index >= blocks - 1)(functools.partial(run, blocks))


def turn_back(value, cosine, sine):
    half = value.shape[-1] // 2
    first, second = value[:, :half], value[:, half:]
    return jnp.concatenate(
        [first * cosine + second * sine, second * cosine - first * sine], axis=-1
    )


def attend_back_kernel(
    block,
    reach,
    q_ref,
    k_ref,
    v_ref,
    g_ref,
    low_ref,
    log_ref,
    cos_ref,
    sin_ref,
    grad_ref,
    dk_ref,
    dv_ref,
):
    index = pl.program_id(1)
    steps = pl.num_programs(1)

    @pl.when(index == 0)
    def _():
        dk_ref[...] = jnp.zeros_like(dk_ref)
        dv_ref[...] = jnp.zeros_like(dv_ref)

    own = pl.ds(pl.multiple_of(index * block, block), block)

    def run(blocks):
        first = (index - (blocks - 1)) * block
        span = pl.ds(pl.multiple_of(first, block), blocks * block)
        query, grad = q_ref[...], g_ref[...]
        key = k_ref[span, :]
        bent, capped = score_parts(query, key, low_ref[...], index * block, first)
        prob = jnp.exp(capped - log_ref[...])
        grad_prob = lax.dot_general(
            grad, v_ref[span, :], (((1,), (1,)), ((), ())), preferred_element_type=jnp.float32
        )
        delta = jnp.sum(prob * grad_prob, axis=-1, keepdims=True)
        grad_score = (prob * (grad_prob - delta) * (1.0 - bent * bent)).astype(jnp.bfloat16)
        dq = jnp.dot(grad_score, key, preferred_element_type=jnp.float32)
        dq = dq * (1.0 / math.sqrt(HEAD_SIZE))
        dq = turn_back(dq, cos_ref[own, :], sin_ref[own, :])
        grad_ref[own, :HEAD_SIZE] = dq.astype(jnp.bfloat16)
        across = (((0,), (0,)), ((), ()))
        dk_ref[span, :] += lax.dot_general(
            grad_score, query, across, preferred_element_type=jnp.float32
        )
        dv_ref[span, :] += lax.dot_general(
            prob.astype(jnp.bfloat16), grad, across, preferred_element_type=jnp.float32
        )

    for blocks in range(1, reach + 1):
        if blocks < reach:
            pl.when(index == blocks - 1)(functools.partial(run, blocks))
        else:
            pl.when(index >= blocks - 1)(functools.partial(run, blocks))

    @pl.when(index == steps - 1)
    def _():
        dk = turn_back(dk_ref[...], cos_ref[...], sin_ref[...])
        grad_ref[:, HEAD_SIZE : 2 * HEAD_SIZE] = dk.astype(jnp.bfloat16)
        grad_ref[:, 2 * HEAD_SIZE :] = dv_ref[...].astype(jnp.bfloat16)


def block_shape(length):
    for block in (384, 256, 128):
        if length % block == 0:
            reach = min(length // block, (WIN - 1 + block - 1) // block + 1)
            return block, reach
    raise ValueError("sequence length")


def attend_specs(length, block):
    whole = pl.BlockSpec((None, length, HEAD_SIZE), lambda m, i: (m, 0, 0))
    half = pl.BlockSpec((None, length, HEAD_SIZE // 2), lambda m, i: (m, 0, 0))
    rows = pl.BlockSpec((None, block, HEAD_SIZE), lambda m, i: (m, i, 0))
    line = pl.BlockSpec((None, block, 1), lambda m, i: (m, i, 0))
    return whole, half, rows, line


def project_kernel(x_ref, w_ref, cos_ref, sin_ref, q_ref, k_ref, v_ref):
    product = final_dot(x_ref[...], w_ref[...])
    cosine, sine = cos_ref[...], sin_ref[...]
    query, key = product[:, :HEAD_SIZE], product[:, HEAD_SIZE : 2 * HEAD_SIZE]
    query = rotate(query, cosine, sine, 1.0) * (1.0 / math.sqrt(HEAD_SIZE))
    q_ref[...] = query.astype(jnp.bfloat16)
    k_ref[...] = rotate(key, cosine, sine, 1.0).astype(jnp.bfloat16)
    v_ref[...] = product[:, 2 * HEAD_SIZE :].astype(jnp.bfloat16)


def project(whole, weight, cosine, sine):
    batches, length, width = whole.shape
    block = block_shape(length)[0]
    _, _, rows, _ = attend_specs(length, block)
    half = pl.BlockSpec((None, block, HEAD_SIZE // 2), lambda m, i: (m, i, 0))
    return pl.pallas_call(
        project_kernel,
        grid=(batches, length // block),
        in_specs=[
            pl.BlockSpec((None, block, width), lambda m, i: (m, i, 0)),
            pl.BlockSpec(weight.shape, lambda m, i: (0, 0)),
            half,
            half,
        ],
        out_specs=[rows] * 3,
        out_shape=[jax.ShapeDtypeStruct((batches, length, HEAD_SIZE), jnp.bfloat16)] * 3,
        compiler_params=pltpu.CompilerParams(vmem_limit_bytes=40 * 2**20),
        cost_estimate=pl.CostEstimate(
            flops=6 * batches * length * width * HEAD_SIZE,
            bytes_accessed=2 * batches * length * width,
            transcendentals=0,
        ),
        name="project",
    )(whole, weight, cosine, sine)


def token_tables(tables, made):
    counts_ref, frequency_ref = tables
    cos_ref, sin_ref, low_ref = made
    batches, length, _ = cos_ref.shape
    block = block_shape(length)[0]
    for batch in range(batches):

        def step(index, carry, batch=batch):
            span = pl.ds(pl.multiple_of(index * block, 16), block)
            place = index * block + lax.broadcasted_iota(jnp.int32, (block, HEAD_SIZE // 2), 0)
            place = place.astype(jnp.float32)
            start = jnp.zeros_like(place)
            for number in range(1, DOCUMENTS):
                row = batch * (DOCUMENTS - 1) + number - 1
                count = counts_ref[row : row + 1, :]
                start = jnp.where(place >= count, count, start)
            phase_angle = (place - start) * frequency_ref[...]
            cos_ref[batch, span, :] = jnp.cos(phase_angle)
            sin_ref[batch, span, :] = jnp.sin(phase_angle)
            low = jnp.maximum(start, place - (WIN - 1))
            low_ref[batch, span, :] = low[:, :1].astype(jnp.int32)
            return carry

        lax.fori_loop(0, length // block, step, 0)


def attend(query, key, value, low_bound):
    batches, length = query.shape[:2]
    block, reach = block_shape(length)
    whole, half, rows, line = attend_specs(length, block)
    area = batches * block * block * reach * (length // block)
    return pl.pallas_call(
        functools.partial(attend_kernel, block, reach),
        grid=(batches, length // block),
        in_specs=[rows, whole, whole, line],
        out_specs=[rows, line],
        out_shape=[
            jax.ShapeDtypeStruct((batches, length, HEAD_SIZE), jnp.bfloat16),
            jax.ShapeDtypeStruct((batches, length, 1), jnp.float32),
        ],
        compiler_params=pltpu.CompilerParams(vmem_limit_bytes=40 * 2**20),
        cost_estimate=pl.CostEstimate(
            flops=4 * area * HEAD_SIZE,
            bytes_accessed=10 * batches * length * HEAD_SIZE,
            transcendentals=2 * area,
        ),
        name="attend",
    )(query, key, value, low_bound)


def attend_back(query, key, value, grad, low_bound, log_total, cosine, sine):
    batches, length = query.shape[:2]
    block, reach = block_shape(length)
    whole, half, rows, line = attend_specs(length, block)
    area = batches * block * block * reach * (length // block)
    return pl.pallas_call(
        functools.partial(attend_back_kernel, block, reach),
        grid=(batches, length // block),
        in_specs=[rows, whole, whole, rows, line, line, half, half],
        out_specs=pl.BlockSpec((None, length, 3 * HEAD_SIZE), lambda m, i: (m, 0, 0)),
        out_shape=jax.ShapeDtypeStruct((batches, length, 3 * HEAD_SIZE), jnp.bfloat16),
        scratch_shapes=[pltpu.VMEM((length, HEAD_SIZE), jnp.float32)] * 2,
        compiler_params=pltpu.CompilerParams(vmem_limit_bytes=48 * 2**20),
        cost_estimate=pl.CostEstimate(
            flops=10 * area * HEAD_SIZE,
            bytes_accessed=24 * batches * length * HEAD_SIZE,
            transcendentals=2 * area,
        ),
        name="attend_back",
    )(query, key, value, grad, low_bound, log_total, cosine, sine)


class ByHeads:
    def __init__(self, w_query, key_weight, value_weight, w_out):
        place = lax.axis_index("seq")
        count = lax.axis_size("seq")
        layers = lax.axis_size("fsdp")
        half = HEAD_SIZE // 2

        def columns(weight, width):
            return lax.dynamic_slice_in_dim(weight, place * width, width, axis=1)

        joined = jnp.concatenate(
            [columns(w_query, HEAD_SIZE), columns(key_weight, half), columns(value_weight, half)],
            axis=1,
        )
        self.joined = gather_rows(joined)
        own = self.joined[:, HEAD_SIZE:]
        other = lax.ppermute(own, "seq", [(i, i ^ 1) for i in range(count)])
        odd = place % 2 == 1
        low, high = jnp.where(odd, other, own), jnp.where(odd, own, other)
        self.weights = jnp.concatenate(
            [self.joined[:, :HEAD_SIZE], low[:, :half], high[:, :half], low[:, half:], high[:, half:]],
            axis=1,
        )
        depth = HEAD_SIZE // count
        here = QUERY_HEADS // layers
        part = w_out.reshape(here, count, depth, w_out.shape[1])
        part = lax.dynamic_index_in_dim(part, place, axis=1, keepdims=False)
        part = gather_rows(part.reshape(here * depth, -1))
        self.out_rows = swap_parts(part, 0, 0)

    def forward(self, normed, segments):
        batches, rows, width = normed.shape
        length = rows * lax.axis_size("seq")
        half = HEAD_SIZE // 2
        counts = [
            jnp.sum((segments[batch] < number).astype(jnp.float32))
            for batch in range(batches)
            for number in range(1, DOCUMENTS)
        ]
        counts += [jnp.zeros(())] * (8 - len(counts))
        counts = jnp.broadcast_to(jnp.stack(counts)[:, None], (8, half))
        counts = small_sum(counts, False, 8, "sum_counts")
        frequency = 10000.0 ** (-jnp.arange(half, dtype=jnp.float32) * 2.0 / HEAD_SIZE)
        table = jax.ShapeDtypeStruct((batches, length, half), jnp.float32)
        bound = jax.ShapeDtypeStruct((batches, length, 1), jnp.int32)
        whole, cosine, sine, low_bound = plane_gather(
            normed,
            0,
            "gather_normed",
            Job(
                None,
                tables=[counts, frequency[None]],
                spare=(token_tables, [table, table, bound]),
            ),
        )
        query, key, value = project(whole, self.weights, cosine, sine)
        attended, log_total = attend(query, key, value, low_bound)
        job = Job(
            rows_compute, weights=[self.out_rows], flops=2 * batches * length * HEAD_SIZE * width
        )
        (mixed,) = plane_scatter([attended], width, 1, "scatter_mixed", job)
        return mixed, (whole, query, key, value, low_bound, log_total, cosine, sine, attended)

    def backward(self, grad_mixed_b, saved, side, meanwhile):
        whole, query, key, value, low_bound, log_total, cosine, sine, attended = saved
        batches, length = key.shape[:2]
        width = grad_mixed_b.shape[-1]
        job = Job(
            head_back_compute,
            weights=[self.out_rows],
            outs=[(HEAD_SIZE, jnp.bfloat16)],
            side=side,
            sums=[(side[0].shape[2], side[1].shape[2])],
            flops=2 * batches * length * (HEAD_SIZE * width + side[0].shape[2] * side[1].shape[2]),
        )
        grad_whole, grad_att, side_sum = plane_gather(grad_mixed_b, 2, "gather_grad_mixed", job)
        grad_att, meanwhile = lax.optimization_barrier((grad_att, scatter_rows(meanwhile)))
        grads = attend_back(
            query, key, value, grad_att, low_bound, log_total, cosine, sine
        )
        self.record = (whole, grads, attended, grad_whole)
        job = Job(
            back_compute, weights=[self.weights], flops=6 * batches * length * HEAD_SIZE * width
        )
        (grad_normed,) = plane_scatter([grads], width, 3, "scatter_grad_normed", job)
        return grad_normed, side_sum, meanwhile

    def weight_grads(self):
        half = HEAD_SIZE // 2
        count = lax.axis_size("seq")
        layers = lax.axis_size("fsdp")
        whole, grads, attended, grad_whole = self.record
        joined = dot_rows(whole, grads).astype(jnp.bfloat16)
        k_low, k_high, v_low, v_high = (
            joined[:, HEAD_SIZE + half * i : HEAD_SIZE + half * (i + 1)] for i in range(4)
        )
        low = jnp.concatenate([k_low, v_low], axis=1)
        high = jnp.concatenate([k_high, v_high], axis=1)
        odd = lax.axis_index("seq") % 2 == 1
        came = lax.ppermute(
            jnp.where(odd, low, high), "seq", [(i, i ^ 1) for i in range(count)]
        )
        kept = jnp.where(odd, high, low)
        kept = (kept.astype(jnp.float32) + came.astype(jnp.float32)).astype(jnp.bfloat16)
        joined = scatter_rows(jnp.concatenate([joined[:, :HEAD_SIZE], kept], axis=1))

        width = grad_whole.shape[-1]
        out = dot_rows(attended, grad_whole).astype(jnp.bfloat16)
        out = scatter_rows(swap_parts(out, 0, 0))
        here = QUERY_HEADS // layers
        out = swap_parts(out.reshape(1, here, HEAD_SIZE // count, width), 3, 0)
        out = out.transpose(1, 0, 2, 3).reshape(here * HEAD_SIZE, -1)
        joined = joined.astype(jnp.float32)
        return (
            joined[:, :HEAD_SIZE],
            joined[:, HEAD_SIZE : HEAD_SIZE + half],
            joined[:, HEAD_SIZE + half :],
            out.astype(jnp.float32),
        )


class ByTokens:
    def __init__(self, w_query, key_weight, value_weight, w_out):
        self.weights = fetch_attention(w_query, key_weight, value_weight, w_out)
        self.records = []

    def forward(self, normed, segments):
        seg_whole = lax.all_gather(segments, "seq", axis=1, tiled=True)
        done = [self.forward_one(*pair) for pair in zip(normed, seg_whole)]
        return jnp.stack([mixed for mixed, _ in done]), [saved for _, saved in done]

    def forward_one(self, normed, seg_whole):
        token_rows = normed.shape[0]
        halo_count = (WIN - 2 + token_rows) // token_rows
        w_query, key_weight, value_weight, w_out = self.weights
        seq_place = lax.axis_index("seq")
        seg_here = lax.dynamic_slice_in_dim(seg_whole, seq_place * token_rows, token_rows)
        position = jnp.arange(seg_whole.shape[0], dtype=jnp.int32) - doc_starts(seg_whole)
        position = lax.dynamic_slice_in_dim(position, seq_place * token_rows, token_rows)
        cosine, sine = (table[:, None] for table in angles(position, HEAD_SIZE))
        query = rotate(
            final_dot(normed, w_query).reshape(token_rows, QUERY_HEADS, HEAD_SIZE),
            cosine,
            sine,
            1.0,
        )
        query = (query * (1.0 / math.sqrt(HEAD_SIZE))).astype(jnp.bfloat16)
        key = rotate(
            final_dot(normed, key_weight).reshape(token_rows, KEY_VALUE_HEADS, HEAD_SIZE),
            cosine,
            sine,
            1.0,
        ).astype(jnp.bfloat16)
        value = final_dot(normed, value_weight).reshape(token_rows, KEY_VALUE_HEADS, HEAD_SIZE)
        pair = key_window(jnp.stack([key, value.astype(jnp.bfloat16)]), halo_count)
        allowed = window_mask(seg_here, seg_whole, seq_place, token_rows, halo_count)
        query = query.reshape(token_rows, KEY_VALUE_HEADS, -1, HEAD_SIZE)
        score = jnp.einsum("qhgd,khd->hgqk", query, pair[0], preferred_element_type=jnp.float32)
        capped = jnp.where(allowed, CAP * jnp.tanh(score / CAP), -jnp.inf)
        peak = jnp.max(capped, axis=-1, keepdims=True)
        power = jnp.exp(capped - peak)
        total = jnp.sum(power, axis=-1, keepdims=True)
        attended = jnp.einsum(
            "hgqk,khd->qhgd",
            (power / total).astype(jnp.bfloat16),
            pair[1],
            preferred_element_type=jnp.float32,
        )
        attended = attended.reshape(token_rows, QUERY_HEADS * HEAD_SIZE).astype(jnp.bfloat16)
        mixed = final_dot(attended, w_out)
        log_total = peak + jnp.log(total)
        return mixed, (normed, query, pair, allowed, log_total, cosine, sine, attended)

    def backward(self, grad_mixed_b, saved, side, meanwhile):
        grads = [self.backward_one(*pair) for pair in zip(grad_mixed_b, saved)]
        return jnp.stack(grads), dot_rows(*side), scatter_rows(meanwhile)

    def backward_one(self, grad_mixed_b, saved):
        normed, query, pair, allowed, log_total, cosine, sine, attended = saved
        token_rows = normed.shape[0]
        halo_count = (WIN - 2 + token_rows) // token_rows
        w_query, key_weight, value_weight, w_out = self.weights
        grad_att = dot_back(grad_mixed_b, w_out).astype(jnp.bfloat16)
        grad_att = grad_att.reshape(token_rows, KEY_VALUE_HEADS, -1, HEAD_SIZE)
        score = jnp.einsum("qhgd,khd->hgqk", query, pair[0], preferred_element_type=jnp.float32)
        bent = jnp.tanh(score / CAP)
        prob = jnp.exp(jnp.where(allowed, CAP * bent, -jnp.inf) - log_total)
        grad_prob = jnp.einsum(
            "qhgd,khd->hgqk", grad_att, pair[1], preferred_element_type=jnp.float32
        )
        delta = jnp.sum(prob * grad_prob, axis=-1, keepdims=True)
        grad_score = (prob * (grad_prob - delta) * (1.0 - bent * bent)).astype(jnp.bfloat16)
        dq = jnp.einsum("hgqk,khd->qhgd", grad_score, pair[0], preferred_element_type=jnp.float32)
        dk = jnp.einsum("hgqk,qhgd->khd", grad_score, query, preferred_element_type=jnp.float32)
        dv = jnp.einsum(
            "hgqk,qhgd->khd", prob.astype(jnp.bfloat16), grad_att, preferred_element_type=jnp.float32
        )
        paired = window_grads(jnp.stack([dk, dv]), halo_count, token_rows)
        dq = rotate(
            dq.reshape(token_rows, QUERY_HEADS, HEAD_SIZE) * (1.0 / math.sqrt(HEAD_SIZE)),
            cosine,
            sine,
            -1.0,
        )
        dq = dq.reshape(token_rows, -1).astype(jnp.bfloat16)
        dk = rotate(paired[0], cosine, sine, -1.0).reshape(token_rows, -1).astype(jnp.bfloat16)
        dv = paired[1].reshape(token_rows, -1).astype(jnp.bfloat16)
        self.records.append((normed, dq, dk, dv, attended, grad_mixed_b))
        return dot_back(dq, w_query) + dot_back(dk, key_weight) + dot_back(dv, value_weight)

    def weight_grads(self):
        normed, dq, dk, dv, attended, grad_mixed_b = (
            jnp.concatenate(parts, axis=0) for parts in zip(*self.records)
        )
        normed = lax.all_gather(normed, "seq", axis=0, tiled=True)
        attended = lax.all_gather(attended, "seq", axis=0, tiled=True)
        sums = []
        for rows, grads in ((normed, dq), (normed, dk), (normed, dv), (attended, grad_mixed_b)):
            column_sum = dot_rows(rows, swap_parts(grads, 1, 0)).astype(jnp.bfloat16)
            owned = lax.psum_scatter(column_sum, "fsdp", scatter_dimension=0, tiled=True)
            sums.append(owned.astype(jnp.float32))
        return tuple(sums)


class FeedForward:
    def __init__(self, w_gate, w_up, w_down, by_kernel):
        place = lax.axis_index("seq")
        count = lax.axis_size("seq")
        self.by_kernel = by_kernel
        self.run = w_gate.shape[1] // (count * count)

        def columns(weight):
            parts = [
                lax.dynamic_slice_in_dim(
                    weight, (t * count + place) * self.run, self.run, axis=1
                )
                for t in range(count)
            ]
            return jnp.concatenate(parts, axis=1)

        here = w_down.shape[0] // (count * self.run)
        part = w_down.reshape(here, count, self.run, w_down.shape[1])
        part = lax.dynamic_index_in_dim(part, place, axis=1, keepdims=False)
        self.gate = gather_rows(columns(w_gate))
        self.up = gather_rows(columns(w_up))
        self.down = gather_rows(part.reshape(here * self.run, -1))

    def forward(self, ffn_in):
        hidden_width, width = self.down.shape
        if self.by_kernel:
            rows = ffn_in.shape[0] * ffn_in.shape[1] * lax.axis_size("seq")
            job = Job(
                hidden_compute,
                weights=[self.gate, self.up],
                outs=[(hidden_width, jnp.bfloat16)] * 3,
                flops=4 * rows * width * hidden_width,
            )
            whole, gate_proj, up_proj, hidden = plane_gather(ffn_in, 4, "gather_ffn_in", job)
            job = Job(
                rows_compute, weights=[self.down], flops=2 * rows * width * hidden_width
            )
            (down_proj,) = plane_scatter([hidden], width, 5, "scatter_down", job)
        else:
            whole = lax.all_gather(ffn_in, "seq", axis=1, tiled=True)
            gate_proj = final_dot(whole, self.gate)
            up_proj = final_dot(whole, self.up)
            hidden = geglu(gate_proj, up_proj).astype(jnp.bfloat16)
            down_proj = lax.psum_scatter(
                final_dot(hidden, self.down).astype(jnp.bfloat16),
                "seq",
                scatter_dimension=1,
                tiled=True,
            ).astype(jnp.float32)
        return down_proj, (whole, gate_proj, up_proj, hidden)

    def backward(self, grad_down_b, saved):
        whole, gate_proj, up_proj, hidden = saved
        hidden_width, width = self.down.shape
        if self.by_kernel:
            rows = whole.shape[0] * whole.shape[1]
            job = Job(
                hidden_back_compute,
                weights=[self.down],
                extras=[gate_proj, up_proj, hidden],
                outs=[(hidden_width, jnp.bfloat16)] * 2,
                sums=[(hidden_width, width)],
                flops=4 * rows * width * hidden_width,
            )
            _, grad_gate, grad_up, self.down_sum = plane_gather(
                grad_down_b, 6, "gather_grad_down", job
            )
            job = Job(
                back_compute,
                weights=[self.gate, self.up],
                side=[whole, grad_gate],
                sums=[(width, hidden_width)],
                flops=6 * rows * width * hidden_width,
            )
            grad_ffn_in, self.gate_sum = plane_scatter(
                [grad_gate, grad_up], width, 7, "scatter_grad_ffn_in", job
            )
        else:
            grad_whole = lax.all_gather(grad_down_b, "seq", axis=1, tiled=True)
            grad_hidden = dot_back(grad_whole, self.down)
            _, pullback = jax.vjp(geglu, gate_proj, up_proj)
            grad_gate, grad_up = (g.astype(jnp.bfloat16) for g in pullback(grad_hidden))
            partial = dot_back(grad_gate, self.gate) + dot_back(grad_up, self.up)
            grad_ffn_in = lax.psum_scatter(
                partial.astype(jnp.bfloat16), "seq", scatter_dimension=1, tiled=True
            ).astype(jnp.float32)
            self.down_sum = dot_rows(hidden, grad_whole)
            self.gate_sum = dot_rows(whole, grad_gate)
        self.up_side = (whole, grad_up)
        return grad_ffn_in

    def weight_grads(self, gate_own, up_own, down_own):
        count = lax.axis_size("seq")

        down = down_own
        here = down.shape[0] // self.run
        down = swap_parts(down.reshape(1, here, self.run, -1), 3, 0)
        down = down.transpose(1, 0, 2, 3).reshape(here * count * self.run, -1)

        def columns(own):
            return swap_parts(own, 1, 1).astype(jnp.float32)

        return columns(gate_own), columns(up_own), down.astype(jnp.float32)


def on_device(
    tokens,
    segments,
    w_query,
    key_weight,
    value_weight,
    w_out,
    w_gate,
    w_up,
    w_down,
    gain_attn_in,
    gain_attn_out,
    gain_ffn_in,
    gain_ffn_out,
    cotangent,
):
    by_kernel = (
        lax.axis_size("seq") == QUERY_HEADS
        and tokens.shape[0] == 2
        and QUERY_HEADS % lax.axis_size("fsdp") == 0
    )
    attention = (ByHeads if by_kernel else ByTokens)(w_query, key_weight, value_weight, w_out)
    ffn = FeedForward(w_gate, w_up, w_down, by_kernel)

    stream = tokens[:, 0].astype(jnp.float32)
    normed = rms_gain(stream, gain_attn_in).astype(jnp.bfloat16)
    mixed, attention_saved = attention.forward(normed, segments[:, 0])
    middle = stream + rms_gain(mixed, gain_attn_out)
    ffn_in = rms_gain(middle, gain_ffn_in).astype(jnp.bfloat16)
    down_proj, ffn_saved = ffn.forward(ffn_in)
    result = middle + rms_gain(down_proj, gain_ffn_out)

    grad_result = cotangent[:, 0].astype(jnp.float32)
    _, pullback = jax.vjp(rms_gain, down_proj, gain_ffn_out)
    grad_down, grad_gain_four = pullback(grad_result)
    grad_ffn_in = ffn.backward(grad_down.astype(jnp.bfloat16), ffn_saved)
    _, pullback = jax.vjp(rms_gain, middle, gain_ffn_in)
    grad_middle, grad_gain_three = pullback(grad_ffn_in)
    grad_middle = grad_result + grad_middle
    _, pullback = jax.vjp(rms_gain, mixed, gain_attn_out)
    grad_mixed, grad_gain_two = pullback(grad_middle)
    grad_mixed, down_own = lax.optimization_barrier(
        (grad_mixed.astype(jnp.bfloat16), scatter_rows(ffn.down_sum))
    )
    grad_normed, up_sum, gate_own = attention.backward(
        grad_mixed, attention_saved, ffn.up_side, ffn.gate_sum
    )
    _, pullback = jax.vjp(rms_gain, stream, gain_attn_in)
    grad_stream, grad_gain_one = pullback(grad_normed)
    grad_stream = grad_middle + grad_stream

    w_gate_grad, w_up_grad, w_down_grad = ffn.weight_grads(
        gate_own, scatter_rows(up_sum), down_own
    )
    query_grad, key_grad, value_grad, out_grad = attention.weight_grads()
    gains = jnp.stack([grad_gain_one, grad_gain_two, grad_gain_three, grad_gain_four])
    if by_kernel:
        gains = small_sum(jnp.pad(gains, ((0, 4), (0, 0))), True, 9, "sum_gains")
    else:
        gains = lax.psum(gains, ("seq", "fsdp"))
    return (
        result.astype(jnp.bfloat16)[:, None],
        grad_stream[:, None],
        query_grad,
        key_grad,
        value_grad,
        out_grad,
        w_gate_grad,
        w_up_grad,
        w_down_grad,
        gains[0],
        gains[1],
        gains[2],
        gains[3],
    )


def solution(mesh):
    in_specs = (
        P(None, "fsdp", "seq", None),
        P(None, "fsdp", "seq"),
        P("fsdp", None),
        P("fsdp", None),
        P("fsdp", None),
        P("fsdp", None),
        P("fsdp", None),
        P("fsdp", None),
        P("fsdp", None),
        P(),
        P(),
        P(),
        P(),
        P(None, "fsdp", "seq", None),
    )
    out_specs = (
        P(None, "fsdp", "seq", None),
        P(None, "fsdp", "seq", None),
        P("fsdp", "seq"),
        P("fsdp", "seq"),
        P("fsdp", "seq"),
        P("fsdp", "seq"),
        P("fsdp", "seq"),
        P("fsdp", "seq"),
        P("fsdp", "seq"),
        P(),
        P(),
        P(),
        P(),
    )
    return jax.shard_map(
        on_device, mesh=mesh, in_specs=in_specs, out_specs=out_specs, check_vma=False
    )
```

```python
import functools
import math

import jax
import jax.numpy as jnp
from jax import lax
from jax.experimental import pallas as pl
from jax.experimental.pallas import tpu as pltpu
from jax.sharding import PartitionSpec as P

QUERY_HEADS = 8
KEY_VALUE_HEADS = 4
HEAD_SIZE = 256
CAP = 50
WIN = 1024
DOCUMENTS = 4
VMEM_LIMIT = 60 * 2**20
SPAN_BYTES = 270_000_000


epsilon = 1e-06


def shifted(value, axis, steps):
    count = lax.axis_size(axis)
    initial, last = (max(0, -steps), min(count, count - steps))
    return lax.ppermute(value, axis, [(source, source + steps) for source in range(initial, last)])


def rms_gain(stream, gain):
    return stream * lax.rsqrt(jnp.mean(stream * stream, axis=-1, keepdims=True) + epsilon) * gain


def geglu(gate_proj, up_proj):
    return jax.nn.gelu(gate_proj, approximate=True) * up_proj


def angles(position, size):
    frequency = 10000.0 ** (-jnp.arange(size // 2, dtype=jnp.float32) * 2.0 / size)
    phase_angle = position.astype(jnp.float32)[..., None] * frequency
    return (jnp.cos(phase_angle), jnp.sin(phase_angle))


def rotate(value_rows, cosine_table, sine_table, direction):
    half_size = value_rows.shape[-1] // 2
    first_half = value_rows[..., :half_size]
    second = value_rows[..., half_size:]
    return jnp.concatenate(
        [
            first_half * cosine_table - direction * second * sine_table,
            second * cosine_table + direction * first_half * sine_table,
        ],
        axis=-1,
    )


def doc_starts(segment):
    starts = jnp.zeros_like(segment)
    for number in range(1, DOCUMENTS):
        count = jnp.sum((segment < number).astype(jnp.int32), axis=-1, keepdims=True)
        starts = jnp.where(segment >= number, count, starts)
    return starts


def final_dot(left_side, right_side):
    return jnp.dot(left_side, right_side, preferred_element_type=jnp.float32)


def dot_back(left_side, right_side):
    contract = (((left_side.ndim - 1,), (1,)), ((), ()))
    return lax.dot_general(left_side, right_side, contract, preferred_element_type=jnp.float32)


def dot_rows(left_side, right_side):
    left_side = left_side.reshape(-1, left_side.shape[-1])
    right_side = right_side.reshape(-1, right_side.shape[-1])
    return lax.dot_general(
        left_side, right_side, (((0,), (0,)), ((), ())), preferred_element_type=jnp.float32
    )


def fetch_attention(w_query, key_weight, value_weight, w_out):
    return (
        lax.all_gather(w_query, "fsdp", axis=0, tiled=True),
        lax.all_gather(key_weight, "fsdp", axis=0, tiled=True),
        lax.all_gather(value_weight, "fsdp", axis=0, tiled=True),
        lax.all_gather(w_out, "fsdp", axis=0, tiled=True),
    )


def key_window(kv_pair, halo_count):
    arrived = [shifted(kv_pair, "seq", offset) for offset in range(halo_count, 0, -1)]
    return jnp.concatenate(arrived + [kv_pair], axis=1)


def window_grads(paired_gradient, halo_count, token_rows):
    summed = paired_gradient[:, halo_count * token_rows :]
    for offset in range(1, halo_count + 1):
        begin = (halo_count - offset) * token_rows
        summed = summed + shifted(
            paired_gradient[:, begin : begin + token_rows].astype(jnp.bfloat16), "seq", -offset
        ).astype(jnp.float32)
    return summed


def window_mask(seg_here, seg_whole, seq_place, token_rows, halo_count):
    padded = jnp.concatenate([jnp.full((halo_count * token_rows,), -1, jnp.int32), seg_whole])
    key_seg = lax.dynamic_slice_in_dim(
        padded, seq_place * token_rows, (halo_count + 1) * token_rows
    )
    query_pos = seq_place * token_rows + jnp.arange(token_rows, dtype=jnp.int32)
    key_pos = (
        seq_place * token_rows
        - halo_count * token_rows
        + jnp.arange((halo_count + 1) * token_rows, dtype=jnp.int32)
    )
    distance = query_pos[:, None] - key_pos[None, :]
    return (seg_here[:, None] == key_seg[None, :]) & (distance >= 0) & (distance < WIN)


def gather_rows(rows):
    return lax.all_gather(rows, "fsdp", axis=0, tiled=True)


def scatter_rows(partial):
    return lax.psum_scatter(
        partial.astype(jnp.bfloat16), "fsdp", scatter_dimension=0, tiled=True
    )


def swap_parts(value, split_axis, concat_axis):
    return lax.all_to_all(
        value, "seq", split_axis=split_axis, concat_axis=concat_axis, tiled=True
    )


MESH = pl.DeviceIdType.MESH


def plane_places():
    me = lax.axis_index("seq")
    other_core = me + 1 - 2 * (me % 2)
    along_x = me + 2 - 4 * ((me // 2) % 2)
    along_y = me + 4 - 8 * (me // 4)
    return me, other_core, along_x, along_y


def greet(neighbours, spread=None):
    barrier = pltpu.get_barrier_semaphore()
    for neighbour in neighbours:
        pl.semaphore_signal(barrier, inc=1, device_id={"seq": neighbour}, device_id_type=MESH)
    count = len(neighbours)
    if spread is not None:
        count = count + spread.greet(barrier)
    pl.semaphore_wait(barrier, count)


class Spread:
    def __init__(self, parts_ref, placed_ref, send, recv):
        self.parts, self.placed, self.send, self.recv = parts_ref, placed_ref, send, recv
        self.me, self.layer = lax.axis_index("seq"), lax.axis_index("fsdp")
        layers = lax.axis_size("fsdp")
        shared = lax.axis_size("seq") // layers
        self.owner = self.me // shared
        self.slot = (self.me - self.owner * shared) * layers + self.layer
        self.targets = [(place, self.owner) for place in range(shared * layers)]
        self.sources = [
            (self.layer * shared + part, from_layer)
            for part in range(shared)
            for from_layer in range(layers)
        ]

    def away(self, device):
        return (device[0] != self.me) | (device[1] != self.layer)

    def greet(self, barrier):
        for place, layer in self.targets + self.sources:

            @pl.when(self.away((place, layer)))
            def _(place=place, layer=layer):
                device = {"seq": place, "fsdp": layer}
                pl.semaphore_signal(barrier, inc=1, device_id=device, device_id_type=MESH)

        return 2 * len(self.targets) - 2 * (self.owner == self.layer).astype(jnp.int32)

    def copy(self, index, slot, device):
        return pltpu.make_async_remote_copy(
            src_ref=self.parts.at[index],
            dst_ref=self.placed.at[slot],
            send_sem=self.send.at[index],
            recv_sem=self.recv.at[slot],
            device_id={"seq": device[0], "fsdp": device[1]},
            device_id_type=MESH,
        )

    def own(self):
        source, target = self.parts.at[self.me], self.placed.at[self.slot]
        return pltpu.make_async_copy(source, target, self.send.at[len(self.targets)])

    def begin(self):
        for index, device in enumerate(self.targets):
            pl.when(self.away(device))(self.copy(index, self.slot, device).start)
        pl.when(self.owner == self.layer)(self.own().start)

    def end(self):
        for index, device in enumerate(self.targets):
            pl.when(self.away(device))(self.copy(index, self.slot, device).wait_send)
        for index, device in enumerate(self.sources):
            pl.when(self.away(device))(self.copy(0, index, device).wait_recv)
        pl.when(self.owner == self.layer)(self.own().wait)


BRAID = 384


def braid_width(arrays):
    return sum(array.shape[-1] for array in arrays)


def braided(arrays):
    return len(arrays) == 2 and arrays[0].shape[-1] == arrays[1].shape[-1]


def copies_into(sources, target, sem):
    if not braided(sources):
        copies, at = [], 0
        for i, source in enumerate(sources):
            width = source.shape[-1]
            copies.append(
                pltpu.make_async_copy(source, target.at[:, pl.ds(at, width)], sem.at[i])
            )
            at += width
        return copies
    groups = sources[0].shape[-1] // BRAID
    copies = []
    for group in range(groups):
        for part, source in enumerate(sources):
            at = group * len(sources) + part
            copies.append(
                pltpu.make_async_copy(
                    source.at[:, pl.ds(group * BRAID, BRAID)],
                    target.at[:, pl.ds(at * BRAID, BRAID)],
                    sem.at[at],
                )
            )
    return copies


def copy_count(arrays):
    return braid_width(arrays) // BRAID if braided(arrays) else len(arrays)


def unit_rows(place, rows):
    return pl.ds(pl.multiple_of((place // 2) * (2 * rows), 16), 2 * rows)


class Job:
    def __init__(
        self,
        compute,
        weights=(),
        extras=(),
        outs=(),
        sums=(),
        side=(),
        tables=(),
        spare=None,
        spread=None,
        flops=0,
    ):
        self.spread = spread
        self.compute, self.flops, self.spare = compute, flops, spare
        self.tables = list(tables)
        self.weights, self.extras, self.outs = list(weights), list(extras), list(outs)
        self.sums, self.side = list(sums), list(side)


def gather_kernel(job, rows, *refs):
    refs = list(refs)
    take = lambda n: [refs.pop(0) for _ in range(n)]
    (local_ref,) = take(1)
    weight_refs, extra_refs, side_refs = (
        take(len(job.weights)),
        take(len(job.extras)),
        take(len(job.side)),
    )
    table_refs = take(len(job.tables))
    (whole_ref,), out_refs, final_refs = take(1), take(len(job.outs)), take(len(job.sums))
    made_refs = take(len(job.spare[1]) if job.spare else 0)
    send_sem, recv_sem, own_sem, x_buf = take(4)
    weight_bufs = take(1 if job.weights else 0)
    extra_bufs, side_bufs, out_bufs = (
        take(len(job.extras)),
        take(len(job.side)),
        take(len(job.outs)),
    )
    sum_bufs, final_bufs = take(len(job.sums)), take(len(job.sums))
    weight_sem, load_sem, side_sem, store_sem, final_sem = take(5)

    me, other_core, along_x, along_y = plane_places()
    across = along_x + along_y - me
    core = me % 2

    def piece(batch, place):
        return whole_ref.at[batch, pl.ds(pl.multiple_of(place * rows, 16), rows)]

    def transfer(slot, source, batch, place, target):
        return pltpu.make_async_remote_copy(
            src_ref=source,
            dst_ref=piece(batch, place),
            send_sem=send_sem.at[slot],
            recv_sem=recv_sem.at[slot],
            device_id={"seq": target},
            device_id_type=MESH,
        )

    def forward(slot, batch, place, target):
        return transfer(slot, piece(batch, place), batch, place, target)

    moves = [
        transfer(0, local_ref.at[0], 0, me, along_x),
        transfer(1, local_ref.at[1], 1, me, along_x),
        transfer(2, local_ref.at[1], 1, me, along_y),
        transfer(3, local_ref.at[0], 0, me, along_y),
        forward(4, 0, along_x, along_y),
        forward(5, 1, along_y, along_x),
        transfer(6, local_ref.at[0], 0, me, other_core),
        transfer(7, local_ref.at[1], 1, me, other_core),
        forward(8, 0, along_x, other_core),
        forward(9, 1, along_x, other_core),
        forward(10, 1, along_y, other_core),
        forward(11, 0, along_y, other_core),
        forward(12, 0, across, other_core),
        forward(13, 1, across, other_core),
    ]
    greet((other_core, along_x, along_y))
    for slot in (0, 2, 1, 3, 6, 7):
        moves[slot].start()
    owns = [
        pltpu.make_async_copy(local_ref.at[batch], piece(batch, me), own_sem.at[batch])
        for batch in range(2)
    ]
    for own in owns:
        own.start()
    fetches = copies_into(weight_refs, weight_bufs[0], weight_sem) if job.weights else []
    for fetch in fetches:
        fetch.start()
    if job.spare:
        job.spare[0](table_refs, made_refs)
    stores = []

    order = [
        (me, 0),
        (me, 1),
        (along_x, 0),
        (along_y, 1),
        (along_x, 1),
        (along_y, 0),
        (across, 0),
        (across, 1),
    ]

    def extra_loads(step):
        place, batch = order[step]
        span = unit_rows(place, rows)
        return [
            pltpu.make_async_copy(ref.at[batch, span], buf.at[step % 2], load_sem.at[2 + i, step % 2])
            for i, (ref, buf) in enumerate(zip(extra_refs, extra_bufs))
        ]

    for load in extra_loads(0):
        load.start()

    def own_half(which):
        return x_buf.at[pl.ds(pl.multiple_of(which * rows, 16), rows)]

    def unit(place, batch, own=False):
        if job.compute is None:
            return
        span = unit_rows(place, rows)
        if own:
            loads = [
                pltpu.make_async_copy(local_ref.at[batch], own_half(core), load_sem.at[0, 0]),
                pltpu.make_async_copy(
                    piece(batch, other_core), own_half(1 - core), load_sem.at[1, 0]
                ),
            ]
        else:
            loads = [pltpu.make_async_copy(whole_ref.at[batch, span], x_buf, load_sem.at[0, 0])]
        step = len(stores)
        for load in loads:
            load.start()
        loads += extra_loads(step)
        if step < 7:
            for load in extra_loads(step + 1):
                load.start()
        if step == 0:
            for fetch in fetches:
                fetch.wait()
        if step >= 2:
            for store in stores[step - 2]:
                store.wait()
        for load in loads:
            load.wait()
        slot = step % 2
        extras = [buf.at[slot] for buf in extra_bufs]
        outs = [buf.at[slot] for buf in out_bufs]
        job.compute(x_buf, weight_bufs, extras, outs, sum_bufs, step == 0)
        stores.append(
            [
                pltpu.make_async_copy(buf.at[slot], ref.at[batch, span], store_sem.at[slot, i])
                for i, (ref, buf) in enumerate(zip(out_refs, out_bufs))
            ]
        )
        for store in stores[-1]:
            store.start()

    side = Side(rows, side_refs, side_bufs, sum_bufs, side_sem)

    for batch in range(2):
        moves[6 + batch].wait_recv()
        unit(me, batch, own=True)
        side.run(1)
    moves[0].wait_recv()
    moves[4].start()
    moves[8].start()
    moves[2].wait_recv()
    moves[5].start()
    moves[10].start()
    side.run(2)
    moves[8].wait_recv()
    unit(along_x, 0)
    moves[10].wait_recv()
    unit(along_y, 1)
    side.run(1)
    moves[1].wait_recv()
    moves[9].start()
    moves[3].wait_recv()
    moves[11].start()
    side.run(3)
    moves[9].wait_recv()
    unit(along_x, 1)
    moves[11].wait_recv()
    unit(along_y, 0)
    early = 1 if job.side else 0
    finish_sums(sum_bufs[:early], final_bufs[:early], final_refs[:early], final_sem)
    moves[4].wait_recv()
    moves[12].start()
    moves[5].wait_recv()
    moves[13].start()
    moves[12].wait_recv()
    unit(across, 0)
    moves[13].wait_recv()
    unit(across, 1)
    finish_sums(sum_bufs[early:], final_bufs[early:], final_refs[early:], final_sem)
    for move in moves:
        move.wait_send()
    for own in owns:
        own.wait()
    for group in stores[-2:]:
        for store in group:
            store.wait()


class Side:
    def __init__(self, rows, refs, bufs, sums, sem):
        self.rows, self.refs, self.bufs, self.sums, self.sem = rows, refs, bufs, sums, sem
        self.block = 0
        self.start()

    def copies(self):
        span = pl.ds((self.block % 4) * 2 * self.rows, 2 * self.rows)
        return [
            pltpu.make_async_copy(ref.at[self.block // 4, span], buf, self.sem.at[i])
            for i, (ref, buf) in enumerate(zip(self.refs, self.bufs))
        ]

    def start(self):
        if self.refs and self.block < 8:
            for copy in self.copies():
                copy.start()

    def run(self, count):
        for _ in range(count if self.refs else 0):
            for copy in self.copies():
                copy.wait()
            add_outer(self.bufs[0], self.bufs[1], self.sums[0], self.block == 0)
            self.block += 1
            self.start()


def finish_sums(sum_bufs, final_bufs, final_refs, sem):
    for i, (total, buf, ref) in enumerate(zip(sum_bufs, final_bufs, final_refs)):
        copies = []
        size = buf.shape[1]
        for block in range(total.shape[0] // size):
            slot = block % 2
            span = pl.ds(block * size, size)
            if block >= 2:
                copies[block - 2].wait()
            buf[slot] = total[span, :].astype(buf.dtype)
            copies.append(pltpu.make_async_copy(buf.at[slot], ref.at[span], sem.at[i, slot]))
            copies[-1].start()
        for copy in copies[-2:]:
            copy.wait()


def plane_gather(local, ident, name, job=None):
    job = job or Job(None)
    batches, rows, width = local.shape
    length = rows * lax.axis_size("seq")
    semaphores = pltpu.SemaphoreType.DMA
    scratch = [semaphores((14,)), semaphores((14,)), semaphores((2,))]
    scratch += [pltpu.VMEM((2 * rows if job.compute else 8, width), local.dtype)]
    if job.weights:
        depth = job.weights[0].shape[0]
        scratch += [pltpu.VMEM((depth, braid_width(job.weights)), job.weights[0].dtype)]
    scratch += [pltpu.VMEM((2, 2 * rows, array.shape[2]), array.dtype) for array in job.extras]
    scratch += [pltpu.VMEM((2 * rows, array.shape[2]), array.dtype) for array in job.side]
    scratch += [pltpu.VMEM((2, 2 * rows, wide), kind) for wide, kind in job.outs]
    scratch += [pltpu.VMEM(shape, jnp.float32) for shape in job.sums]
    scratch += [pltpu.VMEM((2, HEAD_SIZE // 2, shape[1]), jnp.bfloat16) for shape in job.sums]
    scratch += [
        semaphores((copy_count(job.weights) if job.weights else 1,)),
        semaphores((2 + len(job.extras), 2)),
        semaphores((max(1, len(job.side)),)),
        semaphores((2, max(1, len(job.outs)))),
        semaphores((max(1, len(job.sums)), 2)),
    ]
    any_space = pl.BlockSpec(memory_space=pl.ANY)
    out_shape = [jax.ShapeDtypeStruct((batches, length, width), local.dtype)]
    out_shape += [jax.ShapeDtypeStruct((batches, length, wide), kind) for wide, kind in job.outs]
    out_shape += [jax.ShapeDtypeStruct(shape, jnp.bfloat16) for shape in job.sums]
    inputs = [local, *job.weights, *job.extras, *job.side]
    in_specs = [any_space] * len(inputs)
    in_specs += [pl.BlockSpec(memory_space=pltpu.VMEM)] * len(job.tables)
    inputs += job.tables
    out_specs = [any_space] * len(out_shape)
    if job.spare:
        out_shape += job.spare[1]
        out_specs += [pl.BlockSpec(memory_space=pltpu.VMEM)] * len(job.spare[1])
    return pl.pallas_call(
        functools.partial(gather_kernel, job, rows),
        in_specs=in_specs,
        out_specs=out_specs,
        out_shape=out_shape,
        scratch_shapes=scratch,
        compiler_params=pltpu.CompilerParams(
            collective_id=ident, has_side_effects=True, vmem_limit_bytes=VMEM_LIMIT
        ),
        cost_estimate=pl.CostEstimate(
            flops=job.flops, bytes_accessed=SPAN_BYTES, transcendentals=0
        ),
        name=name,
    )(*inputs)


def scatter_kernel(job, rows, *refs):
    refs = list(refs)
    take = lambda n: [refs.pop(0) for _ in range(n)]
    part_refs, weight_refs, side_refs = (
        take(len(job.extras)),
        take(len(job.weights)),
        take(len(job.side)),
    )
    spread_refs = take(1 if job.spread is not None else 0)
    (out_ref,), final_refs = take(1), take(len(job.sums))
    spread_refs += take(len(spread_refs))
    part_buf, weight_buf, sums, held, from_core, from_link, out_buf = take(7)
    side_bufs, sum_bufs, final_bufs = take(len(job.side)), take(len(job.sums)), take(len(job.sums))
    weight_sem, load_sem, side_sem, final_sem, out_sem = take(5)
    core_send, core_recv, link_send, link_recv, credit = take(5)
    spread = Spread(*spread_refs, *take(2)) if spread_refs else None

    me, other_core, along_x, along_y = plane_places()
    across = along_x + along_y - me
    core = me % 2
    kept = pl.ds(pl.multiple_of(core * rows, 16), rows)
    given = pl.ds(pl.multiple_of((1 - core) * rows, 16), rows)
    units = [
        (across, 0),
        (across, 1),
        (along_x, 0),
        (along_y, 1),
        (along_x, 1),
        (along_y, 0),
        (me, 0),
        (me, 1),
    ]
    targets = [along_x, along_y, along_x, along_y, along_x, along_y]
    added = {4: (1,), 5: (0,), 6: (2, 5), 7: (3, 4)}

    def load(step):
        place, batch = units[step]
        span = unit_rows(place, rows)
        sources = [ref.at[batch, span] for ref in part_refs]
        return copies_into(sources, part_buf.at[step % 2], load_sem.at[step % 2])

    loads = [load(step) for step in range(8)]
    fetches = copies_into(weight_refs, weight_buf, weight_sem)
    for copy in loads[0] + fetches:
        copy.start()
    gives = [
        pltpu.make_async_remote_copy(
            src_ref=sums.at[step % 2, given],
            dst_ref=from_core.at[step % 4],
            send_sem=core_send.at[step],
            recv_sem=core_recv.at[step],
            device_id={"seq": other_core},
            device_id_type=MESH,
        )
        for step in range(8)
    ]
    sends = [
        pltpu.make_async_remote_copy(
            src_ref=held.at[step],
            dst_ref=from_link.at[step],
            send_sem=link_send.at[step],
            recv_sem=link_recv.at[step],
            device_id={"seq": targets[step]},
            device_id_type=MESH,
        )
        for step in range(6)
    ]
    greet((other_core, along_x, along_y), spread)
    if spread is not None:
        spread.begin()

    def finish(step):
        gives[step].wait_recv()
        kind = jnp.bfloat16 if step < 4 else jnp.float32
        total = sums[step % 2, kept].astype(kind) + from_core[step % 4].astype(kind)
        if step < 4:
            pl.semaphore_signal(credit, inc=1, device_id={"seq": other_core}, device_id_type=MESH)
        for arrived in added.get(step, ()):
            sends[arrived].wait_recv()
            total = total + from_link[arrived].astype(jnp.float32)
        if step < 6:
            held[step] = total.astype(jnp.bfloat16)
            sends[step].start()
        else:
            out = pltpu.make_async_copy(out_buf, out_ref.at[step - 6], out_sem.at[step - 6])
            out_buf[...] = total
            out.start()
            out.wait()

    side = Side(rows, side_refs, side_bufs, sum_bufs, side_sem)
    for step in range(8):
        for copy in loads[step]:
            copy.wait()
        if step == 0:
            for fetch in fetches:
                fetch.wait()
        if step < 7:
            for copy in loads[step + 1]:
                copy.start()
        if step >= 2:
            gives[step - 2].wait_send()
        job.compute(part_buf.at[step % 2], weight_buf, sums.at[step % 2])
        if step >= 4:
            pl.semaphore_wait(credit, 1)
        gives[step].start()
        if step >= 1:
            finish(step - 1)
        side.run((0, 0, 1, 1, 1, 1, 2, 2)[step])
    if job.side:
        finish_sums(sum_bufs, final_bufs, final_refs, final_sem)
    finish(7)
    for move in gives[6:] + sends:
        move.wait_send()
    if spread is not None:
        spread.end()


def plane_scatter(parts, width, ident, name, job):
    job.extras = list(parts)
    batches, length = parts[0].shape[:2]
    rows = length // lax.axis_size("seq")
    any_space = pl.BlockSpec(memory_space=pl.ANY)
    semaphores = pltpu.SemaphoreType.DMA
    weights = job.weights
    scratch = [
        pltpu.VMEM((2, 2 * rows, braid_width(parts)), parts[0].dtype),
        pltpu.VMEM((weights[0].shape[0], braid_width(weights)), weights[0].dtype),
        pltpu.VMEM((2, 2 * rows, width), jnp.bfloat16),
        pltpu.VMEM((6, rows, width), jnp.bfloat16),
        pltpu.VMEM((4, rows, width), jnp.bfloat16),
        pltpu.VMEM((6, rows, width), jnp.bfloat16),
        pltpu.VMEM((rows, width), jnp.float32),
    ]
    scratch += [pltpu.VMEM((2 * rows, array.shape[2]), array.dtype) for array in job.side]
    scratch += [pltpu.VMEM(shape, jnp.float32) for shape in job.sums]
    scratch += [pltpu.VMEM((2, HEAD_SIZE // 2, shape[1]), jnp.bfloat16) for shape in job.sums]
    scratch += [
        semaphores((copy_count(weights),)),
        semaphores((2, copy_count(parts))),
        semaphores((max(1, len(job.side)),)),
        semaphores((max(1, len(job.sums)), 2)),
        semaphores((2,)),
        semaphores((8,)),
        semaphores((8,)),
        semaphores((6,)),
        semaphores((6,)),
        pltpu.SemaphoreType.REGULAR,
    ]
    out_shape = [jax.ShapeDtypeStruct((batches, rows, width), jnp.float32)]
    out_shape += [jax.ShapeDtypeStruct(shape, jnp.bfloat16) for shape in job.sums]
    inputs = [*parts, *weights, *job.side]
    if job.spread is not None:
        inputs.append(job.spread)
        out_shape.append(jax.ShapeDtypeStruct(job.spread.shape, job.spread.dtype))
        scratch += [semaphores((job.spread.shape[0] + 1,)), semaphores((job.spread.shape[0],))]
    return pl.pallas_call(
        functools.partial(scatter_kernel, job, rows),
        in_specs=[any_space] * len(inputs),
        out_specs=[any_space] * len(out_shape),
        out_shape=out_shape,
        scratch_shapes=scratch,
        compiler_params=pltpu.CompilerParams(
            collective_id=ident, has_side_effects=True, vmem_limit_bytes=VMEM_LIMIT
        ),
        cost_estimate=pl.CostEstimate(
            flops=job.flops, bytes_accessed=SPAN_BYTES, transcendentals=0
        ),
        name=name,
    )(*inputs)


def small_sum_kernel(over_layers, value_ref, out_ref, plane_buf, layer_buf, *sems):
    plane_send, plane_recv, layer_send, layer_recv = sems
    neighbours = plane_places()[1:]
    layer, layers = lax.axis_index("fsdp"), lax.axis_size("fsdp")
    others = [lax.rem(layer + hop, layers) for hop in range(1, layers)] if over_layers else []
    barrier = pltpu.get_barrier_semaphore()
    for neighbour in neighbours:
        pl.semaphore_signal(barrier, inc=1, device_id={"seq": neighbour}, device_id_type=MESH)
    for other in others:
        pl.semaphore_signal(barrier, inc=1, device_id={"fsdp": other}, device_id_type=MESH)
    pl.semaphore_wait(barrier, len(neighbours) + len(others))
    out_ref[...] = value_ref[...]
    copies = []
    for turn, neighbour in enumerate(neighbours):
        plane_buf[turn, 0] = out_ref[...]
        copies.append(
            pltpu.make_async_remote_copy(
                src_ref=plane_buf.at[turn, 0],
                dst_ref=plane_buf.at[turn, 1],
                send_sem=plane_send.at[turn],
                recv_sem=plane_recv.at[turn],
                device_id={"seq": neighbour},
                device_id_type=MESH,
            )
        )
        copies[-1].start()
        copies[-1].wait_recv()
        out_ref[...] = plane_buf[turn, 0] + plane_buf[turn, 1]
    if over_layers:
        layer_buf[layer] = out_ref[...]
        layer_copies = [
            pltpu.make_async_remote_copy(
                src_ref=layer_buf.at[layer],
                dst_ref=layer_buf.at[layer],
                send_sem=layer_send.at[hop],
                recv_sem=layer_recv.at[hop],
                device_id={"fsdp": other},
                device_id_type=MESH,
            )
            for hop, other in enumerate(others)
        ]
        for copy in layer_copies:
            copy.start()
        for copy in layer_copies:
            copy.wait_recv()
        total = layer_buf[0]
        for index in range(1, layers):
            total = total + layer_buf[index]
        out_ref[...] = total
        copies += layer_copies
    for copy in copies:
        copy.wait_send()


def small_sum(value, over_layers, ident, name):
    layers = lax.axis_size("fsdp")
    semaphores = pltpu.SemaphoreType.DMA
    return pl.pallas_call(
        functools.partial(small_sum_kernel, over_layers),
        in_specs=[pl.BlockSpec(memory_space=pltpu.VMEM)],
        out_specs=pl.BlockSpec(memory_space=pltpu.VMEM),
        out_shape=jax.ShapeDtypeStruct(value.shape, jnp.float32),
        scratch_shapes=[
            pltpu.VMEM((3, 2) + value.shape, jnp.float32),
            pltpu.VMEM((layers,) + value.shape, jnp.float32),
            semaphores((3,)),
            semaphores((3,)),
            semaphores((layers,)),
            semaphores((layers,)),
        ],
        compiler_params=pltpu.CompilerParams(collective_id=ident, has_side_effects=True),
        name=name,
    )(value)


def tiles(width, tile, body):
    def step(index, carry):
        body(pl.ds(pl.multiple_of(index * tile, 128), tile))
        return carry

    lax.fori_loop(0, width // tile, step, 0)


GELU_SCALE = 0.7978845608
GELU_CUBE = 0.044715


def gelu_parts(gate):
    square = gate * gate
    bent = jnp.tanh(GELU_SCALE * gate * (1.0 + GELU_CUBE * square))
    half = 0.5 * (1.0 + bent)
    slope = half + 0.5 * gate * (1.0 - bent * bent) * GELU_SCALE * (1.0 + 3.0 * GELU_CUBE * square)
    return gate * half, slope


def add_outer(left, right, total, first):
    def body(span):
        outer = lax.dot_general(
            left[:, span], right[...], (((0,), (0,)), ((), ())), preferred_element_type=jnp.float32
        )
        total[span, :] = outer if first else total[span, :] + outer

    wide = left.shape[1]
    tiles(wide, next(tile for tile in (2 * BRAID, BRAID, HEAD_SIZE) if wide % tile == 0), body)


def hidden_compute(x_buf, weights, extras, outs, sums, first):
    gate_out, up_out, hidden_out = outs
    (weight,) = weights

    def step(index, carry):
        both = pl.ds(pl.multiple_of(index * 2 * BRAID, 128), 2 * BRAID)
        span = pl.ds(pl.multiple_of(index * BRAID, 128), BRAID)
        product = final_dot(x_buf[...], weight[:, both])
        gate, up = product[:, :BRAID], product[:, BRAID:]
        gate_out[:, span] = gate.astype(gate_out.dtype)
        up_out[:, span] = up.astype(up_out.dtype)
        hidden_out[:, span] = (gelu_parts(gate)[0] * up).astype(hidden_out.dtype)
        return carry

    lax.fori_loop(0, weight.shape[1] // (2 * BRAID), step, 0)


def hidden_back_compute(x_buf, weights, extras, outs, sums, first):
    (down_w,) = weights
    gate_in, up_in, hidden_in = extras
    gate_out, up_out = outs
    product = dot_back(x_buf[...], down_w[...])
    for start in range(0, product.shape[1], BRAID):
        span = slice(start, start + BRAID)
        grad = product[:, span]
        value, slope = gelu_parts(gate_in[:, span].astype(jnp.float32))
        gate_out[:, span] = (grad * up_in[:, span].astype(jnp.float32) * slope).astype(
            gate_out.dtype
        )
        up_out[:, span] = (grad * value).astype(up_out.dtype)
    add_outer(hidden_in, x_buf, sums[0], first)


def head_back_compute(x_buf, weights, extras, outs, sums, first):
    outs[0][...] = dot_back(x_buf[...], weights[0][...]).astype(outs[0].dtype)
    add_outer(extras[0], x_buf, sums[1], first)


def rows_compute(part, weight, out):
    def body(span):
        out[:, span] = final_dot(part[...], weight[:, span]).astype(out.dtype)

    tiles(weight.shape[1], 2 * BRAID, body)


def back_compute(part, weight, out):
    def body(span):
        out[:, span] = dot_back(part[...], weight[span, :]).astype(out.dtype)

    tiles(weight.shape[0], 2 * BRAID, body)


def score_parts(query, key, low_bound, row_start, col_start):
    raw = lax.dot_general(
        query, key, (((1,), (1,)), ((), ())), preferred_element_type=jnp.float32
    )
    bent = jnp.tanh(raw * (1.0 / CAP))
    shape = raw.shape
    row = row_start + lax.broadcasted_iota(jnp.int32, shape, 0)
    col = col_start + lax.broadcasted_iota(jnp.int32, shape, 1)
    allowed = (col <= row) & (col >= low_bound)
    return bent, jnp.where(allowed, CAP * bent, -1e30)


def attend_kernel(block, reach, q_ref, k_ref, v_ref, low_ref, out_ref, log_ref):
    index = pl.program_id(1)

    def run(blocks):
        first = (index - (blocks - 1)) * block
        span = pl.ds(pl.multiple_of(first, block), blocks * block)
        _, capped = score_parts(
            q_ref[...], k_ref[span, :], low_ref[...], index * block, first
        )
        peak = jnp.max(capped, axis=-1, keepdims=True)
        power = jnp.exp(capped - peak)
        total = jnp.sum(power, axis=-1, keepdims=True)
        prob = (power * (1.0 / total)).astype(jnp.bfloat16)
        out = jnp.dot(prob, v_ref[span, :], preferred_element_type=jnp.float32)
        out_ref[...] = out.astype(jnp.bfloat16)
        log_ref[...] = peak + jnp.log(total)

    for blocks in range(1, reach + 1):
        if blocks < reach:
            pl.when(index == blocks - 1)(functools.partial(run, blocks))
        else:
            pl.when(index >= blocks - 1)(functools.partial(run, blocks))


def turn_back(value, cosine, sine):
    half = value.shape[-1] // 2
    first, second = value[:, :half], value[:, half:]
    return jnp.concatenate(
        [first * cosine + second * sine, second * cosine - first * sine], axis=-1
    )


def attend_back_kernel(
    block,
    reach,
    q_ref,
    k_ref,
    v_ref,
    g_ref,
    low_ref,
    log_ref,
    cos_ref,
    sin_ref,
    grad_ref,
    dk_ref,
    dv_ref,
):
    index = pl.program_id(1)
    steps = pl.num_programs(1)

    @pl.when(index == 0)
    def _():
        dk_ref[...] = jnp.zeros_like(dk_ref)
        dv_ref[...] = jnp.zeros_like(dv_ref)

    own = pl.ds(pl.multiple_of(index * block, block), block)

    def run(blocks):
        first = (index - (blocks - 1)) * block
        span = pl.ds(pl.multiple_of(first, block), blocks * block)
        query, grad = q_ref[...], g_ref[...]
        key = k_ref[span, :]
        bent, capped = score_parts(query, key, low_ref[...], index * block, first)
        prob = jnp.exp(capped - log_ref[...])
        grad_prob = lax.dot_general(
            grad, v_ref[span, :], (((1,), (1,)), ((), ())), preferred_element_type=jnp.float32
        )
        delta = jnp.sum(prob * grad_prob, axis=-1, keepdims=True)
        grad_score = (prob * (grad_prob - delta) * (1.0 - bent * bent)).astype(jnp.bfloat16)
        dq = jnp.dot(grad_score, key, preferred_element_type=jnp.float32)
        dq = dq * (1.0 / math.sqrt(HEAD_SIZE))
        dq = turn_back(dq, cos_ref[own, :], sin_ref[own, :])
        grad_ref[own, :HEAD_SIZE] = dq.astype(jnp.bfloat16)
        across = (((0,), (0,)), ((), ()))
        dk_ref[span, :] += lax.dot_general(
            grad_score, query, across, preferred_element_type=jnp.float32
        )
        dv_ref[span, :] += lax.dot_general(
            prob.astype(jnp.bfloat16), grad, across, preferred_element_type=jnp.float32
        )

    for blocks in range(1, reach + 1):
        if blocks < reach:
            pl.when(index == blocks - 1)(functools.partial(run, blocks))
        else:
            pl.when(index >= blocks - 1)(functools.partial(run, blocks))

    @pl.when(index == steps - 1)
    def _():
        half = HEAD_SIZE // 2
        odd = lax.axis_index("seq") % 2 == 1
        dk = turn_back(dk_ref[...], cos_ref[...], sin_ref[...])
        for part, grad in enumerate((dk, dv_ref[...])):
            low, high = grad[:, :half], grad[:, half:]
            own = HEAD_SIZE + half * part
            grad_ref[:, own : own + half] = jnp.where(odd, high, low).astype(jnp.bfloat16)
            own += HEAD_SIZE
            grad_ref[:, own : own + half] = jnp.where(odd, low, high).astype(jnp.bfloat16)


def block_shape(length):
    for block in (384, 256, 128):
        if length % block == 0:
            reach = min(length // block, (WIN - 1 + block - 1) // block + 1)
            return block, reach
    raise ValueError("sequence length")


def attend_specs(length, block):
    whole = pl.BlockSpec((None, length, HEAD_SIZE), lambda m, i: (m, 0, 0))
    half = pl.BlockSpec((None, length, HEAD_SIZE // 2), lambda m, i: (m, 0, 0))
    rows = pl.BlockSpec((None, block, HEAD_SIZE), lambda m, i: (m, i, 0))
    line = pl.BlockSpec((None, block, 1), lambda m, i: (m, i, 0))
    return whole, half, rows, line


def project_kernel(x_ref, w_ref, far_ref, cos_ref, sin_ref, q_ref, k_ref, v_ref):
    product = final_dot(x_ref[...], w_ref[...])
    far = final_dot(x_ref[...], far_ref[...])
    cosine, sine = cos_ref[...], sin_ref[...]
    half = HEAD_SIZE // 2
    query = product[:, :HEAD_SIZE]
    own_k, own_v = product[:, HEAD_SIZE : HEAD_SIZE + half], product[:, HEAD_SIZE + half :]
    far_k, far_v = far[:, :half], far[:, half:]
    odd = lax.axis_index("seq") % 2 == 1
    key = jnp.concatenate([jnp.where(odd, far_k, own_k), jnp.where(odd, own_k, far_k)], axis=1)
    query = rotate(query, cosine, sine, 1.0) * (1.0 / math.sqrt(HEAD_SIZE))
    q_ref[...] = query.astype(jnp.bfloat16)
    k_ref[...] = rotate(key, cosine, sine, 1.0).astype(jnp.bfloat16)
    v_ref[:, :half] = jnp.where(odd, far_v, own_v).astype(jnp.bfloat16)
    v_ref[:, half:] = jnp.where(odd, own_v, far_v).astype(jnp.bfloat16)


def project(whole, weight, far, cosine, sine):
    batches, length, width = whole.shape
    block = block_shape(length)[0]
    _, _, rows, _ = attend_specs(length, block)
    half = pl.BlockSpec((None, block, HEAD_SIZE // 2), lambda m, i: (m, i, 0))
    return pl.pallas_call(
        project_kernel,
        grid=(batches, length // block),
        in_specs=[
            pl.BlockSpec((None, block, width), lambda m, i: (m, i, 0)),
            pl.BlockSpec(weight.shape, lambda m, i: (0, 0)),
            pl.BlockSpec(far.shape, lambda m, i: (0, 0)),
            half,
            half,
        ],
        out_specs=[rows] * 3,
        out_shape=[jax.ShapeDtypeStruct((batches, length, HEAD_SIZE), jnp.bfloat16)] * 3,
        compiler_params=pltpu.CompilerParams(vmem_limit_bytes=40 * 2**20),
        cost_estimate=pl.CostEstimate(
            flops=6 * batches * length * width * HEAD_SIZE,
            bytes_accessed=2 * batches * length * width,
            transcendentals=0,
        ),
        name="project",
    )(whole, weight, far, cosine, sine)


def token_tables(tables, made):
    counts_ref, frequency_ref = tables
    cos_ref, sin_ref, low_ref = made
    batches, length, _ = cos_ref.shape
    block = block_shape(length)[0]
    for batch in range(batches):

        def step(index, carry, batch=batch):
            span = pl.ds(pl.multiple_of(index * block, 16), block)
            place = index * block + lax.broadcasted_iota(jnp.int32, (block, HEAD_SIZE // 2), 0)
            place = place.astype(jnp.float32)
            start = jnp.zeros_like(place)
            for number in range(1, DOCUMENTS):
                row = batch * (DOCUMENTS - 1) + number - 1
                count = counts_ref[row : row + 1, :]
                start = jnp.where(place >= count, count, start)
            phase_angle = (place - start) * frequency_ref[...]
            cos_ref[batch, span, :] = jnp.cos(phase_angle)
            sin_ref[batch, span, :] = jnp.sin(phase_angle)
            low = jnp.maximum(start, place - (WIN - 1))
            low_ref[batch, span, :] = low[:, :1].astype(jnp.int32)
            return carry

        lax.fori_loop(0, length // block, step, 0)


def attend(query, key, value, low_bound):
    batches, length = query.shape[:2]
    block, reach = block_shape(length)
    whole, half, rows, line = attend_specs(length, block)
    area = batches * block * block * reach * (length // block)
    return pl.pallas_call(
        functools.partial(attend_kernel, block, reach),
        grid=(batches, length // block),
        in_specs=[rows, whole, whole, line],
        out_specs=[rows, line],
        out_shape=[
            jax.ShapeDtypeStruct((batches, length, HEAD_SIZE), jnp.bfloat16),
            jax.ShapeDtypeStruct((batches, length, 1), jnp.float32),
        ],
        compiler_params=pltpu.CompilerParams(vmem_limit_bytes=40 * 2**20),
        cost_estimate=pl.CostEstimate(
            flops=4 * area * HEAD_SIZE,
            bytes_accessed=10 * batches * length * HEAD_SIZE,
            transcendentals=2 * area,
        ),
        name="attend",
    )(query, key, value, low_bound)


def attend_back(query, key, value, grad, low_bound, log_total, cosine, sine):
    batches, length = query.shape[:2]
    block, reach = block_shape(length)
    whole, half, rows, line = attend_specs(length, block)
    area = batches * block * block * reach * (length // block)
    return pl.pallas_call(
        functools.partial(attend_back_kernel, block, reach),
        grid=(batches, length // block),
        in_specs=[rows, whole, whole, rows, line, line, half, half],
        out_specs=pl.BlockSpec((None, length, 3 * HEAD_SIZE), lambda m, i: (m, 0, 0)),
        out_shape=jax.ShapeDtypeStruct((batches, length, 3 * HEAD_SIZE), jnp.bfloat16),
        scratch_shapes=[pltpu.VMEM((length, HEAD_SIZE), jnp.float32)] * 2,
        compiler_params=pltpu.CompilerParams(vmem_limit_bytes=48 * 2**20),
        cost_estimate=pl.CostEstimate(
            flops=10 * area * HEAD_SIZE,
            bytes_accessed=24 * batches * length * HEAD_SIZE,
            transcendentals=2 * area,
        ),
        name="attend_back",
    )(query, key, value, grad, low_bound, log_total, cosine, sine)


class ByHeads:
    def __init__(self, w_query, key_weight, value_weight, w_out):
        place = lax.axis_index("seq")
        count = lax.axis_size("seq")
        layers = lax.axis_size("fsdp")
        half = HEAD_SIZE // 2

        def columns(weight, width):
            return lax.dynamic_slice_in_dim(weight, place * width, width, axis=1)

        joined = jnp.concatenate(
            [columns(w_query, HEAD_SIZE), columns(key_weight, half), columns(value_weight, half)],
            axis=1,
        )
        depth = HEAD_SIZE // count
        here = QUERY_HEADS // layers
        part = w_out.reshape(here, count, depth, w_out.shape[1])
        part = lax.dynamic_index_in_dim(part, place, axis=1, keepdims=False)
        rows = joined.shape[0]
        both = jnp.concatenate([joined, part.reshape(-1, joined.shape[1])], axis=0)
        self.both = lax.all_gather(both, "fsdp", axis=0)
        self.split = rows
        self.part_shape = (QUERY_HEADS * depth, w_out.shape[1])

    def forward(self, normed, segments):
        batches, rows, width = normed.shape
        length = rows * lax.axis_size("seq")
        half = HEAD_SIZE // 2
        counts = [
            jnp.sum((segments[batch] < number).astype(jnp.float32))
            for batch in range(batches)
            for number in range(1, DOCUMENTS)
        ]
        counts += [jnp.zeros(())] * (8 - len(counts))
        counts = jnp.broadcast_to(jnp.stack(counts)[:, None], (8, half))
        counts = small_sum(counts, False, 8, "sum_counts")
        frequency = 10000.0 ** (-jnp.arange(half, dtype=jnp.float32) * 2.0 / HEAD_SIZE)
        table = jax.ShapeDtypeStruct((batches, length, half), jnp.float32)
        bound = jax.ShapeDtypeStruct((batches, length, 1), jnp.int32)
        whole, cosine, sine, low_bound = plane_gather(
            normed,
            0,
            "gather_normed",
            Job(
                None,
                tables=[counts, frequency[None]],
                spare=(token_tables, [table, table, bound]),
            ),
        )
        whole, both = lax.optimization_barrier((whole, self.both))
        self.joined = both[:, : self.split].reshape(-1, both.shape[2])
        self.out_rows = swap_parts(both[:, self.split :].reshape(self.part_shape), 0, 0)
        self.far = lax.ppermute(
            self.joined[:, HEAD_SIZE:], "seq", [(i, i ^ 1) for i in range(QUERY_HEADS)]
        )
        query, key, value = project(whole, self.joined, self.far, cosine, sine)
        attended, log_total = attend(query, key, value, low_bound)
        job = Job(
            rows_compute, weights=[self.out_rows], flops=2 * batches * length * HEAD_SIZE * width
        )
        (mixed,) = plane_scatter([attended], width, 1, "scatter_mixed", job)
        return mixed, (whole, query, key, value, low_bound, log_total, cosine, sine, attended)

    def open_back(self, grad_mixed_b, saved, side):
        attended = saved[-1]
        batches, length = attended.shape[:2]
        width = grad_mixed_b.shape[-1]
        job = Job(
            head_back_compute,
            weights=[self.out_rows],
            extras=[attended],
            outs=[(HEAD_SIZE, jnp.bfloat16)],
            side=side,
            sums=[(side[0].shape[2], side[1].shape[2]), (HEAD_SIZE, width)],
            flops=2 * batches * length * (HEAD_SIZE * width + side[0].shape[2] * side[1].shape[2]),
        )
        _, grad_att, side_sum, self.out_sum = plane_gather(
            grad_mixed_b, 2, "gather_grad_mixed", job
        )
        return grad_att, side_sum

    def middle_back(self, grad_att, saved):
        _, query, key, value, low_bound, log_total, cosine, sine, _ = saved
        grads = attend_back(query, key, value, grad_att, low_bound, log_total, cosine, sine)
        grads, self.out_own = lax.optimization_barrier((grads, scatter_rows(self.out_sum)))
        return grads

    def close_back(self, grads, saved, meanwhile):
        count = lax.axis_size("seq")
        joined = dot_rows(saved[0], grads).astype(jnp.bfloat16)
        own, far = joined[:, HEAD_SIZE : 2 * HEAD_SIZE], joined[:, 2 * HEAD_SIZE :]
        came = lax.ppermute(far, "seq", [(i, i ^ 1) for i in range(count)])
        own = (own.astype(jnp.float32) + came.astype(jnp.float32)).astype(jnp.bfloat16)
        joined = jnp.concatenate([joined[:, :HEAD_SIZE], own], axis=1)
        grads, joined, meanwhile = lax.optimization_barrier((grads, joined, meanwhile))
        self.joined_sum = joined

        parts = self.out_own.reshape(self.out_own.shape[0], count, -1).transpose(1, 0, 2)
        rows = grads.shape[0] * grads.shape[1]
        width = self.joined.shape[0]
        job = Job(
            back_compute,
            weights=[self.joined, self.far],
            spread=parts,
            flops=6 * rows * HEAD_SIZE * width,
        )
        grad_normed, self.placed = plane_scatter([grads], width, 3, "scatter_grad_normed", job)
        return grad_normed, meanwhile

    def weight_grads(self, gains):
        half = HEAD_SIZE // 2
        joined = scatter_rows(self.joined_sum).astype(jnp.float32)
        gains = small_sum(jnp.pad(gains, ((0, 4), (0, 0))), True, 9, "sum_gains")
        return (
            joined[:, :HEAD_SIZE],
            joined[:, HEAD_SIZE : HEAD_SIZE + half],
            joined[:, HEAD_SIZE + half :],
            self.placed.astype(jnp.float32).reshape(-1, self.placed.shape[2]),
            gains,
        )


class ByTokens:
    def __init__(self, w_query, key_weight, value_weight, w_out):
        self.weights = fetch_attention(w_query, key_weight, value_weight, w_out)
        self.records = []

    def forward(self, normed, segments):
        seg_whole = lax.all_gather(segments, "seq", axis=1, tiled=True)
        done = [self.forward_one(*pair) for pair in zip(normed, seg_whole)]
        return jnp.stack([mixed for mixed, _ in done]), [saved for _, saved in done]

    def forward_one(self, normed, seg_whole):
        token_rows = normed.shape[0]
        halo_count = (WIN - 2 + token_rows) // token_rows
        w_query, key_weight, value_weight, w_out = self.weights
        seq_place = lax.axis_index("seq")
        seg_here = lax.dynamic_slice_in_dim(seg_whole, seq_place * token_rows, token_rows)
        position = jnp.arange(seg_whole.shape[0], dtype=jnp.int32) - doc_starts(seg_whole)
        position = lax.dynamic_slice_in_dim(position, seq_place * token_rows, token_rows)
        cosine, sine = (table[:, None] for table in angles(position, HEAD_SIZE))
        query = rotate(
            final_dot(normed, w_query).reshape(token_rows, QUERY_HEADS, HEAD_SIZE),
            cosine,
            sine,
            1.0,
        )
        query = (query * (1.0 / math.sqrt(HEAD_SIZE))).astype(jnp.bfloat16)
        key = rotate(
            final_dot(normed, key_weight).reshape(token_rows, KEY_VALUE_HEADS, HEAD_SIZE),
            cosine,
            sine,
            1.0,
        ).astype(jnp.bfloat16)
        value = final_dot(normed, value_weight).reshape(token_rows, KEY_VALUE_HEADS, HEAD_SIZE)
        pair = key_window(jnp.stack([key, value.astype(jnp.bfloat16)]), halo_count)
        allowed = window_mask(seg_here, seg_whole, seq_place, token_rows, halo_count)
        query = query.reshape(token_rows, KEY_VALUE_HEADS, -1, HEAD_SIZE)
        score = jnp.einsum("qhgd,khd->hgqk", query, pair[0], preferred_element_type=jnp.float32)
        capped = jnp.where(allowed, CAP * jnp.tanh(score / CAP), -jnp.inf)
        peak = jnp.max(capped, axis=-1, keepdims=True)
        power = jnp.exp(capped - peak)
        total = jnp.sum(power, axis=-1, keepdims=True)
        attended = jnp.einsum(
            "hgqk,khd->qhgd",
            (power / total).astype(jnp.bfloat16),
            pair[1],
            preferred_element_type=jnp.float32,
        )
        attended = attended.reshape(token_rows, QUERY_HEADS * HEAD_SIZE).astype(jnp.bfloat16)
        mixed = final_dot(attended, w_out)
        log_total = peak + jnp.log(total)
        return mixed, (normed, query, pair, allowed, log_total, cosine, sine, attended)

    def open_back(self, grad_mixed_b, saved, side):
        return grad_mixed_b, dot_rows(*side)

    def middle_back(self, grad_mixed_b, saved):
        return grad_mixed_b

    def close_back(self, grad_mixed_b, saved, meanwhile):
        grads = [self.backward_one(*pair) for pair in zip(grad_mixed_b, saved)]
        return jnp.stack(grads), meanwhile

    def backward_one(self, grad_mixed_b, saved):
        normed, query, pair, allowed, log_total, cosine, sine, attended = saved
        token_rows = normed.shape[0]
        halo_count = (WIN - 2 + token_rows) // token_rows
        w_query, key_weight, value_weight, w_out = self.weights
        grad_att = dot_back(grad_mixed_b, w_out).astype(jnp.bfloat16)
        grad_att = grad_att.reshape(token_rows, KEY_VALUE_HEADS, -1, HEAD_SIZE)
        score = jnp.einsum("qhgd,khd->hgqk", query, pair[0], preferred_element_type=jnp.float32)
        bent = jnp.tanh(score / CAP)
        prob = jnp.exp(jnp.where(allowed, CAP * bent, -jnp.inf) - log_total)
        grad_prob = jnp.einsum(
            "qhgd,khd->hgqk", grad_att, pair[1], preferred_element_type=jnp.float32
        )
        delta = jnp.sum(prob * grad_prob, axis=-1, keepdims=True)
        grad_score = (prob * (grad_prob - delta) * (1.0 - bent * bent)).astype(jnp.bfloat16)
        dq = jnp.einsum("hgqk,khd->qhgd", grad_score, pair[0], preferred_element_type=jnp.float32)
        dk = jnp.einsum("hgqk,qhgd->khd", grad_score, query, preferred_element_type=jnp.float32)
        dv = jnp.einsum(
            "hgqk,qhgd->khd", prob.astype(jnp.bfloat16), grad_att, preferred_element_type=jnp.float32
        )
        paired = window_grads(jnp.stack([dk, dv]), halo_count, token_rows)
        dq = rotate(
            dq.reshape(token_rows, QUERY_HEADS, HEAD_SIZE) * (1.0 / math.sqrt(HEAD_SIZE)),
            cosine,
            sine,
            -1.0,
        )
        dq = dq.reshape(token_rows, -1).astype(jnp.bfloat16)
        dk = rotate(paired[0], cosine, sine, -1.0).reshape(token_rows, -1).astype(jnp.bfloat16)
        dv = paired[1].reshape(token_rows, -1).astype(jnp.bfloat16)
        self.records.append((normed, dq, dk, dv, attended, grad_mixed_b))
        return dot_back(dq, w_query) + dot_back(dk, key_weight) + dot_back(dv, value_weight)

    def weight_grads(self, gains):
        normed, dq, dk, dv, attended, grad_mixed_b = (
            jnp.concatenate(parts, axis=0) for parts in zip(*self.records)
        )
        normed = lax.all_gather(normed, "seq", axis=0, tiled=True)
        attended = lax.all_gather(attended, "seq", axis=0, tiled=True)
        sums = []
        for rows, grads in ((normed, dq), (normed, dk), (normed, dv), (attended, grad_mixed_b)):
            column_sum = dot_rows(rows, swap_parts(grads, 1, 0)).astype(jnp.bfloat16)
            owned = lax.psum_scatter(column_sum, "fsdp", scatter_dimension=0, tiled=True)
            sums.append(owned.astype(jnp.float32))
        return tuple(sums) + (lax.psum(gains, ("seq", "fsdp")),)


class FeedForward:
    def __init__(self, w_gate, w_up, w_down, by_kernel):
        place = lax.axis_index("seq")
        count = lax.axis_size("seq")
        self.by_kernel = by_kernel
        self.run = w_gate.shape[1] // (count * count)

        def columns(weight):
            parts = [
                lax.dynamic_slice_in_dim(
                    weight, (t * count + place) * self.run, self.run, axis=1
                )
                for t in range(count)
            ]
            return jnp.concatenate(parts, axis=1)

        here = w_down.shape[0] // (count * self.run)
        part = w_down.reshape(here, count, self.run, w_down.shape[1])
        part = lax.dynamic_index_in_dim(part, place, axis=1, keepdims=False)
        self.gate = gather_rows(columns(w_gate))
        self.up = gather_rows(columns(w_up))
        self.down = gather_rows(part.reshape(here * self.run, -1))

    def forward(self, ffn_in):
        hidden_width, width = self.down.shape
        if self.by_kernel:
            rows = ffn_in.shape[0] * ffn_in.shape[1] * lax.axis_size("seq")
            job = Job(
                hidden_compute,
                weights=[self.gate, self.up],
                outs=[(hidden_width, jnp.bfloat16)] * 3,
                flops=4 * rows * width * hidden_width,
            )
            whole, gate_proj, up_proj, hidden = plane_gather(ffn_in, 4, "gather_ffn_in", job)
            job = Job(
                rows_compute, weights=[self.down], flops=2 * rows * width * hidden_width
            )
            (down_proj,) = plane_scatter([hidden], width, 5, "scatter_down", job)
        else:
            whole = lax.all_gather(ffn_in, "seq", axis=1, tiled=True)
            gate_proj = final_dot(whole, self.gate)
            up_proj = final_dot(whole, self.up)
            hidden = geglu(gate_proj, up_proj).astype(jnp.bfloat16)
            down_proj = lax.psum_scatter(
                final_dot(hidden, self.down).astype(jnp.bfloat16),
                "seq",
                scatter_dimension=1,
                tiled=True,
            ).astype(jnp.float32)
        return down_proj, (whole, gate_proj, up_proj, hidden)

    def backward(self, grad_down_b, saved):
        whole, gate_proj, up_proj, hidden = saved
        hidden_width, width = self.down.shape
        if self.by_kernel:
            rows = whole.shape[0] * whole.shape[1]
            job = Job(
                hidden_back_compute,
                weights=[self.down],
                extras=[gate_proj, up_proj, hidden],
                outs=[(hidden_width, jnp.bfloat16)] * 2,
                sums=[(hidden_width, width)],
                flops=4 * rows * width * hidden_width,
            )
            _, grad_gate, grad_up, self.down_sum = plane_gather(
                grad_down_b, 6, "gather_grad_down", job
            )
            job = Job(
                back_compute,
                weights=[self.gate, self.up],
                side=[whole, grad_gate],
                sums=[(width, hidden_width)],
                flops=6 * rows * width * hidden_width,
            )
            grad_ffn_in, self.gate_sum = plane_scatter(
                [grad_gate, grad_up], width, 7, "scatter_grad_ffn_in", job
            )
        else:
            grad_whole = lax.all_gather(grad_down_b, "seq", axis=1, tiled=True)
            grad_hidden = dot_back(grad_whole, self.down)
            _, pullback = jax.vjp(geglu, gate_proj, up_proj)
            grad_gate, grad_up = (g.astype(jnp.bfloat16) for g in pullback(grad_hidden))
            partial = dot_back(grad_gate, self.gate) + dot_back(grad_up, self.up)
            grad_ffn_in = lax.psum_scatter(
                partial.astype(jnp.bfloat16), "seq", scatter_dimension=1, tiled=True
            ).astype(jnp.float32)
            self.down_sum = dot_rows(hidden, grad_whole)
            self.gate_sum = dot_rows(whole, grad_gate)
        self.up_side = (whole, grad_up)
        return grad_ffn_in

    def own_columns(self, own):
        return swap_parts(own, 1, 1).astype(jnp.float32)

    def own_rows(self, own):
        here = own.shape[0] // self.run
        moved = swap_parts(own, 1, 0)
        moved = moved.reshape(-1, here, self.run, moved.shape[1]).transpose(1, 0, 2, 3)
        return moved.astype(jnp.float32).reshape(-1, moved.shape[3])


def on_device(
    tokens,
    segments,
    w_query,
    key_weight,
    value_weight,
    w_out,
    w_gate,
    w_up,
    w_down,
    gain_attn_in,
    gain_attn_out,
    gain_ffn_in,
    gain_ffn_out,
    cotangent,
):
    by_kernel = (
        lax.axis_size("seq") == QUERY_HEADS
        and tokens.shape[0] == 2
        and QUERY_HEADS % lax.axis_size("fsdp") == 0
    )
    attention = (ByHeads if by_kernel else ByTokens)(w_query, key_weight, value_weight, w_out)
    ffn = FeedForward(w_gate, w_up, w_down, by_kernel)

    stream = tokens[:, 0].astype(jnp.float32)
    normed = rms_gain(stream, gain_attn_in).astype(jnp.bfloat16)
    mixed, attention_saved = attention.forward(normed, segments[:, 0])
    middle = stream + rms_gain(mixed, gain_attn_out)
    ffn_in = rms_gain(middle, gain_ffn_in).astype(jnp.bfloat16)
    down_proj, ffn_saved = ffn.forward(ffn_in)
    result = middle + rms_gain(down_proj, gain_ffn_out)

    grad_result = cotangent[:, 0].astype(jnp.float32)
    _, pullback = jax.vjp(rms_gain, down_proj, gain_ffn_out)
    grad_down, grad_gain_four = pullback(grad_result)
    grad_ffn_in = ffn.backward(grad_down.astype(jnp.bfloat16), ffn_saved)
    _, pullback = jax.vjp(rms_gain, middle, gain_ffn_in)
    grad_middle, grad_gain_three = pullback(grad_ffn_in)
    grad_middle = grad_result + grad_middle
    _, pullback = jax.vjp(rms_gain, mixed, gain_attn_out)
    grad_mixed, grad_gain_two = pullback(grad_middle)
    grad_mixed, w_down_grad = lax.optimization_barrier(
        (grad_mixed.astype(jnp.bfloat16), scatter_rows(ffn.down_sum))
    )
    grad_att, up_sum = attention.open_back(grad_mixed, attention_saved, ffn.up_side)
    grad_att, w_gate_grad = lax.optimization_barrier((grad_att, scatter_rows(ffn.gate_sum)))
    w_down_grad = ffn.own_rows(w_down_grad)
    grads = attention.middle_back(grad_att, attention_saved)
    grads, w_gate_grad, w_down_grad = lax.optimization_barrier((grads, w_gate_grad, w_down_grad))
    grad_normed, w_gate_grad = attention.close_back(
        grads, attention_saved, ffn.own_columns(w_gate_grad)
    )
    _, pullback = jax.vjp(rms_gain, stream, gain_attn_in)
    grad_stream, grad_gain_one = pullback(grad_normed)
    grad_stream = grad_middle + grad_stream

    w_up_grad = ffn.own_columns(scatter_rows(up_sum))
    gains = jnp.stack([grad_gain_one, grad_gain_two, grad_gain_three, grad_gain_four])
    query_grad, key_grad, value_grad, out_grad, gains = attention.weight_grads(gains)
    return (
        result.astype(jnp.bfloat16)[:, None],
        grad_stream[:, None],
        query_grad,
        key_grad,
        value_grad,
        out_grad,
        w_gate_grad,
        w_up_grad,
        w_down_grad,
        gains[0],
        gains[1],
        gains[2],
        gains[3],
    )


def solution(mesh):
    in_specs = (
        P(None, "fsdp", "seq", None),
        P(None, "fsdp", "seq"),
        P("fsdp", None),
        P("fsdp", None),
        P("fsdp", None),
        P("fsdp", None),
        P("fsdp", None),
        P("fsdp", None),
        P("fsdp", None),
        P(),
        P(),
        P(),
        P(),
        P(None, "fsdp", "seq", None),
    )
    out_specs = (
        P(None, "fsdp", "seq", None),
        P(None, "fsdp", "seq", None),
        P("fsdp", "seq"),
        P("fsdp", "seq"),
        P("fsdp", "seq"),
        P("fsdp", "seq"),
        P("fsdp", "seq"),
        P("fsdp", "seq"),
        P("fsdp", "seq"),
        P(),
        P(),
        P(),
        P(),
    )
    return jax.shard_map(
        on_device, mesh=mesh, in_specs=in_specs, out_specs=out_specs, check_vma=False
    )
```

```python
import functools
import math

import jax
import jax.numpy as jnp
from jax import lax
from jax.experimental import pallas as pl
from jax.experimental.pallas import tpu as pltpu
from jax.sharding import PartitionSpec as P

QUERY_HEADS = 8
KEY_VALUE_HEADS = 4
HEAD_SIZE = 256
CAP = 50
WIN = 1024
DOCUMENTS = 4
VMEM_LIMIT = 60 * 2**20
SPAN_BYTES = 270_000_000


epsilon = 1e-06


def shifted(value, axis, steps):
    count = lax.axis_size(axis)
    initial, last = (max(0, -steps), min(count, count - steps))
    return lax.ppermute(value, axis, [(source, source + steps) for source in range(initial, last)])


def rms_gain(stream, gain):
    return stream * lax.rsqrt(jnp.mean(stream * stream, axis=-1, keepdims=True) + epsilon) * gain


def geglu(gate_proj, up_proj):
    return jax.nn.gelu(gate_proj, approximate=True) * up_proj


def angles(position, size):
    frequency = 10000.0 ** (-jnp.arange(size // 2, dtype=jnp.float32) * 2.0 / size)
    phase_angle = position.astype(jnp.float32)[..., None] * frequency
    return (jnp.cos(phase_angle), jnp.sin(phase_angle))


def rotate(value_rows, cosine_table, sine_table, direction):
    half_size = value_rows.shape[-1] // 2
    first_half = value_rows[..., :half_size]
    second = value_rows[..., half_size:]
    return jnp.concatenate(
        [
            first_half * cosine_table - direction * second * sine_table,
            second * cosine_table + direction * first_half * sine_table,
        ],
        axis=-1,
    )


def doc_starts(segment):
    starts = jnp.zeros_like(segment)
    for number in range(1, DOCUMENTS):
        count = jnp.sum((segment < number).astype(jnp.int32), axis=-1, keepdims=True)
        starts = jnp.where(segment >= number, count, starts)
    return starts


def final_dot(left_side, right_side):
    return jnp.dot(left_side, right_side, preferred_element_type=jnp.float32)


def dot_back(left_side, right_side):
    contract = (((left_side.ndim - 1,), (1,)), ((), ()))
    return lax.dot_general(left_side, right_side, contract, preferred_element_type=jnp.float32)


def dot_rows(left_side, right_side):
    left_side = left_side.reshape(-1, left_side.shape[-1])
    right_side = right_side.reshape(-1, right_side.shape[-1])
    return lax.dot_general(
        left_side, right_side, (((0,), (0,)), ((), ())), preferred_element_type=jnp.float32
    )


def fetch_attention(w_query, key_weight, value_weight, w_out):
    return (
        lax.all_gather(w_query, "fsdp", axis=0, tiled=True),
        lax.all_gather(key_weight, "fsdp", axis=0, tiled=True),
        lax.all_gather(value_weight, "fsdp", axis=0, tiled=True),
        lax.all_gather(w_out, "fsdp", axis=0, tiled=True),
    )


def key_window(kv_pair, halo_count):
    arrived = [shifted(kv_pair, "seq", offset) for offset in range(halo_count, 0, -1)]
    return jnp.concatenate(arrived + [kv_pair], axis=1)


def window_grads(paired_gradient, halo_count, token_rows):
    summed = paired_gradient[:, halo_count * token_rows :]
    for offset in range(1, halo_count + 1):
        begin = (halo_count - offset) * token_rows
        summed = summed + shifted(
            paired_gradient[:, begin : begin + token_rows].astype(jnp.bfloat16), "seq", -offset
        ).astype(jnp.float32)
    return summed


def window_mask(seg_here, seg_whole, seq_place, token_rows, halo_count):
    padded = jnp.concatenate([jnp.full((halo_count * token_rows,), -1, jnp.int32), seg_whole])
    key_seg = lax.dynamic_slice_in_dim(
        padded, seq_place * token_rows, (halo_count + 1) * token_rows
    )
    query_pos = seq_place * token_rows + jnp.arange(token_rows, dtype=jnp.int32)
    key_pos = (
        seq_place * token_rows
        - halo_count * token_rows
        + jnp.arange((halo_count + 1) * token_rows, dtype=jnp.int32)
    )
    distance = query_pos[:, None] - key_pos[None, :]
    return (seg_here[:, None] == key_seg[None, :]) & (distance >= 0) & (distance < WIN)


def gather_rows(rows):
    return lax.all_gather(rows, "fsdp", axis=0, tiled=True)


def scatter_rows(partial):
    return lax.psum_scatter(
        partial.astype(jnp.bfloat16), "fsdp", scatter_dimension=0, tiled=True
    )


def swap_parts(value, split_axis, concat_axis):
    return lax.all_to_all(
        value, "seq", split_axis=split_axis, concat_axis=concat_axis, tiled=True
    )


MESH = pl.DeviceIdType.MESH


def plane_places():
    me = lax.axis_index("seq")
    other_core = me + 1 - 2 * (me % 2)
    along_x = me + 2 - 4 * ((me // 2) % 2)
    along_y = me + 4 - 8 * (me // 4)
    return me, other_core, along_x, along_y


def greet(neighbours, *others):
    barrier = pltpu.get_barrier_semaphore()
    for neighbour in neighbours:
        pl.semaphore_signal(barrier, inc=1, device_id={"seq": neighbour}, device_id_type=MESH)
    count = len(neighbours)
    for other in others:
        count = count + other.greet(barrier)
    pl.semaphore_wait(barrier, count)


class Spread:
    def __init__(self, parts_ref, placed_ref, send, recv):
        self.parts, self.placed, self.send, self.recv = parts_ref, placed_ref, send, recv
        self.me, self.layer = lax.axis_index("seq"), lax.axis_index("fsdp")
        layers = lax.axis_size("fsdp")
        shared = lax.axis_size("seq") // layers
        self.owner = self.me // shared
        self.slot = (self.me - self.owner * shared) * layers + self.layer
        self.targets = [(place, self.owner) for place in range(shared * layers)]
        self.sources = [
            (self.layer * shared + part, from_layer)
            for part in range(shared)
            for from_layer in range(layers)
        ]

    def turn(self):
        pass

    def away(self, device):
        return (device[0] != self.me) | (device[1] != self.layer)

    def greet(self, barrier):
        for place, layer in self.targets + self.sources:

            @pl.when(self.away((place, layer)))
            def _(place=place, layer=layer):
                device = {"seq": place, "fsdp": layer}
                pl.semaphore_signal(barrier, inc=1, device_id=device, device_id_type=MESH)

        return 2 * len(self.targets) - 2 * (self.owner == self.layer).astype(jnp.int32)

    def copy(self, index, slot, device):
        return pltpu.make_async_remote_copy(
            src_ref=self.parts.at[index],
            dst_ref=self.placed.at[slot],
            send_sem=self.send.at[index],
            recv_sem=self.recv.at[slot],
            device_id={"seq": device[0], "fsdp": device[1]},
            device_id_type=MESH,
        )

    def own(self):
        source, target = self.parts.at[self.me], self.placed.at[self.slot]
        return pltpu.make_async_copy(source, target, self.send.at[len(self.targets)])

    def begin(self):
        for index, device in enumerate(self.targets):
            pl.when(self.away(device))(self.copy(index, self.slot, device).start)
        pl.when(self.owner == self.layer)(self.own().start)

    def end(self):
        for index, device in enumerate(self.targets):
            pl.when(self.away(device))(self.copy(index, self.slot, device).wait_send)
        for index, device in enumerate(self.sources):
            pl.when(self.away(device))(self.copy(0, index, device).wait_recv)
        pl.when(self.owner == self.layer)(self.own().wait)


class SmallSum:
    def __init__(self, over_layers, value_ref, out_ref, *scratch):
        self.over_layers, self.value, self.out = over_layers, value_ref, out_ref
        self.plane_buf, self.layer_buf, self.plane_sems, self.layer_sems = scratch
        self.me, *neighbours = plane_places()
        steps = [neighbour - self.me for neighbour in neighbours]
        self.peers = [
            self.me + sum(step for bit, step in enumerate(steps) if (index >> bit) % 2)
            for index in range(1, 8)
        ]
        self.layer, self.layers = lax.axis_index("fsdp"), lax.axis_size("fsdp")
        hops = range(1, self.layers) if over_layers else []
        self.others = [lax.rem(self.layer + hop, self.layers) for hop in hops]

    @staticmethod
    def scratch(value):
        layers = lax.axis_size("fsdp")
        return [
            pltpu.VMEM((8,) + value.shape, value.dtype),
            pltpu.VMEM((layers,) + value.shape, value.dtype),
            pltpu.SemaphoreType.DMA((2, 7)),
            pltpu.SemaphoreType.DMA((2, layers)),
        ]

    def greet(self, barrier):
        farther = [peer for index, peer in enumerate(self.peers) if index not in (0, 1, 3)]
        for peer in farther:
            pl.semaphore_signal(barrier, inc=1, device_id={"seq": peer}, device_id_type=MESH)
        for other in self.others:
            pl.semaphore_signal(barrier, inc=1, device_id={"fsdp": other}, device_id_type=MESH)
        return len(farther) + len(self.others)

    def copy(self, buf, sems, slot, index, device):
        return pltpu.make_async_remote_copy(
            src_ref=buf.at[slot],
            dst_ref=buf.at[slot],
            send_sem=sems.at[0, index],
            recv_sem=sems.at[1, index],
            device_id=device,
            device_id_type=MESH,
        )

    def plane_copies(self):
        return [
            self.copy(self.plane_buf, self.plane_sems, self.me, index, {"seq": peer})
            for index, peer in enumerate(self.peers)
        ]

    def layer_copies(self):
        return [
            self.copy(self.layer_buf, self.layer_sems, self.layer, index, {"fsdp": other})
            for index, other in enumerate(self.others)
        ]

    def begin(self):
        self.plane_buf[self.me] = self.value[...]
        for copy in self.plane_copies():
            copy.start()

    def turn(self):
        for copy in self.plane_copies():
            copy.wait_recv()
        total = self.plane_buf[0]
        for index in range(1, 8):
            total = total + self.plane_buf[index]
        if not self.over_layers:
            self.out[...] = total
            return
        self.layer_buf[self.layer] = total
        for copy in self.layer_copies():
            copy.start()

    def end(self):
        for copy in self.layer_copies():
            copy.wait_recv()
        if self.over_layers:
            total = self.layer_buf[0]
            for index in range(1, self.layers):
                total = total + self.layer_buf[index]
            self.out[...] = total
        for copy in self.plane_copies() + self.layer_copies():
            copy.wait_send()


BRAID = 384


def braid_width(arrays):
    return sum(array.shape[-1] for array in arrays)


def braided(arrays):
    return len(arrays) == 2 and arrays[0].shape[-1] == arrays[1].shape[-1]


def copies_into(sources, target, sem):
    if not braided(sources):
        copies, at = [], 0
        for i, source in enumerate(sources):
            width = source.shape[-1]
            copies.append(
                pltpu.make_async_copy(source, target.at[:, pl.ds(at, width)], sem.at[i])
            )
            at += width
        return copies
    groups = sources[0].shape[-1] // BRAID
    copies = []
    for group in range(groups):
        for part, source in enumerate(sources):
            at = group * len(sources) + part
            copies.append(
                pltpu.make_async_copy(
                    source.at[:, pl.ds(group * BRAID, BRAID)],
                    target.at[:, pl.ds(at * BRAID, BRAID)],
                    sem.at[at],
                )
            )
    return copies


def copy_count(arrays):
    return braid_width(arrays) // BRAID if braided(arrays) else len(arrays)


def unit_rows(place, rows):
    return pl.ds(pl.multiple_of((place // 2) * (2 * rows), 16), 2 * rows)


class Job:
    def __init__(
        self,
        compute,
        weights=(),
        extras=(),
        outs=(),
        sums=(),
        side=(),
        tables=(),
        spare=None,
        spread=None,
        small=None,
        flops=0,
    ):
        self.spread, self.small = spread, small
        self.compute, self.flops, self.spare = compute, flops, spare
        self.tables = list(tables)
        self.weights, self.extras, self.outs = list(weights), list(extras), list(outs)
        self.sums, self.side = list(sums), list(side)


def gather_kernel(job, rows, *refs):
    refs = list(refs)
    take = lambda n: [refs.pop(0) for _ in range(n)]
    (local_ref,) = take(1)
    weight_refs, extra_refs, side_refs = (
        take(len(job.weights)),
        take(len(job.extras)),
        take(len(job.side)),
    )
    table_refs, count_refs = take(len(job.tables)), take(1 if job.small is not None else 0)
    (whole_ref,), out_refs, final_refs = take(1), take(len(job.outs)), take(len(job.sums))
    made_refs = take(len(job.spare[1]) if job.spare else 0)
    send_sem, recv_sem, own_sem, x_buf = take(4)
    weight_bufs = take(1 if job.weights else 0)
    extra_bufs, side_bufs, out_bufs = (
        take(len(job.extras)),
        take(len(job.side)),
        take(len(job.outs)),
    )
    sum_bufs, final_bufs = take(len(job.sums)), take(len(job.sums))
    weight_sem, load_sem, side_sem, store_sem, final_sem = take(5)
    if count_refs:
        summed = take(1)[0]
        small = SmallSum(False, count_refs[0], summed, *take(4))
        table_refs = [summed] + table_refs

    me, other_core, along_x, along_y = plane_places()
    across = along_x + along_y - me
    core = me % 2

    def piece(batch, place):
        return whole_ref.at[batch, pl.ds(pl.multiple_of(place * rows, 16), rows)]

    def transfer(slot, source, batch, place, target):
        return pltpu.make_async_remote_copy(
            src_ref=source,
            dst_ref=piece(batch, place),
            send_sem=send_sem.at[slot],
            recv_sem=recv_sem.at[slot],
            device_id={"seq": target},
            device_id_type=MESH,
        )

    def forward(slot, batch, place, target):
        return transfer(slot, piece(batch, place), batch, place, target)

    moves = [
        transfer(0, local_ref.at[0], 0, me, along_x),
        transfer(1, local_ref.at[1], 1, me, along_x),
        transfer(2, local_ref.at[1], 1, me, along_y),
        transfer(3, local_ref.at[0], 0, me, along_y),
        forward(4, 0, along_x, along_y),
        forward(5, 1, along_y, along_x),
        transfer(6, local_ref.at[0], 0, me, other_core),
        transfer(7, local_ref.at[1], 1, me, other_core),
        forward(8, 0, along_x, other_core),
        forward(9, 1, along_x, other_core),
        forward(10, 1, along_y, other_core),
        forward(11, 0, along_y, other_core),
        forward(12, 0, across, other_core),
        forward(13, 1, across, other_core),
    ]
    greet((other_core, along_x, along_y), *([small] if count_refs else []))
    if count_refs:
        small.begin()
    for slot in (0, 2, 1, 3, 6, 7):
        moves[slot].start()
    owns = [
        pltpu.make_async_copy(local_ref.at[batch], piece(batch, me), own_sem.at[batch])
        for batch in range(2)
    ]
    for own in owns:
        own.start()
    fetches = copies_into(weight_refs, weight_bufs[0], weight_sem) if job.weights else []
    for fetch in fetches:
        fetch.start()
    if count_refs:
        small.turn()
    if job.spare:
        job.spare[0](table_refs, made_refs)
    stores = []

    order = [
        (me, 0),
        (me, 1),
        (along_x, 0),
        (along_y, 1),
        (along_x, 1),
        (along_y, 0),
        (across, 0),
        (across, 1),
    ]

    def extra_loads(step):
        place, batch = order[step]
        span = unit_rows(place, rows)
        return [
            pltpu.make_async_copy(ref.at[batch, span], buf.at[step % 2], load_sem.at[2 + i, step % 2])
            for i, (ref, buf) in enumerate(zip(extra_refs, extra_bufs))
        ]

    for load in extra_loads(0):
        load.start()

    def own_half(which):
        return x_buf.at[pl.ds(pl.multiple_of(which * rows, 16), rows)]

    def unit(place, batch, own=False):
        if job.compute is None:
            return
        span = unit_rows(place, rows)
        if own:
            loads = [
                pltpu.make_async_copy(local_ref.at[batch], own_half(core), load_sem.at[0, 0]),
                pltpu.make_async_copy(
                    piece(batch, other_core), own_half(1 - core), load_sem.at[1, 0]
                ),
            ]
        else:
            loads = [pltpu.make_async_copy(whole_ref.at[batch, span], x_buf, load_sem.at[0, 0])]
        step = len(stores)
        for load in loads:
            load.start()
        loads += extra_loads(step)
        if step < 7:
            for load in extra_loads(step + 1):
                load.start()
        if step == 0:
            for fetch in fetches:
                fetch.wait()
        if step >= 2:
            for store in stores[step - 2]:
                store.wait()
        for load in loads:
            load.wait()
        slot = step % 2
        extras = [buf.at[slot] for buf in extra_bufs]
        outs = [buf.at[slot] for buf in out_bufs]
        job.compute(x_buf, weight_bufs, extras, outs, sum_bufs, step == 0)
        stores.append(
            [
                pltpu.make_async_copy(buf.at[slot], ref.at[batch, span], store_sem.at[slot, i])
                for i, (ref, buf) in enumerate(zip(out_refs, out_bufs))
            ]
        )
        for store in stores[-1]:
            store.start()

    side = Side(rows, side_refs, side_bufs, sum_bufs, side_sem)

    for batch in range(2):
        moves[6 + batch].wait_recv()
        unit(me, batch, own=True)
        side.run(1)
    moves[0].wait_recv()
    moves[4].start()
    moves[8].start()
    moves[2].wait_recv()
    moves[5].start()
    moves[10].start()
    side.run(2)
    moves[8].wait_recv()
    unit(along_x, 0)
    moves[10].wait_recv()
    unit(along_y, 1)
    side.run(1)
    moves[1].wait_recv()
    moves[9].start()
    moves[3].wait_recv()
    moves[11].start()
    side.run(3)
    moves[9].wait_recv()
    unit(along_x, 1)
    moves[11].wait_recv()
    unit(along_y, 0)
    early = 1 if job.side else 0
    finish_sums(sum_bufs[:early], final_bufs[:early], final_refs[:early], final_sem)
    moves[4].wait_recv()
    moves[12].start()
    moves[5].wait_recv()
    moves[13].start()
    moves[12].wait_recv()
    unit(across, 0)
    moves[13].wait_recv()
    unit(across, 1)
    finish_sums(sum_bufs[early:], final_bufs[early:], final_refs[early:], final_sem)
    for move in moves:
        move.wait_send()
    for own in owns:
        own.wait()
    if count_refs:
        small.end()
    for group in stores[-2:]:
        for store in group:
            store.wait()


class Side:
    def __init__(self, rows, refs, bufs, sums, sem):
        self.rows, self.refs, self.bufs, self.sums, self.sem = rows, refs, bufs, sums, sem
        self.block = 0
        self.start()

    def copies(self):
        span = pl.ds((self.block % 4) * 2 * self.rows, 2 * self.rows)
        return [
            pltpu.make_async_copy(ref.at[self.block // 4, span], buf, self.sem.at[i])
            for i, (ref, buf) in enumerate(zip(self.refs, self.bufs))
        ]

    def start(self):
        if self.refs and self.block < 8:
            for copy in self.copies():
                copy.start()

    def run(self, count):
        for _ in range(count if self.refs else 0):
            for copy in self.copies():
                copy.wait()
            add_outer(self.bufs[0], self.bufs[1], self.sums[0], self.block == 0)
            self.block += 1
            self.start()


def finish_sums(sum_bufs, final_bufs, final_refs, sem):
    for i, (total, buf, ref) in enumerate(zip(sum_bufs, final_bufs, final_refs)):
        copies = []
        size = buf.shape[1]
        for block in range(total.shape[0] // size):
            slot = block % 2
            span = pl.ds(block * size, size)
            if block >= 2:
                copies[block - 2].wait()
            buf[slot] = total[span, :].astype(buf.dtype)
            copies.append(pltpu.make_async_copy(buf.at[slot], ref.at[span], sem.at[i, slot]))
            copies[-1].start()
        for copy in copies[-2:]:
            copy.wait()


def plane_gather(local, ident, name, job=None):
    job = job or Job(None)
    batches, rows, width = local.shape
    length = rows * lax.axis_size("seq")
    semaphores = pltpu.SemaphoreType.DMA
    scratch = [semaphores((14,)), semaphores((14,)), semaphores((2,))]
    scratch += [pltpu.VMEM((2 * rows if job.compute else 8, width), local.dtype)]
    if job.weights:
        depth = job.weights[0].shape[0]
        scratch += [pltpu.VMEM((depth, braid_width(job.weights)), job.weights[0].dtype)]
    scratch += [pltpu.VMEM((2, 2 * rows, array.shape[2]), array.dtype) for array in job.extras]
    scratch += [pltpu.VMEM((2 * rows, array.shape[2]), array.dtype) for array in job.side]
    scratch += [pltpu.VMEM((2, 2 * rows, wide), kind) for wide, kind in job.outs]
    scratch += [pltpu.VMEM(shape, jnp.float32) for shape in job.sums]
    scratch += [pltpu.VMEM((2, HEAD_SIZE // 2, shape[1]), jnp.bfloat16) for shape in job.sums]
    scratch += [
        semaphores((copy_count(job.weights) if job.weights else 1,)),
        semaphores((2 + len(job.extras), 2)),
        semaphores((max(1, len(job.side)),)),
        semaphores((2, max(1, len(job.outs)))),
        semaphores((max(1, len(job.sums)), 2)),
    ]
    any_space = pl.BlockSpec(memory_space=pl.ANY)
    out_shape = [jax.ShapeDtypeStruct((batches, length, width), local.dtype)]
    out_shape += [jax.ShapeDtypeStruct((batches, length, wide), kind) for wide, kind in job.outs]
    out_shape += [jax.ShapeDtypeStruct(shape, jnp.bfloat16) for shape in job.sums]
    inputs = [local, *job.weights, *job.extras, *job.side]
    in_specs = [any_space] * len(inputs)
    in_specs += [pl.BlockSpec(memory_space=pltpu.VMEM)] * len(job.tables)
    inputs += job.tables
    if job.small is not None:
        inputs.append(job.small)
        in_specs.append(pl.BlockSpec(memory_space=pltpu.VMEM))
        scratch += [pltpu.VMEM(job.small.shape, job.small.dtype)] + SmallSum.scratch(job.small)
    out_specs = [any_space] * len(out_shape)
    if job.spare:
        out_shape += job.spare[1]
        out_specs += [pl.BlockSpec(memory_space=pltpu.VMEM)] * len(job.spare[1])
    return pl.pallas_call(
        functools.partial(gather_kernel, job, rows),
        in_specs=in_specs,
        out_specs=out_specs,
        out_shape=out_shape,
        scratch_shapes=scratch,
        compiler_params=pltpu.CompilerParams(
            collective_id=ident, has_side_effects=True, vmem_limit_bytes=VMEM_LIMIT
        ),
        cost_estimate=pl.CostEstimate(
            flops=job.flops, bytes_accessed=SPAN_BYTES, transcendentals=0
        ),
        name=name,
    )(*inputs)


def scatter_kernel(job, rows, *refs):
    refs = list(refs)
    take = lambda n: [refs.pop(0) for _ in range(n)]
    part_refs, weight_refs, side_refs = (
        take(len(job.extras)),
        take(len(job.weights)),
        take(len(job.side)),
    )
    spread_refs = take(1 if job.spread is not None else 0)
    small_refs = take(1 if job.small is not None else 0)
    (out_ref,), final_refs = take(1), take(len(job.sums))
    spread_refs += take(len(spread_refs))
    small_refs += take(len(small_refs))
    part_buf, weight_buf, sums, held, from_core, from_link, out_buf = take(7)
    side_bufs, sum_bufs, final_bufs = take(len(job.side)), take(len(job.sums)), take(len(job.sums))
    weight_sem, load_sem, side_sem, final_sem, out_sem = take(5)
    core_send, core_recv, link_send, link_recv, credit = take(5)
    riders = []
    if spread_refs:
        riders.append(Spread(*spread_refs, *take(2)))
    if small_refs:
        riders.insert(0, SmallSum(True, *small_refs, *take(4)))

    me, other_core, along_x, along_y = plane_places()
    across = along_x + along_y - me
    core = me % 2
    kept = pl.ds(pl.multiple_of(core * rows, 16), rows)
    given = pl.ds(pl.multiple_of((1 - core) * rows, 16), rows)
    units = [
        (across, 0),
        (across, 1),
        (along_x, 0),
        (along_y, 1),
        (along_x, 1),
        (along_y, 0),
        (me, 0),
        (me, 1),
    ]
    targets = [along_x, along_y, along_x, along_y, along_x, along_y]
    added = {4: (1,), 5: (0,), 6: (2, 5), 7: (3, 4)}

    def load(step):
        place, batch = units[step]
        span = unit_rows(place, rows)
        sources = [ref.at[batch, span] for ref in part_refs]
        return copies_into(sources, part_buf.at[step % 2], load_sem.at[step % 2])

    loads = [load(step) for step in range(8)]
    fetches = copies_into(weight_refs, weight_buf, weight_sem)
    for copy in loads[0] + fetches:
        copy.start()
    gives = [
        pltpu.make_async_remote_copy(
            src_ref=sums.at[step % 2, given],
            dst_ref=from_core.at[step % 4],
            send_sem=core_send.at[step],
            recv_sem=core_recv.at[step],
            device_id={"seq": other_core},
            device_id_type=MESH,
        )
        for step in range(8)
    ]
    sends = [
        pltpu.make_async_remote_copy(
            src_ref=held.at[step],
            dst_ref=from_link.at[step],
            send_sem=link_send.at[step],
            recv_sem=link_recv.at[step],
            device_id={"seq": targets[step]},
            device_id_type=MESH,
        )
        for step in range(6)
    ]
    greet((other_core, along_x, along_y), *riders)
    for rider in riders:
        rider.begin()

    def finish(step):
        gives[step].wait_recv()
        kind = jnp.bfloat16 if step < 4 else jnp.float32
        total = sums[step % 2, kept].astype(kind) + from_core[step % 4].astype(kind)
        if step < 4:
            pl.semaphore_signal(credit, inc=1, device_id={"seq": other_core}, device_id_type=MESH)
        for arrived in added.get(step, ()):
            sends[arrived].wait_recv()
            total = total + from_link[arrived].astype(jnp.float32)
        if step < 6:
            held[step] = total.astype(jnp.bfloat16)
            sends[step].start()
        else:
            out = pltpu.make_async_copy(out_buf, out_ref.at[step - 6], out_sem.at[step - 6])
            out_buf[...] = total
            out.start()
            out.wait()

    side = Side(rows, side_refs, side_bufs, sum_bufs, side_sem)
    for step in range(8):
        for copy in loads[step]:
            copy.wait()
        if step == 0:
            for fetch in fetches:
                fetch.wait()
        if step < 7:
            for copy in loads[step + 1]:
                copy.start()
        if step >= 2:
            gives[step - 2].wait_send()
        job.compute(part_buf.at[step % 2], weight_buf, sums.at[step % 2])
        if step >= 4:
            pl.semaphore_wait(credit, 1)
        gives[step].start()
        if step >= 1:
            finish(step - 1)
        for rider in riders if step == 4 else []:
            rider.turn()
        side.run((0, 0, 1, 1, 1, 1, 2, 2)[step])
    if job.side:
        finish_sums(sum_bufs, final_bufs, final_refs, final_sem)
    finish(7)
    for move in gives[6:] + sends:
        move.wait_send()
    for rider in riders:
        rider.end()


def plane_scatter(parts, width, ident, name, job):
    job.extras = list(parts)
    batches, length = parts[0].shape[:2]
    rows = length // lax.axis_size("seq")
    any_space = pl.BlockSpec(memory_space=pl.ANY)
    semaphores = pltpu.SemaphoreType.DMA
    weights = job.weights
    scratch = [
        pltpu.VMEM((2, 2 * rows, braid_width(parts)), parts[0].dtype),
        pltpu.VMEM((weights[0].shape[0], braid_width(weights)), weights[0].dtype),
        pltpu.VMEM((2, 2 * rows, width), jnp.bfloat16),
        pltpu.VMEM((6, rows, width), jnp.bfloat16),
        pltpu.VMEM((4, rows, width), jnp.bfloat16),
        pltpu.VMEM((6, rows, width), jnp.bfloat16),
        pltpu.VMEM((rows, width), jnp.float32),
    ]
    scratch += [pltpu.VMEM((2 * rows, array.shape[2]), array.dtype) for array in job.side]
    scratch += [pltpu.VMEM(shape, jnp.float32) for shape in job.sums]
    scratch += [pltpu.VMEM((2, HEAD_SIZE // 2, shape[1]), jnp.bfloat16) for shape in job.sums]
    scratch += [
        semaphores((copy_count(weights),)),
        semaphores((2, copy_count(parts))),
        semaphores((max(1, len(job.side)),)),
        semaphores((max(1, len(job.sums)), 2)),
        semaphores((2,)),
        semaphores((8,)),
        semaphores((8,)),
        semaphores((6,)),
        semaphores((6,)),
        pltpu.SemaphoreType.REGULAR,
    ]
    out_shape = [jax.ShapeDtypeStruct((batches, rows, width), jnp.float32)]
    out_shape += [jax.ShapeDtypeStruct(shape, jnp.bfloat16) for shape in job.sums]
    inputs = [*parts, *weights, *job.side]
    in_specs, out_specs = [any_space] * len(inputs), [any_space] * len(out_shape)
    if job.spread is not None:
        inputs.append(job.spread)
        in_specs.append(any_space)
        out_shape.append(jax.ShapeDtypeStruct(job.spread.shape, job.spread.dtype))
        out_specs.append(any_space)
        scratch += [semaphores((job.spread.shape[0] + 1,)), semaphores((job.spread.shape[0],))]
    if job.small is not None:
        inputs.append(job.small)
        in_specs.append(pl.BlockSpec(memory_space=pltpu.VMEM))
        out_shape.append(jax.ShapeDtypeStruct(job.small.shape, job.small.dtype))
        out_specs.append(pl.BlockSpec(memory_space=pltpu.VMEM))
        scratch += SmallSum.scratch(job.small)
    return pl.pallas_call(
        functools.partial(scatter_kernel, job, rows),
        in_specs=in_specs,
        out_specs=out_specs,
        out_shape=out_shape,
        scratch_shapes=scratch,
        compiler_params=pltpu.CompilerParams(
            collective_id=ident, has_side_effects=True, vmem_limit_bytes=VMEM_LIMIT
        ),
        cost_estimate=pl.CostEstimate(
            flops=job.flops, bytes_accessed=SPAN_BYTES, transcendentals=0
        ),
        name=name,
    )(*inputs)


def tiles(width, tile, body):
    def step(index, carry):
        body(pl.ds(pl.multiple_of(index * tile, 128), tile))
        return carry

    lax.fori_loop(0, width // tile, step, 0)


GELU_SCALE = 0.7978845608
GELU_CUBE = 0.044715


def gelu_parts(gate):
    square = gate * gate
    bent = jnp.tanh(GELU_SCALE * gate * (1.0 + GELU_CUBE * square))
    half = 0.5 * (1.0 + bent)
    slope = half + 0.5 * gate * (1.0 - bent * bent) * GELU_SCALE * (1.0 + 3.0 * GELU_CUBE * square)
    return gate * half, slope


def add_outer(left, right, total, first):
    def body(span):
        outer = lax.dot_general(
            left[:, span], right[...], (((0,), (0,)), ((), ())), preferred_element_type=jnp.float32
        )
        total[span, :] = outer if first else total[span, :] + outer

    wide = left.shape[1]
    tiles(wide, next(tile for tile in (2 * BRAID, BRAID, HEAD_SIZE) if wide % tile == 0), body)


def hidden_compute(x_buf, weights, extras, outs, sums, first):
    gate_out, up_out, hidden_out = outs
    (weight,) = weights

    def step(index, carry):
        both = pl.ds(pl.multiple_of(index * 2 * BRAID, 128), 2 * BRAID)
        span = pl.ds(pl.multiple_of(index * BRAID, 128), BRAID)
        product = final_dot(x_buf[...], weight[:, both])
        gate, up = product[:, :BRAID], product[:, BRAID:]
        gate_out[:, span] = gate.astype(gate_out.dtype)
        up_out[:, span] = up.astype(up_out.dtype)
        hidden_out[:, span] = (gelu_parts(gate)[0] * up).astype(hidden_out.dtype)
        return carry

    lax.fori_loop(0, weight.shape[1] // (2 * BRAID), step, 0)


def hidden_back_compute(x_buf, weights, extras, outs, sums, first):
    (down_w,) = weights
    gate_in, up_in, hidden_in = extras
    gate_out, up_out = outs
    product = dot_back(x_buf[...], down_w[...])
    for start in range(0, product.shape[1], BRAID):
        span = slice(start, start + BRAID)
        grad = product[:, span]
        value, slope = gelu_parts(gate_in[:, span].astype(jnp.float32))
        gate_out[:, span] = (grad * up_in[:, span].astype(jnp.float32) * slope).astype(
            gate_out.dtype
        )
        up_out[:, span] = (grad * value).astype(up_out.dtype)
    add_outer(hidden_in, x_buf, sums[0], first)


def head_back_compute(x_buf, weights, extras, outs, sums, first):
    outs[0][...] = dot_back(x_buf[...], weights[0][...]).astype(outs[0].dtype)
    add_outer(extras[0], x_buf, sums[1], first)


def rows_compute(part, weight, out):
    def body(span):
        out[:, span] = final_dot(part[...], weight[:, span]).astype(out.dtype)

    tiles(weight.shape[1], 2 * BRAID, body)


def back_compute(part, weight, out):
    def body(span):
        out[:, span] = dot_back(part[...], weight[span, :]).astype(out.dtype)

    tiles(weight.shape[0], 2 * BRAID, body)


def score_parts(query, key, low_bound, row_start, col_start):
    raw = lax.dot_general(
        query, key, (((1,), (1,)), ((), ())), preferred_element_type=jnp.float32
    )
    bent = jnp.tanh(raw * (1.0 / CAP))
    shape = raw.shape
    row = row_start + lax.broadcasted_iota(jnp.int32, shape, 0)
    col = col_start + lax.broadcasted_iota(jnp.int32, shape, 1)
    allowed = (col <= row) & (col >= low_bound)
    return bent, jnp.where(allowed, CAP * bent, -1e30)


def attend_kernel(block, reach, q_ref, k_ref, v_ref, low_ref, out_ref, log_ref):
    index = pl.program_id(1)

    def run(blocks):
        first = (index - (blocks - 1)) * block
        span = pl.ds(pl.multiple_of(first, block), blocks * block)
        _, capped = score_parts(
            q_ref[...], k_ref[span, :], low_ref[...], index * block, first
        )
        peak = jnp.max(capped, axis=-1, keepdims=True)
        power = jnp.exp(capped - peak)
        total = jnp.sum(power, axis=-1, keepdims=True)
        prob = (power * (1.0 / total)).astype(jnp.bfloat16)
        out = jnp.dot(prob, v_ref[span, :], preferred_element_type=jnp.float32)
        out_ref[...] = out.astype(jnp.bfloat16)
        log_ref[...] = peak + jnp.log(total)

    for blocks in range(1, reach + 1):
        if blocks < reach:
            pl.when(index == blocks - 1)(functools.partial(run, blocks))
        else:
            pl.when(index >= blocks - 1)(functools.partial(run, blocks))


def turn_back(value, cosine, sine):
    half = value.shape[-1] // 2
    first, second = value[:, :half], value[:, half:]
    return jnp.concatenate(
        [first * cosine + second * sine, second * cosine - first * sine], axis=-1
    )


def attend_back_kernel(
    block,
    reach,
    q_ref,
    k_ref,
    v_ref,
    g_ref,
    low_ref,
    log_ref,
    cos_ref,
    sin_ref,
    grad_ref,
    dk_ref,
    dv_ref,
):
    index = pl.program_id(1)
    steps = pl.num_programs(1)

    @pl.when(index == 0)
    def _():
        dk_ref[...] = jnp.zeros_like(dk_ref)
        dv_ref[...] = jnp.zeros_like(dv_ref)

    own = pl.ds(pl.multiple_of(index * block, block), block)

    def run(blocks):
        first = (index - (blocks - 1)) * block
        span = pl.ds(pl.multiple_of(first, block), blocks * block)
        query, grad = q_ref[...], g_ref[...]
        key = k_ref[span, :]
        bent, capped = score_parts(query, key, low_ref[...], index * block, first)
        prob = jnp.exp(capped - log_ref[...])
        grad_prob = lax.dot_general(
            grad, v_ref[span, :], (((1,), (1,)), ((), ())), preferred_element_type=jnp.float32
        )
        delta = jnp.sum(prob * grad_prob, axis=-1, keepdims=True)
        grad_score = (prob * (grad_prob - delta) * (1.0 - bent * bent)).astype(jnp.bfloat16)
        dq = jnp.dot(grad_score, key, preferred_element_type=jnp.float32)
        dq = dq * (1.0 / math.sqrt(HEAD_SIZE))
        dq = turn_back(dq, cos_ref[own, :], sin_ref[own, :])
        grad_ref[own, :HEAD_SIZE] = dq.astype(jnp.bfloat16)
        across = (((0,), (0,)), ((), ()))
        dk_ref[span, :] += lax.dot_general(
            grad_score, query, across, preferred_element_type=jnp.float32
        )
        dv_ref[span, :] += lax.dot_general(
            prob.astype(jnp.bfloat16), grad, across, preferred_element_type=jnp.float32
        )

    for blocks in range(1, reach + 1):
        if blocks < reach:
            pl.when(index == blocks - 1)(functools.partial(run, blocks))
        else:
            pl.when(index >= blocks - 1)(functools.partial(run, blocks))

    @pl.when(index == steps - 1)
    def _():
        half = HEAD_SIZE // 2
        odd = lax.axis_index("seq") % 2 == 1
        dk = turn_back(dk_ref[...], cos_ref[...], sin_ref[...])
        for part, grad in enumerate((dk, dv_ref[...])):
            low, high = grad[:, :half], grad[:, half:]
            own = HEAD_SIZE + half * part
            grad_ref[:, own : own + half] = jnp.where(odd, high, low).astype(jnp.bfloat16)
            own += HEAD_SIZE
            grad_ref[:, own : own + half] = jnp.where(odd, low, high).astype(jnp.bfloat16)


def block_shape(length):
    for block in (384, 256, 128):
        if length % block == 0:
            reach = min(length // block, (WIN - 1 + block - 1) // block + 1)
            return block, reach
    raise ValueError("sequence length")


def attend_specs(length, block):
    whole = pl.BlockSpec((None, length, HEAD_SIZE), lambda m, i: (m, 0, 0))
    half = pl.BlockSpec((None, length, HEAD_SIZE // 2), lambda m, i: (m, 0, 0))
    rows = pl.BlockSpec((None, block, HEAD_SIZE), lambda m, i: (m, i, 0))
    line = pl.BlockSpec((None, block, 1), lambda m, i: (m, i, 0))
    return whole, half, rows, line


def project_kernel(x_ref, w_ref, far_ref, cos_ref, sin_ref, q_ref, k_ref, v_ref):
    product = final_dot(x_ref[...], w_ref[...])
    far = final_dot(x_ref[...], far_ref[...])
    cosine, sine = cos_ref[...], sin_ref[...]
    half = HEAD_SIZE // 2
    query = product[:, :HEAD_SIZE]
    own_k, own_v = product[:, HEAD_SIZE : HEAD_SIZE + half], product[:, HEAD_SIZE + half :]
    far_k, far_v = far[:, :half], far[:, half:]
    odd = lax.axis_index("seq") % 2 == 1
    key = jnp.concatenate([jnp.where(odd, far_k, own_k), jnp.where(odd, own_k, far_k)], axis=1)
    query = rotate(query, cosine, sine, 1.0) * (1.0 / math.sqrt(HEAD_SIZE))
    q_ref[...] = query.astype(jnp.bfloat16)
    k_ref[...] = rotate(key, cosine, sine, 1.0).astype(jnp.bfloat16)
    v_ref[:, :half] = jnp.where(odd, far_v, own_v).astype(jnp.bfloat16)
    v_ref[:, half:] = jnp.where(odd, own_v, far_v).astype(jnp.bfloat16)


def project(whole, weight, far, cosine, sine):
    batches, length, width = whole.shape
    block = block_shape(length)[0]
    _, _, rows, _ = attend_specs(length, block)
    half = pl.BlockSpec((None, block, HEAD_SIZE // 2), lambda m, i: (m, i, 0))
    return pl.pallas_call(
        project_kernel,
        grid=(batches, length // block),
        in_specs=[
            pl.BlockSpec((None, block, width), lambda m, i: (m, i, 0)),
            pl.BlockSpec(weight.shape, lambda m, i: (0, 0)),
            pl.BlockSpec(far.shape, lambda m, i: (0, 0)),
            half,
            half,
        ],
        out_specs=[rows] * 3,
        out_shape=[jax.ShapeDtypeStruct((batches, length, HEAD_SIZE), jnp.bfloat16)] * 3,
        compiler_params=pltpu.CompilerParams(vmem_limit_bytes=40 * 2**20),
        cost_estimate=pl.CostEstimate(
            flops=6 * batches * length * width * HEAD_SIZE,
            bytes_accessed=2 * batches * length * width,
            transcendentals=0,
        ),
        name="project",
    )(whole, weight, far, cosine, sine)


def token_tables(tables, made):
    counts_ref, frequency_ref = tables
    cos_ref, sin_ref, low_ref = made
    batches, length, _ = cos_ref.shape
    block = block_shape(length)[0]
    for batch in range(batches):

        def step(index, carry, batch=batch):
            span = pl.ds(pl.multiple_of(index * block, 16), block)
            place = index * block + lax.broadcasted_iota(jnp.int32, (block, HEAD_SIZE // 2), 0)
            place = place.astype(jnp.float32)
            start = jnp.zeros_like(place)
            for number in range(1, DOCUMENTS):
                row = batch * (DOCUMENTS - 1) + number - 1
                count = counts_ref[row : row + 1, :]
                start = jnp.where(place >= count, count, start)
            phase_angle = (place - start) * frequency_ref[...]
            cos_ref[batch, span, :] = jnp.cos(phase_angle)
            sin_ref[batch, span, :] = jnp.sin(phase_angle)
            low = jnp.maximum(start, place - (WIN - 1))
            low_ref[batch, span, :] = low[:, :1].astype(jnp.int32)
            return carry

        lax.fori_loop(0, length // block, step, 0)


def attend(query, key, value, low_bound):
    batches, length = query.shape[:2]
    block, reach = block_shape(length)
    whole, half, rows, line = attend_specs(length, block)
    area = batches * block * block * reach * (length // block)
    return pl.pallas_call(
        functools.partial(attend_kernel, block, reach),
        grid=(batches, length // block),
        in_specs=[rows, whole, whole, line],
        out_specs=[rows, line],
        out_shape=[
            jax.ShapeDtypeStruct((batches, length, HEAD_SIZE), jnp.bfloat16),
            jax.ShapeDtypeStruct((batches, length, 1), jnp.float32),
        ],
        compiler_params=pltpu.CompilerParams(vmem_limit_bytes=40 * 2**20),
        cost_estimate=pl.CostEstimate(
            flops=4 * area * HEAD_SIZE,
            bytes_accessed=10 * batches * length * HEAD_SIZE,
            transcendentals=2 * area,
        ),
        name="attend",
    )(query, key, value, low_bound)


def attend_back(query, key, value, grad, low_bound, log_total, cosine, sine):
    batches, length = query.shape[:2]
    block, reach = block_shape(length)
    whole, half, rows, line = attend_specs(length, block)
    area = batches * block * block * reach * (length // block)
    return pl.pallas_call(
        functools.partial(attend_back_kernel, block, reach),
        grid=(batches, length // block),
        in_specs=[rows, whole, whole, rows, line, line, half, half],
        out_specs=pl.BlockSpec((None, length, 3 * HEAD_SIZE), lambda m, i: (m, 0, 0)),
        out_shape=jax.ShapeDtypeStruct((batches, length, 3 * HEAD_SIZE), jnp.bfloat16),
        scratch_shapes=[pltpu.VMEM((length, HEAD_SIZE), jnp.float32)] * 2,
        compiler_params=pltpu.CompilerParams(vmem_limit_bytes=48 * 2**20),
        cost_estimate=pl.CostEstimate(
            flops=10 * area * HEAD_SIZE,
            bytes_accessed=24 * batches * length * HEAD_SIZE,
            transcendentals=2 * area,
        ),
        name="attend_back",
    )(query, key, value, grad, low_bound, log_total, cosine, sine)


class ByHeads:
    def __init__(self, w_query, key_weight, value_weight, w_out):
        place = lax.axis_index("seq")
        count = lax.axis_size("seq")
        layers = lax.axis_size("fsdp")
        half = HEAD_SIZE // 2

        def columns(weight, width):
            return lax.dynamic_slice_in_dim(weight, place * width, width, axis=1)

        joined = jnp.concatenate(
            [columns(w_query, HEAD_SIZE), columns(key_weight, half), columns(value_weight, half)],
            axis=1,
        )
        depth = HEAD_SIZE // count
        here = QUERY_HEADS // layers
        part = w_out.reshape(here, count, depth, w_out.shape[1])
        part = lax.dynamic_index_in_dim(part, place, axis=1, keepdims=False)
        rows = joined.shape[0]
        both = jnp.concatenate([joined, part.reshape(-1, joined.shape[1])], axis=0)
        self.first = both
        self.both = lax.all_gather(both, "fsdp", axis=0)
        self.split = rows
        self.part_shape = (QUERY_HEADS * depth, w_out.shape[1])

    def forward(self, normed, segments):
        batches, rows, width = normed.shape
        length = rows * lax.axis_size("seq")
        half = HEAD_SIZE // 2
        numbers = jnp.arange(1, DOCUMENTS, dtype=segments.dtype)
        counts = jnp.sum((segments[:, None] < numbers[:, None]).astype(jnp.float32), axis=2)
        counts = jnp.pad(counts.reshape(-1), (0, 8 - batches * (DOCUMENTS - 1)))
        counts = jnp.broadcast_to(counts[:, None], (8, half))
        frequency = 10000.0 ** (-jnp.arange(half, dtype=jnp.float32) * 2.0 / HEAD_SIZE)
        table = jax.ShapeDtypeStruct((batches, length, half), jnp.float32)
        bound = jax.ShapeDtypeStruct((batches, length, 1), jnp.int32)
        whole, cosine, sine, low_bound = plane_gather(
            normed,
            0,
            "gather_normed",
            Job(
                None,
                tables=[frequency[None]],
                small=counts,
                spare=(token_tables, [table, table, bound]),
            ),
        )
        whole, both = lax.optimization_barrier((whole, self.both))
        self.joined = both[:, : self.split].reshape(-1, both.shape[2])
        self.out_rows = swap_parts(both[:, self.split :].reshape(self.part_shape), 0, 0)
        self.far = lax.ppermute(
            self.joined[:, HEAD_SIZE:], "seq", [(i, i ^ 1) for i in range(QUERY_HEADS)]
        )
        query, key, value = project(whole, self.joined, self.far, cosine, sine)
        attended, log_total = attend(query, key, value, low_bound)
        job = Job(
            rows_compute, weights=[self.out_rows], flops=2 * batches * length * HEAD_SIZE * width
        )
        (mixed,) = plane_scatter([attended], width, 1, "scatter_mixed", job)
        return mixed, (whole, query, key, value, low_bound, log_total, cosine, sine, attended)

    def open_back(self, grad_mixed_b, saved, side):
        attended = saved[-1]
        batches, length = attended.shape[:2]
        width = grad_mixed_b.shape[-1]
        job = Job(
            head_back_compute,
            weights=[self.out_rows],
            extras=[attended],
            outs=[(HEAD_SIZE, jnp.bfloat16)],
            side=side,
            sums=[(side[0].shape[2], side[1].shape[2]), (HEAD_SIZE, width)],
            flops=2 * batches * length * (HEAD_SIZE * width + side[0].shape[2] * side[1].shape[2]),
        )
        _, grad_att, side_sum, self.out_sum = plane_gather(
            grad_mixed_b, 2, "gather_grad_mixed", job
        )
        return grad_att, side_sum

    def middle_back(self, grad_att, saved):
        _, query, key, value, low_bound, log_total, cosine, sine, _ = saved
        grads = attend_back(query, key, value, grad_att, low_bound, log_total, cosine, sine)
        grads, self.out_own = lax.optimization_barrier((grads, scatter_rows(self.out_sum)))
        return grads

    def close_back(self, grads, saved, meanwhile, gains):
        count = lax.axis_size("seq")
        joined = dot_rows(saved[0], grads).astype(jnp.bfloat16)
        wide = 2 * HEAD_SIZE
        pairs = ((joined[:, :wide], self.joined), (joined[:, wide:], self.far))
        through = sum(
            jnp.sum(grad.astype(jnp.float32) * weight.astype(jnp.float32), axis=1)
            for grad, weight in pairs
        )
        gains = jnp.stack([through, *gains])
        own, far = joined[:, HEAD_SIZE : 2 * HEAD_SIZE], joined[:, 2 * HEAD_SIZE :]
        came = lax.ppermute(far, "seq", [(i, i ^ 1) for i in range(count)])
        own = (own.astype(jnp.float32) + came.astype(jnp.float32)).astype(jnp.bfloat16)
        joined = jnp.concatenate([joined[:, :HEAD_SIZE], own], axis=1)
        grads, joined, meanwhile = lax.optimization_barrier((grads, joined, meanwhile))
        self.joined_sum = joined

        parts = self.out_own.reshape(self.out_own.shape[0], count, -1).transpose(1, 0, 2)
        rows = grads.shape[0] * grads.shape[1]
        width = self.joined.shape[0]
        job = Job(
            back_compute,
            weights=[self.joined, self.far],
            spread=parts,
            small=gains.reshape(-1, HEAD_SIZE // 2),
            flops=6 * rows * HEAD_SIZE * width,
        )
        grad_normed, self.placed, gains = plane_scatter(
            [grads], width, 3, "scatter_grad_normed", job
        )
        return grad_normed, meanwhile, gains.reshape(4, -1)

    def weight_grads(self):
        half = HEAD_SIZE // 2
        joined = scatter_rows(self.joined_sum).astype(jnp.float32)
        return (
            joined[:, :HEAD_SIZE],
            joined[:, HEAD_SIZE : HEAD_SIZE + half],
            joined[:, HEAD_SIZE + half :],
            self.placed.astype(jnp.float32).reshape(-1, self.placed.shape[2]),
        )


class ByTokens:
    def __init__(self, w_query, key_weight, value_weight, w_out):
        self.weights = fetch_attention(w_query, key_weight, value_weight, w_out)
        self.records, self.first = [], jnp.zeros(())

    def forward(self, normed, segments):
        seg_whole = lax.all_gather(segments, "seq", axis=1, tiled=True)
        done = [self.forward_one(*pair) for pair in zip(normed, seg_whole)]
        return jnp.stack([mixed for mixed, _ in done]), [saved for _, saved in done]

    def forward_one(self, normed, seg_whole):
        token_rows = normed.shape[0]
        halo_count = (WIN - 2 + token_rows) // token_rows
        w_query, key_weight, value_weight, w_out = self.weights
        seq_place = lax.axis_index("seq")
        seg_here = lax.dynamic_slice_in_dim(seg_whole, seq_place * token_rows, token_rows)
        position = jnp.arange(seg_whole.shape[0], dtype=jnp.int32) - doc_starts(seg_whole)
        position = lax.dynamic_slice_in_dim(position, seq_place * token_rows, token_rows)
        cosine, sine = (table[:, None] for table in angles(position, HEAD_SIZE))
        query = rotate(
            final_dot(normed, w_query).reshape(token_rows, QUERY_HEADS, HEAD_SIZE),
            cosine,
            sine,
            1.0,
        )
        query = (query * (1.0 / math.sqrt(HEAD_SIZE))).astype(jnp.bfloat16)
        key = rotate(
            final_dot(normed, key_weight).reshape(token_rows, KEY_VALUE_HEADS, HEAD_SIZE),
            cosine,
            sine,
            1.0,
        ).astype(jnp.bfloat16)
        value = final_dot(normed, value_weight).reshape(token_rows, KEY_VALUE_HEADS, HEAD_SIZE)
        pair = key_window(jnp.stack([key, value.astype(jnp.bfloat16)]), halo_count)
        allowed = window_mask(seg_here, seg_whole, seq_place, token_rows, halo_count)
        query = query.reshape(token_rows, KEY_VALUE_HEADS, -1, HEAD_SIZE)
        score = jnp.einsum("qhgd,khd->hgqk", query, pair[0], preferred_element_type=jnp.float32)
        capped = jnp.where(allowed, CAP * jnp.tanh(score / CAP), -jnp.inf)
        peak = jnp.max(capped, axis=-1, keepdims=True)
        power = jnp.exp(capped - peak)
        total = jnp.sum(power, axis=-1, keepdims=True)
        attended = jnp.einsum(
            "hgqk,khd->qhgd",
            (power / total).astype(jnp.bfloat16),
            pair[1],
            preferred_element_type=jnp.float32,
        )
        attended = attended.reshape(token_rows, QUERY_HEADS * HEAD_SIZE).astype(jnp.bfloat16)
        mixed = final_dot(attended, w_out)
        log_total = peak + jnp.log(total)
        return mixed, (normed, query, pair, allowed, log_total, cosine, sine, attended)

    def open_back(self, grad_mixed_b, saved, side):
        return grad_mixed_b, dot_rows(*side)

    def middle_back(self, grad_mixed_b, saved):
        return grad_mixed_b

    def close_back(self, grad_mixed_b, saved, meanwhile, gains):
        grads = [self.backward_one(*pair) for pair in zip(grad_mixed_b, saved)]
        return jnp.stack(grads), meanwhile, None

    def backward_one(self, grad_mixed_b, saved):
        normed, query, pair, allowed, log_total, cosine, sine, attended = saved
        token_rows = normed.shape[0]
        halo_count = (WIN - 2 + token_rows) // token_rows
        w_query, key_weight, value_weight, w_out = self.weights
        grad_att = dot_back(grad_mixed_b, w_out).astype(jnp.bfloat16)
        grad_att = grad_att.reshape(token_rows, KEY_VALUE_HEADS, -1, HEAD_SIZE)
        score = jnp.einsum("qhgd,khd->hgqk", query, pair[0], preferred_element_type=jnp.float32)
        bent = jnp.tanh(score / CAP)
        prob = jnp.exp(jnp.where(allowed, CAP * bent, -jnp.inf) - log_total)
        grad_prob = jnp.einsum(
            "qhgd,khd->hgqk", grad_att, pair[1], preferred_element_type=jnp.float32
        )
        delta = jnp.sum(prob * grad_prob, axis=-1, keepdims=True)
        grad_score = (prob * (grad_prob - delta) * (1.0 - bent * bent)).astype(jnp.bfloat16)
        dq = jnp.einsum("hgqk,khd->qhgd", grad_score, pair[0], preferred_element_type=jnp.float32)
        dk = jnp.einsum("hgqk,qhgd->khd", grad_score, query, preferred_element_type=jnp.float32)
        dv = jnp.einsum(
            "hgqk,qhgd->khd", prob.astype(jnp.bfloat16), grad_att, preferred_element_type=jnp.float32
        )
        paired = window_grads(jnp.stack([dk, dv]), halo_count, token_rows)
        dq = rotate(
            dq.reshape(token_rows, QUERY_HEADS, HEAD_SIZE) * (1.0 / math.sqrt(HEAD_SIZE)),
            cosine,
            sine,
            -1.0,
        )
        dq = dq.reshape(token_rows, -1).astype(jnp.bfloat16)
        dk = rotate(paired[0], cosine, sine, -1.0).reshape(token_rows, -1).astype(jnp.bfloat16)
        dv = paired[1].reshape(token_rows, -1).astype(jnp.bfloat16)
        self.records.append((normed, dq, dk, dv, attended, grad_mixed_b))
        return dot_back(dq, w_query) + dot_back(dk, key_weight) + dot_back(dv, value_weight)

    def weight_grads(self):
        normed, dq, dk, dv, attended, grad_mixed_b = (
            jnp.concatenate(parts, axis=0) for parts in zip(*self.records)
        )
        normed = lax.all_gather(normed, "seq", axis=0, tiled=True)
        attended = lax.all_gather(attended, "seq", axis=0, tiled=True)
        sums = []
        for rows, grads in ((normed, dq), (normed, dk), (normed, dv), (attended, grad_mixed_b)):
            column_sum = dot_rows(rows, swap_parts(grads, 1, 0)).astype(jnp.bfloat16)
            owned = lax.psum_scatter(column_sum, "fsdp", scatter_dimension=0, tiled=True)
            sums.append(owned.astype(jnp.float32))
        return tuple(sums)


class FeedForward:
    def __init__(self, w_gate, w_up, w_down, by_kernel, first):
        place = lax.optimization_barrier((lax.axis_index("seq"), first))[0]
        count = lax.axis_size("seq")
        self.by_kernel = by_kernel
        self.run = w_gate.shape[1] // (count * count)

        def columns(weight):
            parts = [
                lax.dynamic_slice_in_dim(
                    weight, (t * count + place) * self.run, self.run, axis=1
                )
                for t in range(count)
            ]
            return jnp.concatenate(parts, axis=1)

        here = w_down.shape[0] // (count * self.run)
        part = w_down.reshape(here, count, self.run, w_down.shape[1])
        part = lax.dynamic_index_in_dim(part, place, axis=1, keepdims=False)
        self.gate = gather_rows(columns(w_gate))
        self.up = gather_rows(columns(w_up))
        self.down = gather_rows(part.reshape(here * self.run, -1))

    def forward(self, ffn_in):
        hidden_width, width = self.down.shape
        if self.by_kernel:
            rows = ffn_in.shape[0] * ffn_in.shape[1] * lax.axis_size("seq")
            job = Job(
                hidden_compute,
                weights=[self.gate, self.up],
                outs=[(hidden_width, jnp.bfloat16)] * 3,
                flops=4 * rows * width * hidden_width,
            )
            whole, gate_proj, up_proj, hidden = plane_gather(ffn_in, 4, "gather_ffn_in", job)
            job = Job(
                rows_compute, weights=[self.down], flops=2 * rows * width * hidden_width
            )
            (down_proj,) = plane_scatter([hidden], width, 5, "scatter_down", job)
        else:
            whole = lax.all_gather(ffn_in, "seq", axis=1, tiled=True)
            gate_proj = final_dot(whole, self.gate)
            up_proj = final_dot(whole, self.up)
            hidden = geglu(gate_proj, up_proj).astype(jnp.bfloat16)
            down_proj = lax.psum_scatter(
                final_dot(hidden, self.down).astype(jnp.bfloat16),
                "seq",
                scatter_dimension=1,
                tiled=True,
            ).astype(jnp.float32)
        return down_proj, (whole, gate_proj, up_proj, hidden)

    def backward(self, grad_down_b, saved):
        whole, gate_proj, up_proj, hidden = saved
        hidden_width, width = self.down.shape
        if self.by_kernel:
            rows = whole.shape[0] * whole.shape[1]
            job = Job(
                hidden_back_compute,
                weights=[self.down],
                extras=[gate_proj, up_proj, hidden],
                outs=[(hidden_width, jnp.bfloat16)] * 2,
                sums=[(hidden_width, width)],
                flops=4 * rows * width * hidden_width,
            )
            _, grad_gate, grad_up, self.down_sum = plane_gather(
                grad_down_b, 6, "gather_grad_down", job
            )
            job = Job(
                back_compute,
                weights=[self.gate, self.up],
                side=[whole, grad_gate],
                sums=[(width, hidden_width)],
                flops=6 * rows * width * hidden_width,
            )
            grad_ffn_in, self.gate_sum = plane_scatter(
                [grad_gate, grad_up], width, 7, "scatter_grad_ffn_in", job
            )
        else:
            grad_whole = lax.all_gather(grad_down_b, "seq", axis=1, tiled=True)
            grad_hidden = dot_back(grad_whole, self.down)
            _, pullback = jax.vjp(geglu, gate_proj, up_proj)
            grad_gate, grad_up = (g.astype(jnp.bfloat16) for g in pullback(grad_hidden))
            partial = dot_back(grad_gate, self.gate) + dot_back(grad_up, self.up)
            grad_ffn_in = lax.psum_scatter(
                partial.astype(jnp.bfloat16), "seq", scatter_dimension=1, tiled=True
            ).astype(jnp.float32)
            self.down_sum = dot_rows(hidden, grad_whole)
            self.gate_sum = dot_rows(whole, grad_gate)
        self.up_side = (whole, grad_up)
        return grad_ffn_in

    def own_columns(self, own):
        return swap_parts(own, 1, 1).astype(jnp.float32)

    def own_rows(self, own):
        here = own.shape[0] // self.run
        moved = swap_parts(own, 1, 0)
        moved = moved.reshape(-1, here, self.run, moved.shape[1]).transpose(1, 0, 2, 3)
        return moved.astype(jnp.float32).reshape(-1, moved.shape[3])


def on_device(
    tokens,
    segments,
    w_query,
    key_weight,
    value_weight,
    w_out,
    w_gate,
    w_up,
    w_down,
    gain_attn_in,
    gain_attn_out,
    gain_ffn_in,
    gain_ffn_out,
    cotangent,
):
    by_kernel = (
        lax.axis_size("seq") == QUERY_HEADS
        and tokens.shape[0] == 2
        and QUERY_HEADS % lax.axis_size("fsdp") == 0
    )
    attention = (ByHeads if by_kernel else ByTokens)(w_query, key_weight, value_weight, w_out)
    ffn = FeedForward(w_gate, w_up, w_down, by_kernel, attention.first)

    stream = tokens[:, 0].astype(jnp.float32)
    normed = rms_gain(stream, gain_attn_in).astype(jnp.bfloat16)
    mixed, attention_saved = attention.forward(normed, segments[:, 0])
    middle = stream + rms_gain(mixed, gain_attn_out)
    ffn_in = rms_gain(middle, gain_ffn_in).astype(jnp.bfloat16)
    down_proj, ffn_saved = ffn.forward(ffn_in)
    result = middle + rms_gain(down_proj, gain_ffn_out)

    grad_result = cotangent[:, 0].astype(jnp.float32)
    _, pullback = jax.vjp(rms_gain, down_proj, gain_ffn_out)
    grad_down, grad_gain_four = pullback(grad_result)
    grad_ffn_in = ffn.backward(grad_down.astype(jnp.bfloat16), ffn_saved)
    _, pullback = jax.vjp(rms_gain, middle, gain_ffn_in)
    grad_middle, grad_gain_three = pullback(grad_ffn_in)
    grad_middle = grad_result + grad_middle
    _, pullback = jax.vjp(rms_gain, mixed, gain_attn_out)
    grad_mixed, grad_gain_two = pullback(grad_middle)
    grad_mixed, w_down_grad = lax.optimization_barrier(
        (grad_mixed.astype(jnp.bfloat16), scatter_rows(ffn.down_sum))
    )
    grad_att, up_sum = attention.open_back(grad_mixed, attention_saved, ffn.up_side)
    grad_att, w_gate_grad = lax.optimization_barrier((grad_att, scatter_rows(ffn.gate_sum)))
    w_down_grad = ffn.own_rows(w_down_grad)
    grads = attention.middle_back(grad_att, attention_saved)
    grads, w_gate_grad, w_down_grad = lax.optimization_barrier((grads, w_gate_grad, w_down_grad))
    grad_normed, w_gate_grad, gains = attention.close_back(
        grads,
        attention_saved,
        ffn.own_columns(w_gate_grad),
        [grad_gain_two, grad_gain_three, grad_gain_four],
    )
    _, pullback = jax.vjp(rms_gain, stream, gain_attn_in)
    grad_stream, grad_gain_one = pullback(grad_normed)
    grad_stream = grad_middle + grad_stream

    w_up_grad = ffn.own_columns(scatter_rows(up_sum))
    if gains is None:
        gains = jnp.stack([grad_gain_one, grad_gain_two, grad_gain_three, grad_gain_four])
        gains = lax.psum(gains, ("seq", "fsdp"))
        grad_gain_one = gains[0]
    else:
        grad_gain_one = gains[0] / gain_attn_in
    query_grad, key_grad, value_grad, out_grad = attention.weight_grads()
    return (
        result.astype(jnp.bfloat16)[:, None],
        grad_stream[:, None],
        query_grad,
        key_grad,
        value_grad,
        out_grad,
        w_gate_grad,
        w_up_grad,
        w_down_grad,
        grad_gain_one,
        gains[1],
        gains[2],
        gains[3],
    )


def solution(mesh):
    in_specs = (
        P(None, "fsdp", "seq", None),
        P(None, "fsdp", "seq"),
        P("fsdp", None),
        P("fsdp", None),
        P("fsdp", None),
        P("fsdp", None),
        P("fsdp", None),
        P("fsdp", None),
        P("fsdp", None),
        P(),
        P(),
        P(),
        P(),
        P(None, "fsdp", "seq", None),
    )
    out_specs = (
        P(None, "fsdp", "seq", None),
        P(None, "fsdp", "seq", None),
        P("fsdp", "seq"),
        P("fsdp", "seq"),
        P("fsdp", "seq"),
        P("fsdp", "seq"),
        P("fsdp", "seq"),
        P("fsdp", "seq"),
        P("fsdp", "seq"),
        P(),
        P(),
        P(),
        P(),
    )
    return jax.shard_map(
        on_device, mesh=mesh, in_specs=in_specs, out_specs=out_specs, check_vma=False
    )
```

```python
import functools
import math

import jax
import jax.numpy as jnp
from jax import lax
from jax.experimental import pallas as pl
from jax.experimental.pallas import tpu as pltpu
from jax.sharding import PartitionSpec as P

QUERY_HEADS = 8
KEY_VALUE_HEADS = 4
HEAD_SIZE = 256
CAP = 50
WIN = 1024
DOCUMENTS = 4
VMEM_LIMIT = 60 * 2**20
SPAN_BYTES = 270_000_000


epsilon = 1e-06


def shifted(value, axis, steps):
    count = lax.axis_size(axis)
    initial, last = (max(0, -steps), min(count, count - steps))
    return lax.ppermute(value, axis, [(source, source + steps) for source in range(initial, last)])


def rms_gain(stream, gain):
    return stream * lax.rsqrt(jnp.mean(stream * stream, axis=-1, keepdims=True) + epsilon) * gain


def geglu(gate_proj, up_proj):
    return jax.nn.gelu(gate_proj, approximate=True) * up_proj


def angles(position, size):
    frequency = 10000.0 ** (-jnp.arange(size // 2, dtype=jnp.float32) * 2.0 / size)
    phase_angle = position.astype(jnp.float32)[..., None] * frequency
    return (jnp.cos(phase_angle), jnp.sin(phase_angle))


def rotate(value_rows, cosine_table, sine_table, direction):
    half_size = value_rows.shape[-1] // 2
    first_half = value_rows[..., :half_size]
    second = value_rows[..., half_size:]
    return jnp.concatenate(
        [
            first_half * cosine_table - direction * second * sine_table,
            second * cosine_table + direction * first_half * sine_table,
        ],
        axis=-1,
    )


def doc_starts(segment):
    starts = jnp.zeros_like(segment)
    for number in range(1, DOCUMENTS):
        count = jnp.sum((segment < number).astype(jnp.int32), axis=-1, keepdims=True)
        starts = jnp.where(segment >= number, count, starts)
    return starts


def final_dot(left_side, right_side):
    return jnp.dot(left_side, right_side, preferred_element_type=jnp.float32)


def dot_back(left_side, right_side):
    contract = (((left_side.ndim - 1,), (1,)), ((), ()))
    return lax.dot_general(left_side, right_side, contract, preferred_element_type=jnp.float32)


def dot_rows(left_side, right_side):
    left_side = left_side.reshape(-1, left_side.shape[-1])
    right_side = right_side.reshape(-1, right_side.shape[-1])
    return lax.dot_general(
        left_side, right_side, (((0,), (0,)), ((), ())), preferred_element_type=jnp.float32
    )


def fetch_attention(w_query, key_weight, value_weight, w_out):
    return (
        lax.all_gather(w_query, "fsdp", axis=0, tiled=True),
        lax.all_gather(key_weight, "fsdp", axis=0, tiled=True),
        lax.all_gather(value_weight, "fsdp", axis=0, tiled=True),
        lax.all_gather(w_out, "fsdp", axis=0, tiled=True),
    )


def key_window(kv_pair, halo_count):
    arrived = [shifted(kv_pair, "seq", offset) for offset in range(halo_count, 0, -1)]
    return jnp.concatenate(arrived + [kv_pair], axis=1)


def window_grads(paired_gradient, halo_count, token_rows):
    summed = paired_gradient[:, halo_count * token_rows :]
    for offset in range(1, halo_count + 1):
        begin = (halo_count - offset) * token_rows
        summed = summed + shifted(
            paired_gradient[:, begin : begin + token_rows].astype(jnp.bfloat16), "seq", -offset
        ).astype(jnp.float32)
    return summed


def window_mask(seg_here, seg_whole, seq_place, token_rows, halo_count):
    padded = jnp.concatenate([jnp.full((halo_count * token_rows,), -1, jnp.int32), seg_whole])
    key_seg = lax.dynamic_slice_in_dim(
        padded, seq_place * token_rows, (halo_count + 1) * token_rows
    )
    query_pos = seq_place * token_rows + jnp.arange(token_rows, dtype=jnp.int32)
    key_pos = (
        seq_place * token_rows
        - halo_count * token_rows
        + jnp.arange((halo_count + 1) * token_rows, dtype=jnp.int32)
    )
    distance = query_pos[:, None] - key_pos[None, :]
    return (seg_here[:, None] == key_seg[None, :]) & (distance >= 0) & (distance < WIN)


def gather_rows(rows):
    return lax.all_gather(rows, "fsdp", axis=0, tiled=True)


def scatter_rows(partial):
    return lax.psum_scatter(
        partial.astype(jnp.bfloat16), "fsdp", scatter_dimension=0, tiled=True
    )


def swap_parts(value, split_axis, concat_axis):
    return lax.all_to_all(
        value, "seq", split_axis=split_axis, concat_axis=concat_axis, tiled=True
    )


MESH = pl.DeviceIdType.MESH


def plane_places():
    me = lax.axis_index("seq")
    other_core = me + 1 - 2 * (me % 2)
    along_x = me + 2 - 4 * ((me // 2) % 2)
    along_y = me + 4 - 8 * (me // 4)
    return me, other_core, along_x, along_y


def greet(neighbours, *others):
    barrier = pltpu.get_barrier_semaphore()
    for neighbour in neighbours:
        pl.semaphore_signal(barrier, inc=1, device_id={"seq": neighbour}, device_id_type=MESH)
    count = len(neighbours)
    for other in others:
        count = count + other.greet(barrier)
    pl.semaphore_wait(barrier, count)


class Spread:
    def __init__(self, parts_ref, placed_ref, send, recv):
        self.parts, self.placed, self.send, self.recv = parts_ref, placed_ref, send, recv
        self.me, self.layer = lax.axis_index("seq"), lax.axis_index("fsdp")
        layers = lax.axis_size("fsdp")
        shared = lax.axis_size("seq") // layers
        self.owner = self.me // shared
        self.slot = (self.me - self.owner * shared) * layers + self.layer
        self.targets = [(place, self.owner) for place in range(shared * layers)]
        self.sources = [
            (self.layer * shared + part, from_layer)
            for part in range(shared)
            for from_layer in range(layers)
        ]

    def turn(self):
        pass

    def away(self, device):
        return (device[0] != self.me) | (device[1] != self.layer)

    def greet(self, barrier):
        for place, layer in self.targets + self.sources:

            @pl.when(self.away((place, layer)))
            def _(place=place, layer=layer):
                device = {"seq": place, "fsdp": layer}
                pl.semaphore_signal(barrier, inc=1, device_id=device, device_id_type=MESH)

        return 2 * len(self.targets) - 2 * (self.owner == self.layer).astype(jnp.int32)

    def copy(self, index, slot, device):
        return pltpu.make_async_remote_copy(
            src_ref=self.parts.at[index],
            dst_ref=self.placed.at[slot],
            send_sem=self.send.at[index],
            recv_sem=self.recv.at[slot],
            device_id={"seq": device[0], "fsdp": device[1]},
            device_id_type=MESH,
        )

    def own(self):
        source, target = self.parts.at[self.me], self.placed.at[self.slot]
        return pltpu.make_async_copy(source, target, self.send.at[len(self.targets)])

    def begin(self):
        for index, device in enumerate(self.targets):
            pl.when(self.away(device))(self.copy(index, self.slot, device).start)
        pl.when(self.owner == self.layer)(self.own().start)

    def end(self):
        for index, device in enumerate(self.targets):
            pl.when(self.away(device))(self.copy(index, self.slot, device).wait_send)
        for index, device in enumerate(self.sources):
            pl.when(self.away(device))(self.copy(0, index, device).wait_recv)
        pl.when(self.owner == self.layer)(self.own().wait)


class SmallSum:
    def __init__(self, over_layers, value_ref, out_ref, *scratch):
        self.over_layers, self.value, self.out = over_layers, value_ref, out_ref
        self.plane_buf, self.layer_buf, self.plane_sems, self.layer_sems = scratch
        self.me, *neighbours = plane_places()
        steps = [neighbour - self.me for neighbour in neighbours]
        self.peers = [
            self.me + sum(step for bit, step in enumerate(steps) if (index >> bit) % 2)
            for index in range(1, 8)
        ]
        self.layer, self.layers = lax.axis_index("fsdp"), lax.axis_size("fsdp")
        hops = range(1, self.layers) if over_layers else []
        self.others = [lax.rem(self.layer + hop, self.layers) for hop in hops]

    @staticmethod
    def scratch(value):
        layers = lax.axis_size("fsdp")
        return [
            pltpu.VMEM((8,) + value.shape, value.dtype),
            pltpu.VMEM((layers,) + value.shape, value.dtype),
            pltpu.SemaphoreType.DMA((2, 7)),
            pltpu.SemaphoreType.DMA((2, layers)),
        ]

    def greet(self, barrier):
        farther = [peer for index, peer in enumerate(self.peers) if index not in (0, 1, 3)]
        for peer in farther:
            pl.semaphore_signal(barrier, inc=1, device_id={"seq": peer}, device_id_type=MESH)
        for other in self.others:
            pl.semaphore_signal(barrier, inc=1, device_id={"fsdp": other}, device_id_type=MESH)
        return len(farther) + len(self.others)

    def copy(self, buf, sems, slot, index, device):
        return pltpu.make_async_remote_copy(
            src_ref=buf.at[slot],
            dst_ref=buf.at[slot],
            send_sem=sems.at[0, index],
            recv_sem=sems.at[1, index],
            device_id=device,
            device_id_type=MESH,
        )

    def plane_copies(self):
        return [
            self.copy(self.plane_buf, self.plane_sems, self.me, index, {"seq": peer})
            for index, peer in enumerate(self.peers)
        ]

    def layer_copies(self):
        return [
            self.copy(self.layer_buf, self.layer_sems, self.layer, index, {"fsdp": other})
            for index, other in enumerate(self.others)
        ]

    def begin(self):
        self.plane_buf[self.me] = self.value[...]
        for copy in self.plane_copies():
            copy.start()

    def turn(self):
        for copy in self.plane_copies():
            copy.wait_recv()
        total = self.plane_buf[0]
        for index in range(1, 8):
            total = total + self.plane_buf[index]
        if not self.over_layers:
            self.out[...] = total
            return
        self.layer_buf[self.layer] = total
        for copy in self.layer_copies():
            copy.start()

    def end(self):
        for copy in self.layer_copies():
            copy.wait_recv()
        if self.over_layers:
            total = self.layer_buf[0]
            for index in range(1, self.layers):
                total = total + self.layer_buf[index]
            self.out[...] = total
        for copy in self.plane_copies() + self.layer_copies():
            copy.wait_send()


BRAID = 384


def braid_width(arrays):
    return sum(array.shape[-1] for array in arrays)


def braided(arrays):
    return len(arrays) == 2 and arrays[0].shape[-1] == arrays[1].shape[-1]


def copies_into(sources, target, sem):
    if not braided(sources):
        copies, at = [], 0
        for i, source in enumerate(sources):
            width = source.shape[-1]
            copies.append(
                pltpu.make_async_copy(source, target.at[:, pl.ds(at, width)], sem.at[i])
            )
            at += width
        return copies
    groups = sources[0].shape[-1] // BRAID
    copies = []
    for group in range(groups):
        for part, source in enumerate(sources):
            at = group * len(sources) + part
            copies.append(
                pltpu.make_async_copy(
                    source.at[:, pl.ds(group * BRAID, BRAID)],
                    target.at[:, pl.ds(at * BRAID, BRAID)],
                    sem.at[at],
                )
            )
    return copies


def copy_count(arrays):
    return braid_width(arrays) // BRAID if braided(arrays) else len(arrays)


def unit_rows(place, rows):
    return pl.ds(pl.multiple_of((place // 2) * (2 * rows), 16), 2 * rows)


class Job:
    def __init__(
        self,
        compute,
        weights=(),
        extras=(),
        outs=(),
        sums=(),
        side=(),
        tables=(),
        spare=None,
        spread=None,
        small=None,
        flops=0,
    ):
        self.spread, self.small = spread, small
        self.compute, self.flops, self.spare = compute, flops, spare
        self.tables = list(tables)
        self.weights, self.extras, self.outs = list(weights), list(extras), list(outs)
        self.sums, self.side = list(sums), list(side)


def gather_kernel(job, rows, *refs):
    refs = list(refs)
    take = lambda n: [refs.pop(0) for _ in range(n)]
    (local_ref,) = take(1)
    weight_refs, extra_refs, side_refs = (
        take(len(job.weights)),
        take(len(job.extras)),
        take(len(job.side)),
    )
    table_refs, count_refs = take(len(job.tables)), take(1 if job.small is not None else 0)
    (whole_ref,), out_refs, final_refs = take(1), take(len(job.outs)), take(len(job.sums))
    made_refs = take(len(job.spare[1]) if job.spare else 0)
    send_sem, recv_sem, own_sem, x_buf = take(4)
    weight_bufs = take(1 if job.weights else 0)
    extra_bufs, side_bufs, out_bufs = (
        take(len(job.extras)),
        take(len(job.side)),
        take(len(job.outs)),
    )
    sum_bufs, final_bufs = take(len(job.sums)), take(len(job.sums))
    weight_sem, load_sem, side_sem, store_sem, final_sem = take(5)
    if count_refs:
        summed = take(1)[0]
        small = SmallSum(False, count_refs[0], summed, *take(4))
        table_refs = [summed] + table_refs

    me, other_core, along_x, along_y = plane_places()
    across = along_x + along_y - me
    core = me % 2

    def piece(batch, place):
        return whole_ref.at[batch, pl.ds(pl.multiple_of(place * rows, 16), rows)]

    def transfer(slot, source, batch, place, target):
        return pltpu.make_async_remote_copy(
            src_ref=source,
            dst_ref=piece(batch, place),
            send_sem=send_sem.at[slot],
            recv_sem=recv_sem.at[slot],
            device_id={"seq": target},
            device_id_type=MESH,
        )

    def forward(slot, batch, place, target):
        return transfer(slot, piece(batch, place), batch, place, target)

    moves = [
        transfer(0, local_ref.at[0], 0, me, along_x),
        transfer(1, local_ref.at[1], 1, me, along_x),
        transfer(2, local_ref.at[1], 1, me, along_y),
        transfer(3, local_ref.at[0], 0, me, along_y),
        forward(4, 0, along_x, along_y),
        forward(5, 1, along_y, along_x),
        transfer(6, local_ref.at[0], 0, me, other_core),
        transfer(7, local_ref.at[1], 1, me, other_core),
        forward(8, 0, along_x, other_core),
        forward(9, 1, along_x, other_core),
        forward(10, 1, along_y, other_core),
        forward(11, 0, along_y, other_core),
        forward(12, 0, across, other_core),
        forward(13, 1, across, other_core),
    ]
    greet((other_core, along_x, along_y), *([small] if count_refs else []))
    if count_refs:
        small.begin()
    for slot in (0, 2, 1, 3, 6, 7):
        moves[slot].start()
    owns = [
        pltpu.make_async_copy(local_ref.at[batch], piece(batch, me), own_sem.at[batch])
        for batch in range(2)
    ]
    for own in owns:
        own.start()
    fetches = copies_into(weight_refs, weight_bufs[0], weight_sem) if job.weights else []
    for fetch in fetches:
        fetch.start()
    if count_refs:
        small.turn()
    if job.spare:
        job.spare[0](table_refs, made_refs)
    stores = []

    order = [
        (me, 0),
        (me, 1),
        (along_x, 0),
        (along_y, 1),
        (along_x, 1),
        (along_y, 0),
        (across, 0),
        (across, 1),
    ]

    def extra_loads(step):
        place, batch = order[step]
        span = unit_rows(place, rows)
        return [
            pltpu.make_async_copy(ref.at[batch, span], buf.at[step % 2], load_sem.at[2 + i, step % 2])
            for i, (ref, buf) in enumerate(zip(extra_refs, extra_bufs))
        ]

    for load in extra_loads(0):
        load.start()

    def own_half(which):
        return x_buf.at[pl.ds(pl.multiple_of(which * rows, 16), rows)]

    def unit(place, batch, own=False):
        if job.compute is None:
            return
        span = unit_rows(place, rows)
        if own:
            loads = [
                pltpu.make_async_copy(local_ref.at[batch], own_half(core), load_sem.at[0, 0]),
                pltpu.make_async_copy(
                    piece(batch, other_core), own_half(1 - core), load_sem.at[1, 0]
                ),
            ]
        else:
            loads = [pltpu.make_async_copy(whole_ref.at[batch, span], x_buf, load_sem.at[0, 0])]
        step = len(stores)
        for load in loads:
            load.start()
        loads += extra_loads(step)
        if step < 7:
            for load in extra_loads(step + 1):
                load.start()
        if step == 0:
            for fetch in fetches:
                fetch.wait()
        if step >= 2:
            for store in stores[step - 2]:
                store.wait()
        for load in loads:
            load.wait()
        slot = step % 2
        extras = [buf.at[slot] for buf in extra_bufs]
        outs = [buf.at[slot] for buf in out_bufs]
        job.compute(x_buf, weight_bufs, extras, outs, sum_bufs, step == 0)
        stores.append(
            [
                pltpu.make_async_copy(buf.at[slot], ref.at[batch, span], store_sem.at[slot, i])
                for i, (ref, buf) in enumerate(zip(out_refs, out_bufs))
            ]
        )
        for store in stores[-1]:
            store.start()

    side = Side(rows, side_refs, side_bufs, sum_bufs, side_sem)

    for batch in range(2):
        moves[6 + batch].wait_recv()
        unit(me, batch, own=True)
        side.run(1)
    moves[0].wait_recv()
    moves[4].start()
    moves[8].start()
    moves[2].wait_recv()
    moves[5].start()
    moves[10].start()
    side.run(2)
    moves[8].wait_recv()
    unit(along_x, 0)
    moves[10].wait_recv()
    unit(along_y, 1)
    side.run(1)
    moves[1].wait_recv()
    moves[9].start()
    moves[3].wait_recv()
    moves[11].start()
    side.run(3)
    moves[9].wait_recv()
    unit(along_x, 1)
    moves[11].wait_recv()
    unit(along_y, 0)
    early = 1 if job.side else 0
    finish_sums(sum_bufs[:early], final_bufs[:early], final_refs[:early], final_sem)
    moves[4].wait_recv()
    moves[12].start()
    moves[5].wait_recv()
    moves[13].start()
    moves[12].wait_recv()
    unit(across, 0)
    moves[13].wait_recv()
    unit(across, 1)
    finish_sums(sum_bufs[early:], final_bufs[early:], final_refs[early:], final_sem)
    for move in moves:
        move.wait_send()
    for own in owns:
        own.wait()
    if count_refs:
        small.end()
    for group in stores[-2:]:
        for store in group:
            store.wait()


class Side:
    def __init__(self, rows, refs, bufs, sums, sem):
        self.rows, self.refs, self.bufs, self.sums, self.sem = rows, refs, bufs, sums, sem
        self.block = 0
        self.start()

    def copies(self):
        span = pl.ds((self.block % 4) * 2 * self.rows, 2 * self.rows)
        return [
            pltpu.make_async_copy(ref.at[self.block // 4, span], buf, self.sem.at[i])
            for i, (ref, buf) in enumerate(zip(self.refs, self.bufs))
        ]

    def start(self):
        if self.refs and self.block < 8:
            for copy in self.copies():
                copy.start()

    def run(self, count):
        for _ in range(count if self.refs else 0):
            for copy in self.copies():
                copy.wait()
            add_outer(self.bufs[0], self.bufs[1], self.sums[0], self.block == 0)
            self.block += 1
            self.start()


def finish_sums(sum_bufs, final_bufs, final_refs, sem):
    for i, (total, buf, ref) in enumerate(zip(sum_bufs, final_bufs, final_refs)):
        copies = []
        size = buf.shape[1]
        for block in range(total.shape[0] // size):
            slot = block % 2
            span = pl.ds(block * size, size)
            if block >= 2:
                copies[block - 2].wait()
            buf[slot] = total[span, :].astype(buf.dtype)
            copies.append(pltpu.make_async_copy(buf.at[slot], ref.at[span], sem.at[i, slot]))
            copies[-1].start()
        for copy in copies[-2:]:
            copy.wait()


def plane_gather(local, ident, name, job=None):
    job = job or Job(None)
    batches, rows, width = local.shape
    length = rows * lax.axis_size("seq")
    semaphores = pltpu.SemaphoreType.DMA
    scratch = [semaphores((14,)), semaphores((14,)), semaphores((2,))]
    scratch += [pltpu.VMEM((2 * rows if job.compute else 8, width), local.dtype)]
    if job.weights:
        depth = job.weights[0].shape[0]
        scratch += [pltpu.VMEM((depth, braid_width(job.weights)), job.weights[0].dtype)]
    scratch += [pltpu.VMEM((2, 2 * rows, array.shape[2]), array.dtype) for array in job.extras]
    scratch += [pltpu.VMEM((2 * rows, array.shape[2]), array.dtype) for array in job.side]
    scratch += [pltpu.VMEM((2, 2 * rows, wide), kind) for wide, kind in job.outs]
    scratch += [pltpu.VMEM(shape, jnp.float32) for shape in job.sums]
    scratch += [pltpu.VMEM((2, HEAD_SIZE // 2, shape[1]), jnp.bfloat16) for shape in job.sums]
    scratch += [
        semaphores((copy_count(job.weights) if job.weights else 1,)),
        semaphores((2 + len(job.extras), 2)),
        semaphores((max(1, len(job.side)),)),
        semaphores((2, max(1, len(job.outs)))),
        semaphores((max(1, len(job.sums)), 2)),
    ]
    any_space = pl.BlockSpec(memory_space=pl.ANY)
    out_shape = [jax.ShapeDtypeStruct((batches, length, width), local.dtype)]
    out_shape += [jax.ShapeDtypeStruct((batches, length, wide), kind) for wide, kind in job.outs]
    out_shape += [jax.ShapeDtypeStruct(shape, jnp.bfloat16) for shape in job.sums]
    inputs = [local, *job.weights, *job.extras, *job.side]
    in_specs = [any_space] * len(inputs)
    in_specs += [pl.BlockSpec(memory_space=pltpu.VMEM)] * len(job.tables)
    inputs += job.tables
    if job.small is not None:
        inputs.append(job.small)
        in_specs.append(pl.BlockSpec(memory_space=pltpu.VMEM))
        scratch += [pltpu.VMEM(job.small.shape, job.small.dtype)] + SmallSum.scratch(job.small)
    out_specs = [any_space] * len(out_shape)
    if job.spare:
        out_shape += job.spare[1]
        out_specs += [pl.BlockSpec(memory_space=pltpu.VMEM)] * len(job.spare[1])
    return pl.pallas_call(
        functools.partial(gather_kernel, job, rows),
        in_specs=in_specs,
        out_specs=out_specs,
        out_shape=out_shape,
        scratch_shapes=scratch,
        compiler_params=pltpu.CompilerParams(
            collective_id=ident, has_side_effects=True, vmem_limit_bytes=VMEM_LIMIT
        ),
        cost_estimate=pl.CostEstimate(
            flops=job.flops, bytes_accessed=SPAN_BYTES, transcendentals=0
        ),
        name=name,
    )(*inputs)


def scatter_kernel(job, rows, *refs):
    refs = list(refs)
    take = lambda n: [refs.pop(0) for _ in range(n)]
    part_refs, weight_refs, side_refs = (
        take(len(job.extras)),
        take(len(job.weights)),
        take(len(job.side)),
    )
    spread_refs = take(1 if job.spread is not None else 0)
    small_refs = take(1 if job.small is not None else 0)
    (out_ref,), final_refs = take(1), take(len(job.sums))
    spread_refs += take(len(spread_refs))
    small_refs += take(len(small_refs))
    part_buf, weight_buf, sums, held, from_core, from_link, out_buf = take(7)
    side_bufs, sum_bufs, final_bufs = take(len(job.side)), take(len(job.sums)), take(len(job.sums))
    weight_sem, load_sem, side_sem, final_sem, out_sem = take(5)
    core_send, core_recv, link_send, link_recv, credit = take(5)
    riders = []
    if spread_refs:
        riders.append(Spread(*spread_refs, *take(2)))
    if small_refs:
        riders.insert(0, SmallSum(True, *small_refs, *take(4)))

    me, other_core, along_x, along_y = plane_places()
    across = along_x + along_y - me
    core = me % 2
    kept = pl.ds(pl.multiple_of(core * rows, 16), rows)
    given = pl.ds(pl.multiple_of((1 - core) * rows, 16), rows)
    units = [
        (across, 0),
        (across, 1),
        (along_x, 0),
        (along_y, 1),
        (along_x, 1),
        (along_y, 0),
        (me, 0),
        (me, 1),
    ]
    targets = [along_x, along_y, along_x, along_y, along_x, along_y]
    added = {4: (1,), 5: (0,), 6: (2, 5), 7: (3, 4)}

    def load(step):
        place, batch = units[step]
        span = unit_rows(place, rows)
        sources = [ref.at[batch, span] for ref in part_refs]
        return copies_into(sources, part_buf.at[step % 2], load_sem.at[step % 2])

    loads = [load(step) for step in range(8)]
    fetches = copies_into(weight_refs, weight_buf, weight_sem)
    for copy in loads[0] + fetches:
        copy.start()
    gives = [
        pltpu.make_async_remote_copy(
            src_ref=sums.at[step % 2, given],
            dst_ref=from_core.at[step % 4],
            send_sem=core_send.at[step],
            recv_sem=core_recv.at[step],
            device_id={"seq": other_core},
            device_id_type=MESH,
        )
        for step in range(8)
    ]
    sends = [
        pltpu.make_async_remote_copy(
            src_ref=held.at[step],
            dst_ref=from_link.at[step],
            send_sem=link_send.at[step],
            recv_sem=link_recv.at[step],
            device_id={"seq": targets[step]},
            device_id_type=MESH,
        )
        for step in range(6)
    ]
    greet((other_core, along_x, along_y), *riders)
    for rider in riders:
        rider.begin()

    outs = []

    def finish(step):
        gives[step].wait_recv()
        kind = jnp.bfloat16 if step < 6 else jnp.float32
        total = sums[step % 2, kept].astype(kind) + from_core[step % 4].astype(kind)
        if step < 4:
            pl.semaphore_signal(credit, inc=1, device_id={"seq": other_core}, device_id_type=MESH)
        for arrived in added.get(step, ()):
            sends[arrived].wait_recv()
            total = total + from_link[arrived].astype(kind)
        if step < 6:
            held[step] = total
            sends[step].start()
        else:
            if outs and out_buf.shape[0] == 1:
                outs.pop().wait()
            slot = (step - 6) % out_buf.shape[0]
            out_buf[slot] = total
            outs.append(
                pltpu.make_async_copy(
                    out_buf.at[slot], out_ref.at[step - 6], out_sem.at[step - 6]
                )
            )
            outs[-1].start()

    side = Side(rows, side_refs, side_bufs, sum_bufs, side_sem)
    for step in range(8):
        for copy in loads[step]:
            copy.wait()
        if step == 0:
            for fetch in fetches:
                fetch.wait()
        if step < 7:
            for copy in loads[step + 1]:
                copy.start()
        if step >= 2:
            gives[step - 2].wait_send()
        job.compute(part_buf.at[step % 2], weight_buf, sums.at[step % 2])
        if step >= 4:
            pl.semaphore_wait(credit, 1)
        gives[step].start()
        if step >= 1:
            finish(step - 1)
        for rider in riders if step == 4 else []:
            rider.turn()
        side.run((0, 0, 1, 1, 1, 1, 2, 2)[step])
    if job.side:
        finish_sums(sum_bufs, final_bufs, final_refs, final_sem)
    finish(7)
    for move in gives[6:] + sends:
        move.wait_send()
    for out in outs:
        out.wait()
    for rider in riders:
        rider.end()


def plane_scatter(parts, width, ident, name, job):
    job.extras = list(parts)
    batches, length = parts[0].shape[:2]
    rows = length // lax.axis_size("seq")
    any_space = pl.BlockSpec(memory_space=pl.ANY)
    semaphores = pltpu.SemaphoreType.DMA
    weights = job.weights
    scratch = [
        pltpu.VMEM((2, 2 * rows, braid_width(parts)), parts[0].dtype),
        pltpu.VMEM((weights[0].shape[0], braid_width(weights)), weights[0].dtype),
        pltpu.VMEM((2, 2 * rows, width), jnp.bfloat16),
        pltpu.VMEM((6, rows, width), jnp.bfloat16),
        pltpu.VMEM((4, rows, width), jnp.bfloat16),
        pltpu.VMEM((6, rows, width), jnp.bfloat16),
        pltpu.VMEM((1 if job.side else 2, rows, width), jnp.float32),
    ]
    scratch += [pltpu.VMEM((2 * rows, array.shape[2]), array.dtype) for array in job.side]
    scratch += [pltpu.VMEM(shape, jnp.float32) for shape in job.sums]
    scratch += [pltpu.VMEM((2, HEAD_SIZE // 2, shape[1]), jnp.bfloat16) for shape in job.sums]
    scratch += [
        semaphores((copy_count(weights),)),
        semaphores((2, copy_count(parts))),
        semaphores((max(1, len(job.side)),)),
        semaphores((max(1, len(job.sums)), 2)),
        semaphores((2,)),
        semaphores((8,)),
        semaphores((8,)),
        semaphores((6,)),
        semaphores((6,)),
        pltpu.SemaphoreType.REGULAR,
    ]
    out_shape = [jax.ShapeDtypeStruct((batches, rows, width), jnp.float32)]
    out_shape += [jax.ShapeDtypeStruct(shape, jnp.bfloat16) for shape in job.sums]
    inputs = [*parts, *weights, *job.side]
    in_specs, out_specs = [any_space] * len(inputs), [any_space] * len(out_shape)
    if job.spread is not None:
        inputs.append(job.spread)
        in_specs.append(any_space)
        out_shape.append(jax.ShapeDtypeStruct(job.spread.shape, job.spread.dtype))
        out_specs.append(any_space)
        scratch += [semaphores((job.spread.shape[0] + 1,)), semaphores((job.spread.shape[0],))]
    if job.small is not None:
        inputs.append(job.small)
        in_specs.append(pl.BlockSpec(memory_space=pltpu.VMEM))
        out_shape.append(jax.ShapeDtypeStruct(job.small.shape, job.small.dtype))
        out_specs.append(pl.BlockSpec(memory_space=pltpu.VMEM))
        scratch += SmallSum.scratch(job.small)
    return pl.pallas_call(
        functools.partial(scatter_kernel, job, rows),
        in_specs=in_specs,
        out_specs=out_specs,
        out_shape=out_shape,
        scratch_shapes=scratch,
        compiler_params=pltpu.CompilerParams(
            collective_id=ident, has_side_effects=True, vmem_limit_bytes=VMEM_LIMIT
        ),
        cost_estimate=pl.CostEstimate(
            flops=job.flops, bytes_accessed=SPAN_BYTES, transcendentals=0
        ),
        name=name,
    )(*inputs)


def tiles(width, tile, body):
    def step(index, carry):
        body(pl.ds(pl.multiple_of(index * tile, 128), tile))
        return carry

    lax.fori_loop(0, width // tile, step, 0)


GELU_SCALE = 0.7978845608
GELU_CUBE = 0.044715


def gelu_parts(gate):
    square = gate * gate
    bent = jnp.tanh(GELU_SCALE * gate * (1.0 + GELU_CUBE * square))
    half = 0.5 * (1.0 + bent)
    slope = half + 0.5 * gate * (1.0 - bent * bent) * GELU_SCALE * (1.0 + 3.0 * GELU_CUBE * square)
    return gate * half, slope


def add_outer(left, right, total, first):
    def body(span):
        outer = lax.dot_general(
            left[:, span], right[...], (((0,), (0,)), ((), ())), preferred_element_type=jnp.float32
        )
        total[span, :] = outer if first else total[span, :] + outer

    wide = left.shape[1]
    tiles(wide, next(tile for tile in (2 * BRAID, BRAID, HEAD_SIZE) if wide % tile == 0), body)


def hidden_compute(x_buf, weights, extras, outs, sums, first):
    gate_out, up_out, hidden_out = outs
    (weight,) = weights

    def step(index, carry):
        both = pl.ds(pl.multiple_of(index * 2 * BRAID, 128), 2 * BRAID)
        span = pl.ds(pl.multiple_of(index * BRAID, 128), BRAID)
        product = final_dot(x_buf[...], weight[:, both])
        gate, up = product[:, :BRAID], product[:, BRAID:]
        gate_out[:, span] = gate.astype(gate_out.dtype)
        up_out[:, span] = up.astype(up_out.dtype)
        hidden_out[:, span] = (gelu_parts(gate)[0] * up).astype(hidden_out.dtype)
        return carry

    lax.fori_loop(0, weight.shape[1] // (2 * BRAID), step, 0)


def hidden_back_compute(x_buf, weights, extras, outs, sums, first):
    (down_w,) = weights
    gate_in, up_in, hidden_in = extras
    gate_out, up_out = outs
    product = dot_back(x_buf[...], down_w[...])
    for start in range(0, product.shape[1], BRAID):
        span = slice(start, start + BRAID)
        grad = product[:, span]
        value, slope = gelu_parts(gate_in[:, span].astype(jnp.float32))
        gate_out[:, span] = (grad * up_in[:, span].astype(jnp.float32) * slope).astype(
            gate_out.dtype
        )
        up_out[:, span] = (grad * value).astype(up_out.dtype)
    add_outer(hidden_in, x_buf, sums[0], first)


def head_back_compute(x_buf, weights, extras, outs, sums, first):
    outs[0][...] = dot_back(x_buf[...], weights[0][...]).astype(outs[0].dtype)
    add_outer(extras[0], x_buf, sums[1], first)


def rows_compute(part, weight, out):
    def body(span):
        out[:, span] = final_dot(part[...], weight[:, span]).astype(out.dtype)

    tiles(weight.shape[1], 2 * BRAID, body)


def back_compute(part, weight, out):
    def body(span):
        out[:, span] = dot_back(part[...], weight[span, :]).astype(out.dtype)

    tiles(weight.shape[0], 2 * BRAID, body)


def score_parts(query, key, low_bound, row_start, col_start):
    raw = lax.dot_general(
        query, key, (((1,), (1,)), ((), ())), preferred_element_type=jnp.float32
    )
    bent = jnp.tanh(raw * (1.0 / CAP))
    shape = raw.shape
    row = row_start + lax.broadcasted_iota(jnp.int32, shape, 0)
    col = col_start + lax.broadcasted_iota(jnp.int32, shape, 1)
    allowed = (col <= row) & (col >= low_bound)
    return bent, jnp.where(allowed, CAP * bent, -1e30)


def attend_kernel(block, reach, q_ref, k_ref, v_ref, low_ref, out_ref, log_ref):
    index = pl.program_id(1)

    def run(blocks):
        first = (index - (blocks - 1)) * block
        span = pl.ds(pl.multiple_of(first, block), blocks * block)
        _, capped = score_parts(
            q_ref[...], k_ref[span, :], low_ref[...], index * block, first
        )
        peak = jnp.max(capped, axis=-1, keepdims=True)
        power = jnp.exp(capped - peak)
        total = jnp.sum(power, axis=-1, keepdims=True)
        prob = (power * (1.0 / total)).astype(jnp.bfloat16)
        out = jnp.dot(prob, v_ref[span, :], preferred_element_type=jnp.float32)
        out_ref[...] = out.astype(jnp.bfloat16)
        log_ref[...] = peak + jnp.log(total)

    for blocks in range(1, reach + 1):
        if blocks < reach:
            pl.when(index == blocks - 1)(functools.partial(run, blocks))
        else:
            pl.when(index >= blocks - 1)(functools.partial(run, blocks))


def turn_back(value, cosine, sine):
    half = value.shape[-1] // 2
    first, second = value[:, :half], value[:, half:]
    return jnp.concatenate(
        [first * cosine + second * sine, second * cosine - first * sine], axis=-1
    )


def attend_back_kernel(
    block,
    reach,
    q_ref,
    k_ref,
    v_ref,
    g_ref,
    low_ref,
    log_ref,
    cos_ref,
    sin_ref,
    grad_ref,
    dk_ref,
    dv_ref,
):
    index = pl.program_id(1)
    steps = pl.num_programs(1)

    @pl.when(index == 0)
    def _():
        dk_ref[...] = jnp.zeros_like(dk_ref)
        dv_ref[...] = jnp.zeros_like(dv_ref)

    own = pl.ds(pl.multiple_of(index * block, block), block)

    def run(blocks):
        first = (index - (blocks - 1)) * block
        span = pl.ds(pl.multiple_of(first, block), blocks * block)
        query, grad = q_ref[...], g_ref[...]
        key = k_ref[span, :]
        bent, capped = score_parts(query, key, low_ref[...], index * block, first)
        prob = jnp.exp(capped - log_ref[...])
        grad_prob = lax.dot_general(
            grad, v_ref[span, :], (((1,), (1,)), ((), ())), preferred_element_type=jnp.float32
        )
        delta = jnp.sum(prob * grad_prob, axis=-1, keepdims=True)
        grad_score = (prob * (grad_prob - delta) * (1.0 - bent * bent)).astype(jnp.bfloat16)
        dq = jnp.dot(grad_score, key, preferred_element_type=jnp.float32)
        dq = dq * (1.0 / math.sqrt(HEAD_SIZE))
        dq = turn_back(dq, cos_ref[own, :], sin_ref[own, :])
        grad_ref[own, :HEAD_SIZE] = dq.astype(jnp.bfloat16)
        across = (((0,), (0,)), ((), ()))
        dk_ref[span, :] += lax.dot_general(
            grad_score, query, across, preferred_element_type=jnp.float32
        )
        dv_ref[span, :] += lax.dot_general(
            prob.astype(jnp.bfloat16), grad, across, preferred_element_type=jnp.float32
        )

    for blocks in range(1, reach + 1):
        if blocks < reach:
            pl.when(index == blocks - 1)(functools.partial(run, blocks))
        else:
            pl.when(index >= blocks - 1)(functools.partial(run, blocks))

    @pl.when(index == steps - 1)
    def _():
        half = HEAD_SIZE // 2
        odd = lax.axis_index("seq") % 2 == 1
        dk = turn_back(dk_ref[...], cos_ref[...], sin_ref[...])
        for part, grad in enumerate((dk, dv_ref[...])):
            low, high = grad[:, :half], grad[:, half:]
            own = HEAD_SIZE + half * part
            grad_ref[:, own : own + half] = jnp.where(odd, high, low).astype(jnp.bfloat16)
            own += HEAD_SIZE
            grad_ref[:, own : own + half] = jnp.where(odd, low, high).astype(jnp.bfloat16)


def block_shape(length):
    for block in (384, 256, 128):
        if length % block == 0:
            reach = min(length // block, (WIN - 1 + block - 1) // block + 1)
            return block, reach
    raise ValueError("sequence length")


def attend_specs(length, block):
    whole = pl.BlockSpec((None, length, HEAD_SIZE), lambda m, i: (m, 0, 0))
    half = pl.BlockSpec((None, length, HEAD_SIZE // 2), lambda m, i: (m, 0, 0))
    rows = pl.BlockSpec((None, block, HEAD_SIZE), lambda m, i: (m, i, 0))
    line = pl.BlockSpec((None, block, 1), lambda m, i: (m, i, 0))
    return whole, half, rows, line


def project_kernel(x_ref, w_ref, far_ref, cos_ref, sin_ref, q_ref, k_ref, v_ref):
    product = final_dot(x_ref[...], w_ref[...])
    far = final_dot(x_ref[...], far_ref[...])
    cosine, sine = cos_ref[...], sin_ref[...]
    half = HEAD_SIZE // 2
    query = product[:, :HEAD_SIZE]
    own_k, own_v = product[:, HEAD_SIZE : HEAD_SIZE + half], product[:, HEAD_SIZE + half :]
    far_k, far_v = far[:, :half], far[:, half:]
    odd = lax.axis_index("seq") % 2 == 1
    key = jnp.concatenate([jnp.where(odd, far_k, own_k), jnp.where(odd, own_k, far_k)], axis=1)
    query = rotate(query, cosine, sine, 1.0) * (1.0 / math.sqrt(HEAD_SIZE))
    q_ref[...] = query.astype(jnp.bfloat16)
    k_ref[...] = rotate(key, cosine, sine, 1.0).astype(jnp.bfloat16)
    v_ref[:, :half] = jnp.where(odd, far_v, own_v).astype(jnp.bfloat16)
    v_ref[:, half:] = jnp.where(odd, own_v, far_v).astype(jnp.bfloat16)


def project(whole, weight, far, cosine, sine):
    batches, length, width = whole.shape
    block = block_shape(length)[0]
    _, _, rows, _ = attend_specs(length, block)
    half = pl.BlockSpec((None, block, HEAD_SIZE // 2), lambda m, i: (m, i, 0))
    return pl.pallas_call(
        project_kernel,
        grid=(batches, length // block),
        in_specs=[
            pl.BlockSpec((None, block, width), lambda m, i: (m, i, 0)),
            pl.BlockSpec(weight.shape, lambda m, i: (0, 0)),
            pl.BlockSpec(far.shape, lambda m, i: (0, 0)),
            half,
            half,
        ],
        out_specs=[rows] * 3,
        out_shape=[jax.ShapeDtypeStruct((batches, length, HEAD_SIZE), jnp.bfloat16)] * 3,
        compiler_params=pltpu.CompilerParams(vmem_limit_bytes=40 * 2**20),
        cost_estimate=pl.CostEstimate(
            flops=6 * batches * length * width * HEAD_SIZE,
            bytes_accessed=2 * batches * length * width,
            transcendentals=0,
        ),
        name="project",
    )(whole, weight, far, cosine, sine)


def token_tables(tables, made):
    counts_ref, frequency_ref = tables
    cos_ref, sin_ref, low_ref = made
    batches, length, _ = cos_ref.shape
    block = block_shape(length)[0]
    for batch in range(batches):

        def step(index, carry, batch=batch):
            span = pl.ds(pl.multiple_of(index * block, 16), block)
            place = index * block + lax.broadcasted_iota(jnp.int32, (block, HEAD_SIZE // 2), 0)
            place = place.astype(jnp.float32)
            start = jnp.zeros_like(place)
            for number in range(1, DOCUMENTS):
                row = batch * (DOCUMENTS - 1) + number - 1
                count = counts_ref[row : row + 1, :]
                start = jnp.where(place >= count, count, start)
            phase_angle = (place - start) * frequency_ref[...]
            cos_ref[batch, span, :] = jnp.cos(phase_angle)
            sin_ref[batch, span, :] = jnp.sin(phase_angle)
            low = jnp.maximum(start, place - (WIN - 1))
            low_ref[batch, span, :] = low[:, :1].astype(jnp.int32)
            return carry

        lax.fori_loop(0, length // block, step, 0)


def attend(query, key, value, low_bound):
    batches, length = query.shape[:2]
    block, reach = block_shape(length)
    whole, half, rows, line = attend_specs(length, block)
    area = batches * block * block * reach * (length // block)
    return pl.pallas_call(
        functools.partial(attend_kernel, block, reach),
        grid=(batches, length // block),
        in_specs=[rows, whole, whole, line],
        out_specs=[rows, line],
        out_shape=[
            jax.ShapeDtypeStruct((batches, length, HEAD_SIZE), jnp.bfloat16),
            jax.ShapeDtypeStruct((batches, length, 1), jnp.float32),
        ],
        compiler_params=pltpu.CompilerParams(vmem_limit_bytes=40 * 2**20),
        cost_estimate=pl.CostEstimate(
            flops=4 * area * HEAD_SIZE,
            bytes_accessed=10 * batches * length * HEAD_SIZE,
            transcendentals=2 * area,
        ),
        name="attend",
    )(query, key, value, low_bound)


def attend_back(query, key, value, grad, low_bound, log_total, cosine, sine):
    batches, length = query.shape[:2]
    block, reach = block_shape(length)
    whole, half, rows, line = attend_specs(length, block)
    area = batches * block * block * reach * (length // block)
    return pl.pallas_call(
        functools.partial(attend_back_kernel, block, reach),
        grid=(batches, length // block),
        in_specs=[rows, whole, whole, rows, line, line, half, half],
        out_specs=pl.BlockSpec((None, length, 3 * HEAD_SIZE), lambda m, i: (m, 0, 0)),
        out_shape=jax.ShapeDtypeStruct((batches, length, 3 * HEAD_SIZE), jnp.bfloat16),
        scratch_shapes=[pltpu.VMEM((length, HEAD_SIZE), jnp.float32)] * 2,
        compiler_params=pltpu.CompilerParams(vmem_limit_bytes=48 * 2**20),
        cost_estimate=pl.CostEstimate(
            flops=10 * area * HEAD_SIZE,
            bytes_accessed=24 * batches * length * HEAD_SIZE,
            transcendentals=2 * area,
        ),
        name="attend_back",
    )(query, key, value, grad, low_bound, log_total, cosine, sine)


class ByHeads:
    def __init__(self, w_query, key_weight, value_weight, w_out):
        place = lax.axis_index("seq")
        count = lax.axis_size("seq")
        layers = lax.axis_size("fsdp")
        half = HEAD_SIZE // 2

        def columns(weight, width):
            return lax.dynamic_slice_in_dim(weight, place * width, width, axis=1)

        joined = jnp.concatenate(
            [columns(w_query, HEAD_SIZE), columns(key_weight, half), columns(value_weight, half)],
            axis=1,
        )
        depth = HEAD_SIZE // count
        here = QUERY_HEADS // layers
        part = w_out.reshape(here, count, depth, w_out.shape[1])
        part = lax.dynamic_index_in_dim(part, place, axis=1, keepdims=False)
        rows = joined.shape[0]
        both = jnp.concatenate([joined, part.reshape(-1, joined.shape[1])], axis=0)
        self.first = both
        self.both = lax.all_gather(both, "fsdp", axis=0)
        self.split = rows
        self.part_shape = (QUERY_HEADS * depth, w_out.shape[1])

    def forward(self, normed, segments):
        batches, rows, width = normed.shape
        length = rows * lax.axis_size("seq")
        half = HEAD_SIZE // 2
        numbers = jnp.arange(1, DOCUMENTS, dtype=segments.dtype)
        counts = jnp.sum((segments[:, None] < numbers[:, None]).astype(jnp.float32), axis=2)
        counts = jnp.pad(counts.reshape(-1), (0, 8 - batches * (DOCUMENTS - 1)))
        counts = jnp.broadcast_to(counts[:, None], (8, half))
        frequency = 10000.0 ** (-jnp.arange(half, dtype=jnp.float32) * 2.0 / HEAD_SIZE)
        table = jax.ShapeDtypeStruct((batches, length, half), jnp.float32)
        bound = jax.ShapeDtypeStruct((batches, length, 1), jnp.int32)
        whole, cosine, sine, low_bound = plane_gather(
            normed,
            0,
            "gather_normed",
            Job(
                None,
                tables=[frequency[None]],
                small=counts,
                spare=(token_tables, [table, table, bound]),
            ),
        )
        whole, both = lax.optimization_barrier((whole, self.both))
        self.joined = both[:, : self.split].reshape(-1, both.shape[2])
        self.out_rows = swap_parts(both[:, self.split :].reshape(self.part_shape), 0, 0)
        self.far = lax.ppermute(
            self.joined[:, HEAD_SIZE:], "seq", [(i, i ^ 1) for i in range(QUERY_HEADS)]
        )
        query, key, value = project(whole, self.joined, self.far, cosine, sine)
        attended, log_total = attend(query, key, value, low_bound)
        job = Job(
            rows_compute, weights=[self.out_rows], flops=2 * batches * length * HEAD_SIZE * width
        )
        (mixed,) = plane_scatter([attended], width, 1, "scatter_mixed", job)
        return mixed, (whole, query, key, value, low_bound, log_total, cosine, sine, attended)

    def open_back(self, grad_mixed_b, saved, side):
        attended = saved[-1]
        batches, length = attended.shape[:2]
        width = grad_mixed_b.shape[-1]
        job = Job(
            head_back_compute,
            weights=[self.out_rows],
            extras=[attended],
            outs=[(HEAD_SIZE, jnp.bfloat16)],
            side=side,
            sums=[(side[0].shape[2], side[1].shape[2]), (HEAD_SIZE, width)],
            flops=2 * batches * length * (HEAD_SIZE * width + side[0].shape[2] * side[1].shape[2]),
        )
        _, grad_att, side_sum, self.out_sum = plane_gather(
            grad_mixed_b, 2, "gather_grad_mixed", job
        )
        return grad_att, side_sum

    def middle_back(self, grad_att, saved):
        _, query, key, value, low_bound, log_total, cosine, sine, _ = saved
        grads = attend_back(query, key, value, grad_att, low_bound, log_total, cosine, sine)
        grads, self.out_own = lax.optimization_barrier((grads, scatter_rows(self.out_sum)))
        return grads

    def close_back(self, grads, saved, meanwhile, gains):
        count = lax.axis_size("seq")
        joined = dot_rows(saved[0], grads).astype(jnp.bfloat16)
        wide = 2 * HEAD_SIZE
        pairs = ((joined[:, :wide], self.joined), (joined[:, wide:], self.far))
        through = sum(
            jnp.sum(grad.astype(jnp.float32) * weight.astype(jnp.float32), axis=1)
            for grad, weight in pairs
        )
        gains = jnp.stack([through, *gains])
        own, far = joined[:, HEAD_SIZE : 2 * HEAD_SIZE], joined[:, 2 * HEAD_SIZE :]
        came = lax.ppermute(far, "seq", [(i, i ^ 1) for i in range(count)])
        own = (own.astype(jnp.float32) + came.astype(jnp.float32)).astype(jnp.bfloat16)
        joined = jnp.concatenate([joined[:, :HEAD_SIZE], own], axis=1)
        grads, joined, meanwhile = lax.optimization_barrier((grads, joined, meanwhile))
        self.joined_sum = joined

        parts = self.out_own.reshape(self.out_own.shape[0], count, -1).transpose(1, 0, 2)
        rows = grads.shape[0] * grads.shape[1]
        width = self.joined.shape[0]
        job = Job(
            back_compute,
            weights=[self.joined, self.far],
            spread=parts,
            small=gains.reshape(-1, HEAD_SIZE // 2),
            flops=6 * rows * HEAD_SIZE * width,
        )
        grad_normed, self.placed, gains = plane_scatter(
            [grads], width, 3, "scatter_grad_normed", job
        )
        return grad_normed, meanwhile, gains.reshape(4, -1)

    def weight_grads(self):
        half = HEAD_SIZE // 2
        joined = scatter_rows(self.joined_sum).astype(jnp.float32)
        return (
            joined[:, :HEAD_SIZE],
            joined[:, HEAD_SIZE : HEAD_SIZE + half],
            joined[:, HEAD_SIZE + half :],
            self.placed.astype(jnp.float32).reshape(-1, self.placed.shape[2]),
        )


class ByTokens:
    def __init__(self, w_query, key_weight, value_weight, w_out):
        self.weights = fetch_attention(w_query, key_weight, value_weight, w_out)
        self.records, self.first = [], jnp.zeros(())

    def forward(self, normed, segments):
        seg_whole = lax.all_gather(segments, "seq", axis=1, tiled=True)
        done = [self.forward_one(*pair) for pair in zip(normed, seg_whole)]
        return jnp.stack([mixed for mixed, _ in done]), [saved for _, saved in done]

    def forward_one(self, normed, seg_whole):
        token_rows = normed.shape[0]
        halo_count = (WIN - 2 + token_rows) // token_rows
        w_query, key_weight, value_weight, w_out = self.weights
        seq_place = lax.axis_index("seq")
        seg_here = lax.dynamic_slice_in_dim(seg_whole, seq_place * token_rows, token_rows)
        position = jnp.arange(seg_whole.shape[0], dtype=jnp.int32) - doc_starts(seg_whole)
        position = lax.dynamic_slice_in_dim(position, seq_place * token_rows, token_rows)
        cosine, sine = (table[:, None] for table in angles(position, HEAD_SIZE))
        query = rotate(
            final_dot(normed, w_query).reshape(token_rows, QUERY_HEADS, HEAD_SIZE),
            cosine,
            sine,
            1.0,
        )
        query = (query * (1.0 / math.sqrt(HEAD_SIZE))).astype(jnp.bfloat16)
        key = rotate(
            final_dot(normed, key_weight).reshape(token_rows, KEY_VALUE_HEADS, HEAD_SIZE),
            cosine,
            sine,
            1.0,
        ).astype(jnp.bfloat16)
        value = final_dot(normed, value_weight).reshape(token_rows, KEY_VALUE_HEADS, HEAD_SIZE)
        pair = key_window(jnp.stack([key, value.astype(jnp.bfloat16)]), halo_count)
        allowed = window_mask(seg_here, seg_whole, seq_place, token_rows, halo_count)
        query = query.reshape(token_rows, KEY_VALUE_HEADS, -1, HEAD_SIZE)
        score = jnp.einsum("qhgd,khd->hgqk", query, pair[0], preferred_element_type=jnp.float32)
        capped = jnp.where(allowed, CAP * jnp.tanh(score / CAP), -jnp.inf)
        peak = jnp.max(capped, axis=-1, keepdims=True)
        power = jnp.exp(capped - peak)
        total = jnp.sum(power, axis=-1, keepdims=True)
        attended = jnp.einsum(
            "hgqk,khd->qhgd",
            (power / total).astype(jnp.bfloat16),
            pair[1],
            preferred_element_type=jnp.float32,
        )
        attended = attended.reshape(token_rows, QUERY_HEADS * HEAD_SIZE).astype(jnp.bfloat16)
        mixed = final_dot(attended, w_out)
        log_total = peak + jnp.log(total)
        return mixed, (normed, query, pair, allowed, log_total, cosine, sine, attended)

    def open_back(self, grad_mixed_b, saved, side):
        return grad_mixed_b, dot_rows(*side)

    def middle_back(self, grad_mixed_b, saved):
        return grad_mixed_b

    def close_back(self, grad_mixed_b, saved, meanwhile, gains):
        grads = [self.backward_one(*pair) for pair in zip(grad_mixed_b, saved)]
        return jnp.stack(grads), meanwhile, None

    def backward_one(self, grad_mixed_b, saved):
        normed, query, pair, allowed, log_total, cosine, sine, attended = saved
        token_rows = normed.shape[0]
        halo_count = (WIN - 2 + token_rows) // token_rows
        w_query, key_weight, value_weight, w_out = self.weights
        grad_att = dot_back(grad_mixed_b, w_out).astype(jnp.bfloat16)
        grad_att = grad_att.reshape(token_rows, KEY_VALUE_HEADS, -1, HEAD_SIZE)
        score = jnp.einsum("qhgd,khd->hgqk", query, pair[0], preferred_element_type=jnp.float32)
        bent = jnp.tanh(score / CAP)
        prob = jnp.exp(jnp.where(allowed, CAP * bent, -jnp.inf) - log_total)
        grad_prob = jnp.einsum(
            "qhgd,khd->hgqk", grad_att, pair[1], preferred_element_type=jnp.float32
        )
        delta = jnp.sum(prob * grad_prob, axis=-1, keepdims=True)
        grad_score = (prob * (grad_prob - delta) * (1.0 - bent * bent)).astype(jnp.bfloat16)
        dq = jnp.einsum("hgqk,khd->qhgd", grad_score, pair[0], preferred_element_type=jnp.float32)
        dk = jnp.einsum("hgqk,qhgd->khd", grad_score, query, preferred_element_type=jnp.float32)
        dv = jnp.einsum(
            "hgqk,qhgd->khd", prob.astype(jnp.bfloat16), grad_att, preferred_element_type=jnp.float32
        )
        paired = window_grads(jnp.stack([dk, dv]), halo_count, token_rows)
        dq = rotate(
            dq.reshape(token_rows, QUERY_HEADS, HEAD_SIZE) * (1.0 / math.sqrt(HEAD_SIZE)),
            cosine,
            sine,
            -1.0,
        )
        dq = dq.reshape(token_rows, -1).astype(jnp.bfloat16)
        dk = rotate(paired[0], cosine, sine, -1.0).reshape(token_rows, -1).astype(jnp.bfloat16)
        dv = paired[1].reshape(token_rows, -1).astype(jnp.bfloat16)
        self.records.append((normed, dq, dk, dv, attended, grad_mixed_b))
        return dot_back(dq, w_query) + dot_back(dk, key_weight) + dot_back(dv, value_weight)

    def weight_grads(self):
        normed, dq, dk, dv, attended, grad_mixed_b = (
            jnp.concatenate(parts, axis=0) for parts in zip(*self.records)
        )
        normed = lax.all_gather(normed, "seq", axis=0, tiled=True)
        attended = lax.all_gather(attended, "seq", axis=0, tiled=True)
        sums = []
        for rows, grads in ((normed, dq), (normed, dk), (normed, dv), (attended, grad_mixed_b)):
            column_sum = dot_rows(rows, swap_parts(grads, 1, 0)).astype(jnp.bfloat16)
            owned = lax.psum_scatter(column_sum, "fsdp", scatter_dimension=0, tiled=True)
            sums.append(owned.astype(jnp.float32))
        return tuple(sums)


class FeedForward:
    def __init__(self, w_gate, w_up, w_down, by_kernel, first):
        place = lax.optimization_barrier((lax.axis_index("seq"), first))[0]
        count = lax.axis_size("seq")
        self.by_kernel = by_kernel
        self.run = w_gate.shape[1] // (count * count)

        def columns(weight):
            parts = [
                lax.dynamic_slice_in_dim(
                    weight, (t * count + place) * self.run, self.run, axis=1
                )
                for t in range(count)
            ]
            return jnp.concatenate(parts, axis=1)

        here = w_down.shape[0] // (count * self.run)
        part = w_down.reshape(here, count, self.run, w_down.shape[1])
        part = lax.dynamic_index_in_dim(part, place, axis=1, keepdims=False)
        self.gate = gather_rows(columns(w_gate))
        self.up = gather_rows(columns(w_up))
        self.down = gather_rows(part.reshape(here * self.run, -1))

    def forward(self, ffn_in):
        hidden_width, width = self.down.shape
        if self.by_kernel:
            rows = ffn_in.shape[0] * ffn_in.shape[1] * lax.axis_size("seq")
            job = Job(
                hidden_compute,
                weights=[self.gate, self.up],
                outs=[(hidden_width, jnp.bfloat16)] * 3,
                flops=4 * rows * width * hidden_width,
            )
            whole, gate_proj, up_proj, hidden = plane_gather(ffn_in, 4, "gather_ffn_in", job)
            job = Job(
                rows_compute, weights=[self.down], flops=2 * rows * width * hidden_width
            )
            (down_proj,) = plane_scatter([hidden], width, 5, "scatter_down", job)
        else:
            whole = lax.all_gather(ffn_in, "seq", axis=1, tiled=True)
            gate_proj = final_dot(whole, self.gate)
            up_proj = final_dot(whole, self.up)
            hidden = geglu(gate_proj, up_proj).astype(jnp.bfloat16)
            down_proj = lax.psum_scatter(
                final_dot(hidden, self.down).astype(jnp.bfloat16),
                "seq",
                scatter_dimension=1,
                tiled=True,
            ).astype(jnp.float32)
        return down_proj, (whole, gate_proj, up_proj, hidden)

    def backward(self, grad_down_b, saved):
        whole, gate_proj, up_proj, hidden = saved
        hidden_width, width = self.down.shape
        if self.by_kernel:
            rows = whole.shape[0] * whole.shape[1]
            job = Job(
                hidden_back_compute,
                weights=[self.down],
                extras=[gate_proj, up_proj, hidden],
                outs=[(hidden_width, jnp.bfloat16)] * 2,
                sums=[(hidden_width, width)],
                flops=4 * rows * width * hidden_width,
            )
            _, grad_gate, grad_up, self.down_sum = plane_gather(
                grad_down_b, 6, "gather_grad_down", job
            )
            job = Job(
                back_compute,
                weights=[self.gate, self.up],
                side=[whole, grad_gate],
                sums=[(width, hidden_width)],
                flops=6 * rows * width * hidden_width,
            )
            grad_ffn_in, self.gate_sum = plane_scatter(
                [grad_gate, grad_up], width, 7, "scatter_grad_ffn_in", job
            )
        else:
            grad_whole = lax.all_gather(grad_down_b, "seq", axis=1, tiled=True)
            grad_hidden = dot_back(grad_whole, self.down)
            _, pullback = jax.vjp(geglu, gate_proj, up_proj)
            grad_gate, grad_up = (g.astype(jnp.bfloat16) for g in pullback(grad_hidden))
            partial = dot_back(grad_gate, self.gate) + dot_back(grad_up, self.up)
            grad_ffn_in = lax.psum_scatter(
                partial.astype(jnp.bfloat16), "seq", scatter_dimension=1, tiled=True
            ).astype(jnp.float32)
            self.down_sum = dot_rows(hidden, grad_whole)
            self.gate_sum = dot_rows(whole, grad_gate)
        self.up_side = (whole, grad_up)
        return grad_ffn_in

    def own_columns(self, own):
        return swap_parts(own, 1, 1).astype(jnp.float32)

    def own_rows(self, own):
        here = own.shape[0] // self.run
        moved = swap_parts(own, 1, 0)
        moved = moved.reshape(-1, here, self.run, moved.shape[1]).transpose(1, 0, 2, 3)
        return moved.astype(jnp.float32).reshape(-1, moved.shape[3])


def on_device(
    tokens,
    segments,
    w_query,
    key_weight,
    value_weight,
    w_out,
    w_gate,
    w_up,
    w_down,
    gain_attn_in,
    gain_attn_out,
    gain_ffn_in,
    gain_ffn_out,
    cotangent,
):
    by_kernel = (
        lax.axis_size("seq") == QUERY_HEADS
        and tokens.shape[0] == 2
        and QUERY_HEADS % lax.axis_size("fsdp") == 0
    )
    attention = (ByHeads if by_kernel else ByTokens)(w_query, key_weight, value_weight, w_out)
    ffn = FeedForward(w_gate, w_up, w_down, by_kernel, attention.first)

    stream = tokens[:, 0].astype(jnp.float32)
    normed = rms_gain(stream, gain_attn_in).astype(jnp.bfloat16)
    mixed, attention_saved = attention.forward(normed, segments[:, 0])
    middle = stream + rms_gain(mixed, gain_attn_out)
    ffn_in = rms_gain(middle, gain_ffn_in).astype(jnp.bfloat16)
    down_proj, ffn_saved = ffn.forward(ffn_in)
    result = middle + rms_gain(down_proj, gain_ffn_out)

    grad_result = cotangent[:, 0].astype(jnp.float32)
    _, pullback = jax.vjp(rms_gain, down_proj, gain_ffn_out)
    grad_down, grad_gain_four = pullback(grad_result)
    grad_ffn_in = ffn.backward(grad_down.astype(jnp.bfloat16), ffn_saved)
    _, pullback = jax.vjp(rms_gain, middle, gain_ffn_in)
    grad_middle, grad_gain_three = pullback(grad_ffn_in)
    grad_middle = grad_result + grad_middle
    _, pullback = jax.vjp(rms_gain, mixed, gain_attn_out)
    grad_mixed, grad_gain_two = pullback(grad_middle)
    grad_mixed, w_down_grad = lax.optimization_barrier(
        (grad_mixed.astype(jnp.bfloat16), scatter_rows(ffn.down_sum))
    )
    grad_att, up_sum = attention.open_back(grad_mixed, attention_saved, ffn.up_side)
    grad_att, w_gate_grad = lax.optimization_barrier((grad_att, scatter_rows(ffn.gate_sum)))
    w_down_grad = ffn.own_rows(w_down_grad)
    grads = attention.middle_back(grad_att, attention_saved)
    grads, w_gate_grad, w_down_grad = lax.optimization_barrier((grads, w_gate_grad, w_down_grad))
    grad_normed, w_gate_grad, gains = attention.close_back(
        grads,
        attention_saved,
        ffn.own_columns(w_gate_grad),
        [grad_gain_two, grad_gain_three, grad_gain_four],
    )
    _, pullback = jax.vjp(rms_gain, stream, gain_attn_in)
    grad_stream, grad_gain_one = pullback(grad_normed)
    grad_stream = grad_middle + grad_stream

    w_up_grad = ffn.own_columns(scatter_rows(up_sum))
    if gains is None:
        gains = jnp.stack([grad_gain_one, grad_gain_two, grad_gain_three, grad_gain_four])
        gains = lax.psum(gains, ("seq", "fsdp"))
        grad_gain_one = gains[0]
    else:
        grad_gain_one = gains[0] / gain_attn_in
    query_grad, key_grad, value_grad, out_grad = attention.weight_grads()
    return (
        result.astype(jnp.bfloat16)[:, None],
        grad_stream[:, None],
        query_grad,
        key_grad,
        value_grad,
        out_grad,
        w_gate_grad,
        w_up_grad,
        w_down_grad,
        grad_gain_one,
        gains[1],
        gains[2],
        gains[3],
    )


def solution(mesh):
    in_specs = (
        P(None, "fsdp", "seq", None),
        P(None, "fsdp", "seq"),
        P("fsdp", None),
        P("fsdp", None),
        P("fsdp", None),
        P("fsdp", None),
        P("fsdp", None),
        P("fsdp", None),
        P("fsdp", None),
        P(),
        P(),
        P(),
        P(),
        P(None, "fsdp", "seq", None),
    )
    out_specs = (
        P(None, "fsdp", "seq", None),
        P(None, "fsdp", "seq", None),
        P("fsdp", "seq"),
        P("fsdp", "seq"),
        P("fsdp", "seq"),
        P("fsdp", "seq"),
        P("fsdp", "seq"),
        P("fsdp", "seq"),
        P("fsdp", "seq"),
        P(),
        P(),
        P(),
        P(),
    )
    return jax.shard_map(
        on_device, mesh=mesh, in_specs=in_specs, out_specs=out_specs, check_vma=False
    )
```
